32 devices in a mesh: rows: 16 (over z, y, x), seq: 2 (over core).
Axes of the slice: x: 2, y: 2, z: 4, core: 2. Of those that a mesh axis runs over, the one named last changes fastest.
Arguments:
- hidden_in: bfloat16 [16, 2048, 768], P('rows', 'seq'), may hold values from -6 to 6
- doc_lengths: int32 [16, 5], P('rows'), may hold values from 0 to 512, as said below
- out_grad: bfloat16 [16, 2048, 768], P('rows', 'seq'), may hold values from -6 to 6
- w_query: bfloat16 [768, 384], replicated, may hold values from -0.21875 to 0.21875
- w_key: bfloat16 [768, 384], replicated, may hold values from -0.21875 to 0.21875
- w_value: bfloat16 [768, 384], replicated, may hold values from -0.21875 to 0.21875
- w_conv_out: bfloat16 [768, 384], replicated, may hold values from -0.21875 to 0.21875
- depth_kernel: bfloat16 [9, 768], replicated, may hold values from -2 to 2
- w_point: bfloat16 [768, 384], replicated, may hold values from -0.21875 to 0.21875
- w_conv_kernel: bfloat16 [384, 54], replicated, may hold values from -0.3125 to 0.3125
- w_output: bfloat16 [768, 768], replicated, may hold values from -0.875 to 0.875
- ln1_gain: bfloat16 [768], replicated, may hold values from 0.5 to 1.5
- ln1_bias: bfloat16 [768], replicated, may hold values from -2.5 to 2.5
- w_ffn_in: bfloat16 [2, 384, 1536], replicated, may hold values from -0.3125 to 0.3125
- w_ffn_out: bfloat16 [2, 1536, 384], replicated, may hold values from -0.15625 to 0.15625
- ln2_gain: bfloat16 [768], replicated, may hold values from 0.5 to 1.5
- ln2_bias: bfloat16 [768], replicated, may hold values from -2.5 to 2.5
Outputs:
- hidden_out: bfloat16 [16, 2048, 768], P('rows', 'seq')
- grad_in: float32 [16, 2048, 768], P('rows', 'seq')
- grad_query: float32 [768, 384], replicated
- grad_key: float32 [768, 384], replicated
- grad_value: float32 [768, 384], replicated
- grad_conv_out: float32 [768, 384], replicated
- grad_depth: float32 [9, 768], replicated
- grad_point: float32 [768, 384], replicated
- grad_conv_kernel: float32 [384, 54], replicated
- grad_output: float32 [768, 768], replicated
- grad_ln1_gain: float32 [768], replicated
- grad_ln1_bias: float32 [768], replicated
- grad_ffn_in: float32 [2, 384, 1536], replicated
- grad_ffn_out: float32 [2, 1536, 384], replicated
- grad_ln2_gain: float32 [768], replicated
- grad_ln2_bias: float32 [768], replicated
The draws below stay inside these ranges and needn't reach their ends.
Inputs may be any that keep to these rules, and one draw needn't show every extreme that they name: `doc_lengths`: in every row the 5 documents stand in this order and are followed by padding up to 2048 positions. The third has exactly 512 tokens and begins in the first half of the row and ends in the second; the first has more than 256 tokens, the second 512 / 2 or more, the fourth 40 or more; only the fifth may be empty.
All inputs are finite; a program needn't handle non-finite values.
Results may differ from the reference program's by a relative error of at most 0.013.
Values may be sent and summed in bfloat16 or wider, within the bound.
No kernel may reach another device: no remote copies, remote signals or barrier semaphores. Data moves between devices by JAX's collectives and lax.ppermute only.
A program may use at most 256 MiB of HBM per device.

```python
import jax
import jax.numpy as jnp
from jax import lax

D = 768
HEADS = 6
HEAD = 64
FF = 3072
KSIZE = 9
GROUPS = 2
MOST = 512
MIN_LEN = 40
DOCS = 5
ROW_LEN = 2048
ROWS = 16


def draw_doc_lengths(key, part):
    key_list = jax.random.split(key, 4)
    len_first = jax.random.randint(key_list[0], (ROWS, 1), MOST // 2 + 1, MOST + 1, dtype=jnp.int32)
    len_second = jax.random.randint(key_list[1], (ROWS, 1), MOST // 2, MOST, dtype=jnp.int32)
    len_middle = jnp.full((ROWS, 1), MOST, dtype=jnp.int32)
    remaining = 4 * MOST - len_first - len_second - len_middle
    len_third = jax.random.randint(key_list[2], (ROWS, 1), MIN_LEN, MOST + 1, dtype=jnp.int32)
    space_left = jnp.minimum(remaining - len_third, MOST)
    len_fourth = jax.random.randint(key_list[3], (ROWS, 1), 0, space_left + 1, dtype=jnp.int32)
    return jnp.concatenate([len_first, len_second, len_middle, len_third, len_fourth], axis=1).astype(jnp.int32)


def shard_levels(own_key, extent, cuts, low, top_value):
    def one(position, parts):
        heights = jax.random.uniform(jax.random.fold_in(jax.random.fold_in(own_key, 6), position), (parts,), jnp.float32, low / len(cuts), top_value / len(cuts))
        return jnp.repeat(jnp.exp(heights), extent[position] // parts).reshape((-1,) + (1,) * (len(extent) - position - 1))

    level = one(*cuts[0])
    for cut in cuts[1:]:
        level = level * one(*cut)
    return level


def scatter_about(own_key, shape, spread, limit, pieces=(), kind=jnp.bfloat16):
    level = shard_levels(own_key, shape, pieces, -0.22, 0.18) if pieces else 1.0
    result = jax.random.normal(own_key, shape, jnp.float32) * spread * level
    return jnp.minimum(jnp.maximum(result, -limit), limit).astype(kind)


def setup_inputs(seed: int = 0) -> dict:
    keys = jax.random.split(jax.random.key(seed), 18)
    hidden_in = scatter_about(keys[0], (ROWS, ROW_LEN, D), 1.0, 6.0, ((0, 16), (1, 2)))
    doc_lengths = draw_doc_lengths(jax.random.fold_in(keys[17], 71), 0)
    out_grad = scatter_about(keys[2], (ROWS, ROW_LEN, D), 1.0, 6.0, ((0, 16), (1, 2)))
    w_query = scatter_about(keys[3], (D, HEADS * HEAD), D ** -0.5, 0.21875)
    w_key = scatter_about(keys[4], (D, HEADS * HEAD), D ** -0.5, 0.21875)
    w_value = scatter_about(keys[5], (D, HEADS * HEAD), D ** -0.5, 0.21875)
    w_conv_out = scatter_about(keys[6], (D, HEADS * HEAD), D ** -0.5, 0.21875)
    depth_kernel = scatter_about(keys[7], (KSIZE, D), KSIZE ** -0.5, 2.0)
    w_point = scatter_about(keys[8], (D, HEADS * HEAD), D ** -0.5, 0.21875)
    w_conv_kernel = scatter_about(keys[9], (HEADS * HEAD, HEADS * KSIZE), (HEADS * HEAD) ** -0.5, 0.3125)
    w_output = scatter_about(keys[10], (D, D), (D // 16) ** -0.5, 0.875)
    ln1_gain = jnp.clip(1.0 + 0.1 * jax.random.normal(keys[11], (D,), jnp.float32), 0.5, 1.5).astype(jnp.bfloat16)
    ln1_bias = scatter_about(keys[12], (D,), 0.5, 2.5)
    w_ffn_in = scatter_about(keys[13], (GROUPS, D // GROUPS, FF // GROUPS), (D // GROUPS) ** -0.5, 0.3125)
    w_ffn_out = scatter_about(keys[14], (GROUPS, FF // GROUPS, D // GROUPS), (FF // GROUPS) ** -0.5, 0.15625)
    ln2_gain = jnp.clip(1.0 + 0.1 * jax.random.normal(keys[15], (D,), jnp.float32), 0.5, 1.5).astype(jnp.bfloat16)
    ln2_bias = scatter_about(keys[16], (D,), 0.5, 2.5)
    return {"hidden_in": hidden_in, "doc_lengths": doc_lengths, "out_grad": out_grad, "w_query": w_query, "w_key": w_key, "w_value": w_value, "w_conv_out": w_conv_out, "depth_kernel": depth_kernel, "w_point": w_point, "w_conv_kernel": w_conv_kernel, "w_output": w_output, "ln1_gain": ln1_gain, "ln1_bias": ln1_bias, "w_ffn_in": w_ffn_in, "w_ffn_out": w_ffn_out, "ln2_gain": ln2_gain, "ln2_bias": ln2_bias}


@jax.custom_vjp
def low(v):
    return lax.optimization_barrier(v.astype(jnp.bfloat16)).astype(jnp.float32)

@jax.custom_vjp
def low_back(v):
    return v

def low_keep(v):
    return (low(v), None)

def low_pass(kept, grad):
    return (grad,)

def back_keep(v):
    return (v, None)

def back_low(kept, grad):
    return (low(grad),)
low.defvjp(low_keep, low_pass)
low_back.defvjp(back_keep, back_low)

def matmul(left, right):
    return jnp.dot(left, right, precision=lax.Precision.HIGHEST)

def layer_norm(values, gain, norm_bias):
    centred = values - lax.optimization_barrier(jnp.mean(values, axis=-1, keepdims=True))
    variance = lax.optimization_barrier(jnp.mean(centred * centred, axis=-1, keepdims=True))
    return centred * lax.rsqrt(variance + 1e-06) * gain + norm_bias

def softmax_last(values):
    shifted = values - lax.optimization_barrier(jnp.max(values, axis=-1, keepdims=True))
    powers = jnp.exp(shifted)
    return powers / lax.optimization_barrier(jnp.sum(powers, axis=-1, keepdims=True))

def gelu_exact(values):
    return 0.5 * values * (1.0 + jax.scipy.special.erf(values * 0.7071067811865476))

def row_segments(lengths, places):
    doc_ends = jnp.cumsum(lengths)
    return lax.optimization_barrier(jnp.sum((places[:, None] >= doc_ends[None, :]).astype(jnp.int32), axis=1))

def row_forward(hidden, lengths, params):
    w_query, w_key, w_value, w_conv_out, depth_kernel, w_point, w_conv_kernel, w_output, ln1_gain, ln1_bias, w_ffn_in, w_ffn_out, ln2_gain, ln2_bias = params
    half_kernel = KSIZE // 2
    attn_width = HEADS * HEAD
    places = jnp.arange(-half_kernel, ROW_LEN + half_kernel, dtype=jnp.int32)
    seg_ext = row_segments(lengths, places)
    seg_row = seg_ext[half_kernel:half_kernel + ROW_LEN]
    valid_mask = (seg_row < DOCS).astype(jnp.float32)
    same_list = [(seg_ext[offset:offset + ROW_LEN] == seg_row).astype(jnp.float32) for offset in range(KSIZE)]
    query_proj = low(low_back(matmul(hidden, w_query)))
    key_proj = low(low_back(matmul(hidden, w_key)))
    value_proj = low(low_back(matmul(hidden, w_value)))
    conv_values = low(low_back(matmul(hidden, w_conv_out)))
    padded = jnp.pad(hidden, ((half_kernel, half_kernel), (0, 0)))
    depth_out = jnp.zeros((ROW_LEN, D), jnp.float32)
    for offset in range(KSIZE):
        depth_out = depth_out + padded[offset:offset + ROW_LEN] * depth_kernel[offset] * same_list[offset][:, None]
    depth_out = low(depth_out)
    conv_key = low_back(matmul(depth_out, w_point))
    mixed_key = low(conv_key * query_proj)
    logits = low_back(matmul(mixed_key, w_conv_kernel)).reshape(ROW_LEN, HEADS, KSIZE)
    kernel = softmax_last(logits)
    value_heads = jnp.pad(conv_values.reshape(ROW_LEN, HEADS, HEAD), ((half_kernel, half_kernel), (0, 0), (0, 0)))
    conv_mix = jnp.zeros((ROW_LEN, HEADS, HEAD), jnp.float32)
    for offset in range(KSIZE):
        conv_mix = conv_mix + kernel[:, :, offset:offset + 1] * same_list[offset][:, None, None] * value_heads[offset:offset + ROW_LEN]
    score_scale = float(HEAD) ** (-0.5)
    query_heads = query_proj.reshape(ROW_LEN, HEADS, HEAD)
    key_heads = key_proj.reshape(ROW_LEN, HEADS, HEAD)
    scores = low_back(jnp.einsum('qhd,khd->hqk', query_heads, key_heads, precision=lax.Precision.HIGHEST) * score_scale)
    same_doc = seg_row[:, None] == seg_row[None, :]
    scores = jnp.where(same_doc[None], scores, -1e+30)
    attn_probs = low(softmax_last(scores))
    context = low_back(jnp.einsum('hqk,khd->qhd', attn_probs, value_proj.reshape(ROW_LEN, HEADS, HEAD), precision=lax.Precision.HIGHEST)).reshape(ROW_LEN, attn_width)
    mixed_heads = low(jnp.concatenate([context, conv_mix.reshape(ROW_LEN, attn_width)], axis=1))
    attended = low_back(matmul(mixed_heads, w_output))
    first_norm = layer_norm(hidden + attended, ln1_gain, ln1_bias)
    ffn_input = low(first_norm).reshape(ROW_LEN, GROUPS, D // GROUPS)
    ffn_hidden = low_back(jnp.einsum('tgi,gio->tgo', ffn_input, w_ffn_in, precision=lax.Precision.HIGHEST))
    active = low(gelu_exact(ffn_hidden))
    ffn_out = low_back(jnp.einsum('tgi,gio->tgo', active, w_ffn_out, precision=lax.Precision.HIGHEST)).reshape(ROW_LEN, D)
    return layer_norm(first_norm + ffn_out, ln2_gain, ln2_bias) * valid_mask[:, None]

def reference(hidden_in, doc_lengths, out_grad, w_query, w_key, w_value, w_conv_out, depth_kernel, w_point, w_conv_kernel, w_output, ln1_gain, ln1_bias, w_ffn_in, w_ffn_out, ln2_gain, ln2_bias):
    params = (w_query.astype(jnp.float32), w_key.astype(jnp.float32), w_value.astype(jnp.float32), w_conv_out.astype(jnp.float32), depth_kernel.astype(jnp.float32), w_point.astype(jnp.float32), w_conv_kernel.astype(jnp.float32), w_output.astype(jnp.float32), ln1_gain.astype(jnp.float32), ln1_bias.astype(jnp.float32), w_ffn_in.astype(jnp.float32), w_ffn_out.astype(jnp.float32), ln2_gain.astype(jnp.float32), ln2_bias.astype(jnp.float32))
    hidden = hidden_in.astype(jnp.float32)
    cotangent = out_grad.astype(jnp.float32)

    def forward(hidden_all, weights):

        def one_row(carry, row_item):
            row_hidden, lengths = row_item
            return (carry, row_forward(row_hidden, lengths, weights))
        unused, outputs = lax.scan(jax.checkpoint(one_row), jnp.zeros((), jnp.float32), (hidden_all, doc_lengths))
        return outputs
    outputs, pullback = jax.vjp(forward, hidden, params)
    grad_hidden, grad_params = pullback(cotangent)
    query_grad, key_grad, value_grad, conv_out_grad, depth_grad, point_grad, conv_kernel_grad, output_grad, gain_one_grad, bias_one_grad, ffn_in_grad, ffn_out_grad, gain_two_grad, bias_two_grad = grad_params
    return (outputs.astype(jnp.bfloat16), grad_hidden, query_grad, key_grad, value_grad, conv_out_grad, depth_grad, point_grad, conv_kernel_grad, output_grad, gain_one_grad, bias_one_grad, ffn_in_grad, ffn_out_grad, gain_two_grad, bias_two_grad)
```

```python
import jax
import jax.numpy as jnp
from jax import lax
from jax.experimental import pallas as pl
from jax.experimental.pallas import tpu as pltpu
from jax.sharding import PartitionSpec as P

KSIZE = 9

HEADS=6
BLK=256
NEG=-1e30
f32=jnp.float32; bf16=jnp.bfloat16

def dot_nt(a,b):
    return lax.dot_general(a,b,(((1,),(1,)),((),())),preferred_element_type=f32)
def dot_nn(a,b):
    return lax.dot_general(a,b,(((1,),(0,)),((),())),preferred_element_type=f32)
def dot_tn(a,b):
    return lax.dot_general(a,b,(((0,),(0,)),((),())),preferred_element_type=f32)

def segs(meta, first, shape):
    pos=first+lax.broadcasted_iota(jnp.int32,shape,0)
    seg=jnp.zeros(shape,jnp.int32)
    for d in range(5):
        seg=seg+jnp.where(pos>=meta[d],1,0)
    return seg

def key_ext(meta, first, n):
    lane=lax.broadcasted_iota(jnp.int32,(n,128),1)
    seg=segs(meta,first,(n,128))
    diff=(lane>=24)&(lane<30)&(lane-24!=seg)
    return jnp.where(lane<24,-1.0,jnp.where(diff,NEG,0.0)).astype(bf16)

def fwd_kernel(meta, q_ref, k_ref, v_ref, ctx_ref, lse_ref, kx_ref, s_ref, m_ref, acc_ref):
    nkb=k_ref.shape[0]//BLK; nqb=q_ref.shape[0]//BLK; npair=HEADS//2
    for b in range(nkb):
        kx_ref[b*BLK:(b+1)*BLK,:]=key_ext(meta,meta[5]+b*BLK,BLK)
    lane=lax.broadcasted_iota(jnp.int32,(BLK,128),1)
    ones_lane=jnp.where(lane==0,1.0,0.0).astype(bf16)
    for qb in range(nqb):
        qrows=slice(qb*BLK,(qb+1)*BLK)
        seg=segs(meta,meta[6]+qb*BLK,(BLK,128))
        qext=jnp.where(lane-24==seg,1.0,0.0).astype(bf16)
        lo=meta[8+2*qb]; hi=meta[9+2*qb]
        m_ref[...]=jnp.full(m_ref.shape,NEG,f32)
        acc_ref[...]=jnp.zeros(acc_ref.shape,f32)
        def phase1(kb,_):
            r0=pl.multiple_of(kb*BLK,BLK)
            kext=kx_ref[pl.ds(r0,BLK),:]
            for j in range(npair):
                kk=jnp.concatenate([k_ref[pl.ds(r0,BLK),j*128:(j+1)*128],kext],axis=1)
                qp=q_ref[qrows,j*128:(j+1)*128]*jnp.asarray(0.125,bf16)
                for hh in range(2):
                    h=2*j+hh
                    qm=jnp.where((lane<64) if hh==0 else (lane>=64),qp,jnp.zeros_like(qp))
                    s=dot_nt(jnp.concatenate([qm,qext],axis=1),kk)
                    s_ref[h,:,pl.ds(r0,BLK)]=s
                    m_ref[h]=jnp.maximum(m_ref[h],jnp.maximum(s[:,:128],s[:,128:]))
            return 0
        lax.fori_loop(lo,hi,phase1,0)
        for h in range(HEADS):
            m_ref[h]=jnp.broadcast_to(jnp.max(m_ref[h],axis=1,keepdims=True),(BLK,128))
        def phase2(kb,_):
            r0=pl.multiple_of(kb*BLK,BLK)
            for j in range(npair):
                vv=jnp.concatenate([v_ref[pl.ds(r0,BLK),j*128:(j+1)*128],ones_lane],axis=1)
                for hh in range(2):
                    h=2*j+hh
                    mm=m_ref[h]
                    p=jnp.exp(s_ref[h,:,pl.ds(r0,BLK)]-jnp.concatenate([mm,mm],axis=1)).astype(bf16)
                    acc_ref[h]=acc_ref[h]+dot_nn(p,vv)
            return 0
        lax.fori_loop(lo,hi,phase2,0)
        lse_all=jnp.zeros((BLK,128),f32)
        for j in range(npair):
            parts=[]
            for hh in range(2):
                h=2*j+hh
                l=jnp.broadcast_to(acc_ref[h][:,128:129],(BLK,128))
                parts.append(acc_ref[h][:,:128]/l)
                lse=m_ref[h]+jnp.log(l)
                sel=(lane==h)|(lane==h+8)|(lane==h+16)
                lse_all=jnp.where(sel,lse,lse_all)
            ctx_ref[qrows,j*128:(j+1)*128]=jnp.where(lane<64,parts[0],parts[1]).astype(ctx_ref.dtype)
        lse_ref[qrows,:]=lse_all

def bwd_kernel(pair, meta, q_ref, k_ref, v_ref, ctx_ref, dctx_ref, lse_ref, dq_ref, dko_ref, dvo_ref, dkv_ref, kx_ref, dk_ref, dv_ref):
    nkb=k_ref.shape[0]//BLK; nqb=q_ref.shape[0]//BLK; npair=1
    width=128
    for b in range(nkb):
        kx_ref[b*BLK:(b+1)*BLK,:]=key_ext(meta,meta[5]+b*BLK,BLK)
    dk_ref[...]=jnp.zeros(dk_ref.shape,f32)
    dv_ref[...]=jnp.zeros(dv_ref.shape,f32)
    dq_ref[...]=jnp.zeros(dq_ref.shape,f32)
    lane=lax.broadcasted_iota(jnp.int32,(BLK,128),1)
    vext=jnp.where(lane<16,-1.0,0.0).astype(bf16)
    r=2*pair+lax.broadcasted_iota(jnp.int32,(width,128),0)//64
    cl=lax.broadcasted_iota(jnp.int32,(width,128),1)
    heads_of=jnp.where((cl<16)&(cl%8==r),1.0,0.0).astype(bf16)
    low=lane<64
    for qb in range(nqb):
        qrows=slice(qb*BLK,(qb+1)*BLK)
        seg=segs(meta,meta[6]+qb*BLK,(BLK,128))
        onehot=lane-24==seg
        lse=lse_ref[qrows,:]
        hi_=lse.astype(bf16).astype(f32)
        r1=lse-hi_
        mid=r1.astype(bf16).astype(f32)
        lo_=r1-mid
        split=jnp.where(lane<8,hi_,jnp.where(lane<16,mid,lo_))
        prod=ctx_ref[qrows,:].astype(f32)*dctx_ref[qrows,:].astype(f32)
        ph=prod.astype(bf16)
        plo=(prod-ph.astype(f32)).astype(bf16)
        dd=dot_nn(ph,heads_of)+dot_nn(plo,heads_of)
        dh=dd.astype(bf16).astype(f32)
        dsplit=jnp.where(lane<8,dh,dd-dh)
        qx=[];dcx=[];qms=[];dcs=[]
        for h in (2*pair,2*pair+1):
            side=low if h%2==0 else ~low
            qp=q_ref[qrows,:]*jnp.asarray(0.125,bf16)
            qm=jnp.where(side,qp,jnp.zeros_like(qp))
            sel=(lane==h)|(lane==h+8)|(lane==h+16)
            qe=jnp.where(sel,split,jnp.where(onehot,1.0,0.0)).astype(bf16)
            qx.append(jnp.concatenate([qm,qe],axis=1))
            dp=dctx_ref[qrows,:]
            dm=jnp.where(side,dp,jnp.zeros_like(dp))
            de=jnp.where((lane==h)|(lane==h+8),dsplit,0.0).astype(bf16)
            dcx.append(jnp.concatenate([dm,de],axis=1))
            qms.append(qm);dcs.append(dm)
        lo=meta[8+2*qb]; hi=meta[9+2*qb]
        def body(kb,_):
            r0=pl.multiple_of(kb*BLK,BLK)
            kext=kx_ref[pl.ds(r0,BLK),:]
            for j in range(npair):
                cols=slice(j*128,(j+1)*128)
                kp=k_ref[pl.ds(r0,BLK),cols]
                kk=jnp.concatenate([kp,kext],axis=1)
                vv=jnp.concatenate([v_ref[pl.ds(r0,BLK),cols],vext],axis=1)
                pts=[];dss=[];ks=[]
                for hh in range(2):
                    pt=jnp.exp(dot_nt(kk,qx[hh]))
                    dpt=dot_nt(vv,dcx[hh])
                    pts.append(pt.astype(bf16))
                    dss.append((pt*dpt).astype(bf16))
                    ks.append(jnp.where(low if hh==0 else ~low,kp,jnp.zeros_like(kp)))
                dv_ref[pl.ds(r0,BLK),cols]+=dot_nn(jnp.concatenate(pts,axis=1),jnp.concatenate(dcs[2*j:2*j+2],axis=0))
                dk_ref[pl.ds(r0,BLK),cols]+=dot_nn(jnp.concatenate(dss,axis=1),jnp.concatenate(qms[2*j:2*j+2],axis=0))
                dq_ref[qrows,cols]+=dot_tn(jnp.concatenate(dss,axis=0),jnp.concatenate(ks,axis=0))
            return 0
        lax.fori_loop(lo,hi,body,0)
        dq_ref[qrows,:]=dq_ref[qrows,:]*0.125
    n=q_ref.shape[0]; half=dkv_ref.shape[0]
    own_off=meta[7]*half; halo_off=(1-meta[7])*n
    for b in range(n//BLK):
        src=pl.multiple_of(own_off+b*BLK,BLK)
        dko_ref[b*BLK:(b+1)*BLK,:]=dk_ref[pl.ds(src,BLK),:]
        dvo_ref[b*BLK:(b+1)*BLK,:]=dv_ref[pl.ds(src,BLK),:]
    for b in range(half//BLK):
        src=pl.multiple_of(halo_off+b*BLK,BLK)
        dkv_ref[b*BLK:(b+1)*BLK,:width]=dk_ref[pl.ds(src,BLK),:].astype(bf16)
        dkv_ref[b*BLK:(b+1)*BLK,width:]=dv_ref[pl.ds(src,BLK),:].astype(bf16)

VM=pl.BlockSpec(memory_space=pltpu.VMEM)
SM=pl.BlockSpec(memory_space=pltpu.SMEM)
def attn_fwd(meta,q,k,v):
    t,w=q.shape
    return pl.pallas_call(fwd_kernel,in_specs=[SM,VM,VM,VM],out_specs=[VM,VM],
        out_shape=[jax.ShapeDtypeStruct((t,w),bf16),jax.ShapeDtypeStruct((t,128),f32)],
        scratch_shapes=[pltpu.VMEM((k.shape[0],128),bf16),pltpu.VMEM((HEADS,BLK,k.shape[0]),f32),
            pltpu.VMEM((HEADS,BLK,128),f32),pltpu.VMEM((HEADS,BLK,256),f32)],
        compiler_params=pltpu.CompilerParams(vmem_limit_bytes=56*2**20),cost_estimate=cost(15.0),name="attn_fwd")(meta,q,k,v)
def attn_bwd(meta,pair,q,k,v,ctx,dctx,lse,carry):
    t,w=q.shape; kn=k.shape[0]
    sd=jax.ShapeDtypeStruct
    def col(n,width):
        return pl.BlockSpec((n,width),lambda i,_pair=pair:(0,_pair))
    def kernel(*refs):
        ins=refs[:7]; outs=refs[-7:]
        bwd_kernel(pair,*ins,*outs)
    first=carry is None
    carry=() if first else tuple(carry)
    return pl.pallas_call(kernel,grid=(1,),
        in_specs=[SM,col(t,128),col(kn,128),col(kn,128),col(t,128),col(t,128),pl.BlockSpec((t,128),lambda i:(0,0))]+[pl.BlockSpec(memory_space=pl.ANY)]*len(carry),
        out_specs=[col(t,128)]*3+[col(kn-t,256)],
        out_shape=[sd((t,w),f32)]*3+[sd((kn-t,2*w),bf16)],
        scratch_shapes=[pltpu.VMEM((kn,128),bf16),pltpu.VMEM((kn,128),f32),pltpu.VMEM((kn,128),f32)],
        input_output_aliases={} if first else {7:0,8:1,9:2,10:3},cost_estimate=cost(8.0),
        compiler_params=pltpu.CompilerParams(vmem_limit_bytes=48*2**20),name="attn_bwd")(meta,q,k,v,ctx,dctx,lse,*carry)

def make_meta(lengths, side, local, full):
    ends=jnp.cumsum(lengths)
    starts=ends-lengths
    win=side*(local//2); own=side*local
    nqb=local//BLK
    b0=own+jnp.arange(nqb)*BLK
    b1=b0+BLK-1
    bounds_lo=jnp.concatenate([jnp.zeros((1,),jnp.int32),ends])
    bounds_hi=jnp.concatenate([ends,jnp.full((1,),full,jnp.int32)])
    seg0=jnp.sum((b0[:,None]>=ends[None]).astype(jnp.int32),1)
    seg1=jnp.sum((b1[:,None]>=ends[None]).astype(jnp.int32),1)
    first=jnp.sum(jnp.where(jnp.arange(6)[None]==seg0[:,None],bounds_lo[None],0),1)
    last=jnp.sum(jnp.where(jnp.arange(6)[None]==seg1[:,None],bounds_hi[None],0),1)
    lo=jnp.maximum(first-win,0)//BLK
    hi=jnp.minimum((last-win+BLK-1)//BLK,(local+local//2)//BLK)
    return jnp.concatenate([ends,win[None],own[None],side[None],jnp.stack([lo,hi],1).reshape(-1)]).astype(jnp.int32)

TB=256

def gelu_parts(z):
    a=jnp.abs(z)
    t=1.0/(1.0+a*(0.3275911*0.7071067811865476))
    e=jnp.exp(-0.5*z*z)
    poly=t*(0.127414796+t*(-0.142248368+t*(0.7107068705+t*(-0.7265760135+t*0.5307027145))))
    ht=poly*e
    phi=jnp.where(z>=0.0,1.0-ht,ht)
    return z*phi, phi+z*(e*0.3989422804014327)

def rows8(x):
    return jnp.sum(x.reshape(x.shape[0]//8,8,x.shape[1]),axis=0)

def norm_parts(z):
    mu=jnp.mean(z,axis=-1,keepdims=True)
    c=z-mu
    var=jnp.mean(c*c,axis=-1,keepdims=True)
    rstd=lax.rsqrt(var+1e-6)
    return c*rstd, rstd

def norm_back(d, gain, xhat, rstd):
    dx=d*gain
    a=jnp.mean(dx,axis=-1,keepdims=True)
    b=jnp.mean(dx*xhat,axis=-1,keepdims=True)
    return rstd*(dx-a-xhat*b)

def ffn_kernel(meta, hid_ref, ctx_ref, cm_ref, og_ref, wo_ref, win_ref, wout_ref, ln_ref,
               ho_ref, dres_ref, dctx_ref, dconv_ref, keep_ref, send_ref, gln_ref,
               act_ref, dff_ref, x1_ref, dfo_ref, datt_ref, gp_ref, mix_ref):
    n=hid_ref.shape[0]; d=hid_ref.shape[1]; groups=win_ref.shape[0]; gi=d//groups; go=win_ref.shape[2]
    attn=dctx_ref.shape[1]
    tile=512
    gln_ref[...]=jnp.zeros(gln_ref.shape,f32)
    def block(i,_):
        r0=pl.multiple_of(i*TB,TB)
        rows=pl.ds(r0,TB)
        g1=ln_ref[0:1,:];b1=ln_ref[1:2,:];g2=ln_ref[2:3,:];b2=ln_ref[3:4,:]
        att=dot_nn(jnp.concatenate([ctx_ref[rows,:],cm_ref[rows,:]],axis=1),wo_ref[...])
        xhat1,rstd1=norm_parts(hid_ref[rows,:].astype(f32)+att)
        first=xhat1*g1+b1
        x1=first.astype(bf16)
        for g in range(groups):
            x1_ref[g,rows,:]=x1[:,g*gi:(g+1)*gi]
        mix_ref[0,rows,:]=ctx_ref[rows,:]
        mix_ref[1,rows,:]=cm_ref[rows,:]
        outs=[]
        for g in range(groups):
            acc=None
            for c in range(go//tile):
                cols=slice(c*tile,(c+1)*tile)
                gc=slice(g*go+c*tile,g*go+(c+1)*tile)
                z=dot_nn(x1[:,g*gi:(g+1)*gi],win_ref[g,:,cols])
                a,gp=gelu_parts(z)
                ab=a.astype(bf16)
                act_ref[g,rows,cols]=ab
                gp_ref[:,gc]=gp
                o=dot_nn(ab,wout_ref[g,cols,:])
                acc=o if acc is None else acc+o
            outs.append(acc)
        xhat2,rstd2=norm_parts(first+jnp.concatenate(outs,axis=1))
        pos=meta[6]+r0+lax.broadcasted_iota(jnp.int32,(TB,d),0)
        valid=pos<meta[4]
        ho_ref[rows,:]=jnp.where(valid,xhat2*g2+b2,0.0).astype(bf16)
        gn=jnp.where(valid,og_ref[rows,:].astype(f32),0.0)
        gln_ref[16:24,:]+=rows8(gn*xhat2)
        gln_ref[24:32,:]+=rows8(gn)
        dres2=norm_back(gn,g2,xhat2,rstd2)
        dfo=dres2.astype(bf16)
        for g in range(groups):
            dfo_ref[g,rows,:]=dfo[:,g*gi:(g+1)*gi]
        backs=[]
        for g in range(groups):
            acc=None
            for c in range(go//tile):
                cols=slice(c*tile,(c+1)*tile)
                gc=slice(g*go+c*tile,g*go+(c+1)*tile)
                da=dot_nt(dfo[:,g*gi:(g+1)*gi],wout_ref[g,cols,:])
                dh=(da*gp_ref[:,gc]).astype(bf16)
                dff_ref[g,rows,cols]=dh
                o=dot_nt(dh,win_ref[g,:,cols])
                acc=o if acc is None else acc+o
            backs.append(acc)
        dfirst=dres2+jnp.concatenate(backs,axis=1)
        gln_ref[0:8,:]+=rows8(dfirst*xhat1)
        gln_ref[8:16,:]+=rows8(dfirst)
        dres1=norm_back(dfirst,g1,xhat1,rstd1)
        dres_ref[rows,:]=dres1
        datt=dres1.astype(bf16)
        datt_ref[rows,:]=datt
        dm=dot_nt(datt,wo_ref[...])
        dctx_ref[rows,:]=dm[:,:attn].astype(bf16)
        dconv_ref[rows,:]=dm[:,attn:]
        return 0
    lax.fori_loop(0,n//TB,block,0)
    side=meta[7]
    for ref,g in ((send_ref,1-side),(keep_ref,side)):
        at=0
        for c in range(go//gi):
            ref[at*gi:(at+1)*gi,:]=dot_tn(act_ref[g,:,c*gi:(c+1)*gi],dfo_ref[g]).astype(ref.dtype)
            at+=1
        for c in range(go//gi):
            ref[at*gi:(at+1)*gi,:]=dot_tn(x1_ref[g],dff_ref[g,:,c*gi:(c+1)*gi]).astype(ref.dtype)
            at+=1
        for c in range(d//attn):
            ref[at*gi:(at+1)*gi,:]=dot_tn(mix_ref[g],datt_ref[:,c*attn:(c+1)*attn]).astype(ref.dtype)
            at+=1

def ffn(meta,hid,ctx,cm,og,wo,win,wout,ln):
    n,d=hid.shape; g,gi,go=win.shape; attn=ctx.shape[1]
    sd=jax.ShapeDtypeStruct
    return pl.pallas_call(ffn_kernel,in_specs=[SM]+[VM]*8,out_specs=[VM]*7,
        out_shape=[sd((n,d),bf16),sd((n,d),f32),sd((n,attn),bf16),sd((n,attn),f32),
                   sd((2*go+d,attn),bf16),sd((2*go+d,attn),bf16),sd((32,d),f32)],
        scratch_shapes=[pltpu.VMEM((g,n,go),bf16),pltpu.VMEM((g,n,go),bf16),pltpu.VMEM((g,n,gi),bf16),
                        pltpu.VMEM((g,n,gi),bf16),pltpu.VMEM((n,d),bf16),pltpu.VMEM((TB,g*go),f32),pltpu.VMEM((2,n,attn),bf16)],
        cost_estimate=cost(40.0),compiler_params=pltpu.CompilerParams(vmem_limit_bytes=60*2**20),name="ffn")(meta,hid,ctx,cm,og,wo,win,wout,ln)

TAPS=9
HALF=4
PAD=8
TB=256
CH=64
CS=32

def doc_bounds(meta, first, shape):
    pos=first+lax.broadcasted_iota(jnp.int32,shape,0)
    nxt=jnp.full(shape,2**30,jnp.int32)
    prv=jnp.full(shape,-2**30,jnp.int32)
    for d in range(5):
        e=meta[d]
        nxt=jnp.minimum(nxt,jnp.where(e>pos,e,2**30))
        prv=jnp.maximum(prv,jnp.where(e<=pos,e,-2**30))
    return nxt-pos, pos-prv

def tap_mask(bounds, o):
    rem,age=bounds
    if o>HALF:
        return rem>(o-HALF)
    return age>=(HALF-o)

def masked(x, bounds, o):
    if o==HALF:
        return x
    return jnp.where(tap_mask(bounds,o),x,0.0)

def tap_onehot(rows, cols, o):
    r=lax.broadcasted_iota(jnp.int32,(rows,cols),0)
    c=lax.broadcasted_iota(jnp.int32,(rows,cols),1)
    return jnp.where(r==(c//64)*TAPS+o,1.0,0.0).astype(bf16)

def pre_kernel(meta, hid_ref, halo_ref, wq_ref, wk_ref, wv_ref, wc_ref, taps_ref, wp_ref, wck_ref,
               q_ref, kw_ref, vw_ref, cx_ref, depth_ref, ck_ref, kern_ref, cm_ref,
               hx_ref, wx_ref, lx_ref):
    n,d=hid_ref.shape; half=halo_ref.shape[0]; attn=q_ref.shape[1]
    side=meta[7]
    own_off=side*half; halo_off=(1-side)*n
    jt=attn//128; jd=d//128
    for o in range(TAPS):
        wx_ref[:,o*attn:(o+1)*attn]=dot_nn(wck_ref[...],tap_onehot(HEADS*TAPS,attn,o)).astype(bf16)
    left=jnp.where(side==1,halo_ref[half-16:half,:].astype(f32),0.0)
    right=jnp.where(side==0,halo_ref[0:16,:].astype(f32),0.0)
    rims=jnp.concatenate([left,right],axis=0).astype(bf16)
    crim=dot_nn(rims,wc_ref[...]).astype(bf16).astype(f32)
    for j in range(jd):
        hx_ref[j,0:PAD,:]=left[PAD:2*PAD,j*128:(j+1)*128]
        hx_ref[j,n+PAD:n+2*PAD,:]=right[0:PAD,j*128:(j+1)*128]
    for j in range(jt):
        cx_ref[j,0:PAD,:]=crim[PAD:2*PAD,j*128:(j+1)*128]
        cx_ref[j,n+PAD:n+2*PAD,:]=crim[16:16+PAD,j*128:(j+1)*128]
    def project(i,_):
        r0=pl.multiple_of(i*TB,TB)
        x=hid_ref[pl.ds(r0,TB),:]
        q_ref[pl.ds(r0,TB),:]=dot_nn(x,wq_ref[...]).astype(bf16)
        ow=pl.multiple_of(own_off+r0,TB)
        kw_ref[pl.ds(ow,TB),:]=dot_nn(x,wk_ref[...]).astype(bf16)
        vw_ref[pl.ds(ow,TB),:]=dot_nn(x,wv_ref[...]).astype(bf16)
        c=dot_nn(x,wc_ref[...]).astype(bf16).astype(f32)
        rp=pl.multiple_of(r0+PAD,PAD)
        for j in range(jt):
            cx_ref[j,pl.ds(rp,TB),:]=c[:,j*128:(j+1)*128]
        xf=x.astype(f32)
        for j in range(jd):
            hx_ref[j,pl.ds(rp,TB),:]=xf[:,j*128:(j+1)*128]
        return 0
    lax.fori_loop(0,n//TB,project,0)
    def project_halo(i,_):
        r0=pl.multiple_of(i*TB,TB)
        x=halo_ref[pl.ds(r0,TB),:]
        ow=pl.multiple_of(halo_off+r0,TB)
        kw_ref[pl.ds(ow,TB),:]=dot_nn(x,wk_ref[...]).astype(bf16)
        vw_ref[pl.ds(ow,TB),:]=dot_nn(x,wv_ref[...]).astype(bf16)
        return 0
    lax.fori_loop(0,half//TB,project_halo,0)
    def depthwise(i,_):
        r0=pl.multiple_of(i*CH,CH)
        bounds=doc_bounds(meta,meta[6]+r0,(CH,128))
        for j in range(jd):
            acc=None
            for o in range(TAPS):
                x=hx_ref[j,pl.ds(r0+PAD+o-HALF,CH),:]
                term=masked(x*taps_ref[o:o+1,j*128:(j+1)*128].astype(f32),bounds,o)
                acc=term if acc is None else acc+term
            depth_ref[pl.ds(r0,CH),j*128:(j+1)*128]=acc.astype(bf16)
        return 0
    lax.fori_loop(0,n//CH,depthwise,0)
    def dynamic(i,_):
        r0=pl.multiple_of(i*TB,TB)
        ck=dot_nn(depth_ref[pl.ds(r0,TB),:],wp_ref[...])
        ck_ref[pl.ds(r0,TB),:]=ck
        mk=(ck*q_ref[pl.ds(r0,TB),:].astype(f32)).astype(bf16)
        for o in range(TAPS):
            lx_ref[o]=dot_nn(mk,wx_ref[:,o*attn:(o+1)*attn])
        def soft(s,_):
            s0=pl.multiple_of(s*CS,CS)
            rows=pl.ds(s0,CS)
            t0=pl.multiple_of(r0+s0,CS)
            bounds=doc_bounds(meta,meta[6]+t0,(CS,128))
            for j in range(jt):
                cols=slice(j*128,(j+1)*128)
                ls=[lx_ref[o,rows,cols] for o in range(TAPS)]
                m=ls[0]
                for o in range(1,TAPS):
                    m=jnp.maximum(m,ls[o])
                es=[jnp.exp(l-m) for l in ls]
                tot=es[0]
                for o in range(1,TAPS):
                    tot=tot+es[o]
                inv=1.0/tot
                acc=None
                for o in range(TAPS):
                    k=es[o]*inv
                    kern_ref[o,pl.ds(t0,CS),cols]=k.astype(bf16)
                    term=masked(k*cx_ref[j,pl.ds(t0+PAD+o-HALF,CS),:],bounds,o)
                    acc=term if acc is None else acc+term
                cm_ref[pl.ds(t0,CS),cols]=acc.astype(bf16)
            return 0
        lax.fori_loop(0,TB//CS,soft,0)
        return 0
    lax.fori_loop(0,n//TB,dynamic,0)

def pre(meta,hid,halo,wq,wk,wv,wc,taps,wp,wck):
    n,d=hid.shape; half=halo.shape[0]; a=wq.shape[1]; sd=jax.ShapeDtypeStruct
    return pl.pallas_call(pre_kernel,in_specs=[SM]+[VM]*9,out_specs=[VM]*8,
        out_shape=[sd((n,a),bf16),sd((n+half,a),bf16),sd((n+half,a),bf16),sd((a//128,n+2*PAD,128),f32),
                   sd((n,d),bf16),sd((n,a),f32),sd((TAPS,n,a),bf16),sd((n,a),bf16)],
        scratch_shapes=[pltpu.VMEM((d//128,n+2*PAD,128),f32),pltpu.VMEM((a,TAPS*a),bf16),pltpu.VMEM((TAPS,TB,a),f32)],
        cost_estimate=cost(30.0),compiler_params=pltpu.CompilerParams(vmem_limit_bytes=60*2**20),name="pre")(meta,hid,halo,wq,wk,wv,wc,taps,wp,wck)

def conv_back_kernel(meta, hid_ref, halo_ref, dconv_ref, cm_ref, kern_ref, cx_ref, q_ref, ck_ref, depth_ref,
                     taps_ref, wp_ref, wck_ref,
                     dqc_ref, dc_ref, dh_ref, rim_ref, gp_ref, gtap_ref,
                     p_ref, pr_ref, dd_ref, dlc_ref, mk_ref, dck_ref, wcx_ref):
    n,d=hid_ref.shape; half=halo_ref.shape[0]; attn=q_ref.shape[1]
    side=meta[7]; jt=attn//128; jd=d//128
    zero=jnp.zeros((2*PAD,128),f32)
    for j in range(jt):
        for o in range(TAPS):
            p_ref[o,j,0:2*PAD,:]=zero
            p_ref[o,j,n+2*PAD:n+4*PAD,:]=zero
    for j in range(jd):
        dd_ref[j,0:2*PAD,:]=zero
        dd_ref[j,n+2*PAD:n+4*PAD,:]=zero
    r=lax.broadcasted_iota(jnp.int32,(HEADS*TAPS,attn),0)
    c=lax.broadcasted_iota(jnp.int32,(HEADS*TAPS,attn),1)
    spread=jnp.where((c%64<TAPS)&(r==(c//64)*TAPS+c%64),1.0,0.0).astype(bf16)
    wcx_ref[...]=dot_nn(wck_ref[...],spread).astype(bf16)
    def ones_block(w):
        return jnp.where(lax.broadcasted_iota(jnp.int32,(w,w),0)//64==lax.broadcasted_iota(jnp.int32,(w,w),1)//64,1.0,0.0).astype(bf16)
    ones256=ones_block(256); ones128=ones_block(128)
    lane=lax.broadcasted_iota(jnp.int32,(TB,attn),1)%64
    def dynamic(i,_):
        r0=pl.multiple_of(i*TB,TB)
        rows=pl.ds(r0,TB)
        def products(s,_):
            s0=pl.multiple_of(s*CS,CS)
            t0=pl.multiple_of(r0+s0,CS)
            bounds=doc_bounds(meta,meta[6]+t0,(CS,128))
            for j in range(jt):
                cols=slice(j*128,(j+1)*128)
                g=dconv_ref[pl.ds(t0,CS),cols]
                cm=cm_ref[pl.ds(t0,CS),cols].astype(f32)
                for o in range(TAPS):
                    cs=masked(cx_ref[j,pl.ds(t0+PAD+o-HALF,CS),:],bounds,o)
                    pr_ref[o,pl.ds(s0,CS),cols]=(g*(cs-cm)).astype(bf16)
                    p_ref[o,j,pl.ds(t0+2*PAD,CS),:]=masked(kern_ref[o,pl.ds(t0,CS),cols].astype(f32)*g,bounds,o)
            return 0
        lax.fori_loop(0,TB//CS,products,0)
        dl=jnp.zeros((TB,attn),f32)
        for o in range(TAPS):
            pr=pr_ref[o]
            dk=jnp.concatenate([dot_nn(pr[:,:256],ones256),dot_nn(pr[:,256:],ones128)],axis=1)
            dl=jnp.where(lane==o,kern_ref[o,rows,:].astype(f32)*dk,dl)
        dlb=dl.astype(bf16)
        dlc_ref[rows,:]=dlb
        dmk=dot_nt(dlb,wcx_ref[...])
        q=q_ref[rows,:].astype(f32)
        ck=ck_ref[rows,:]
        mk_ref[rows,:]=(ck*q).astype(bf16)
        dqc_ref[rows,:]=dmk*ck
        dck=(dmk*q).astype(bf16)
        dck_ref[rows,:]=dck
        dd=dot_nt(dck,wp_ref[...])
        rp=pl.multiple_of(r0+2*PAD,PAD)
        for j in range(jd):
            dd_ref[j,pl.ds(rp,TB),:]=dd[:,j*128:(j+1)*128]
        return 0
    lax.fori_loop(0,n//TB,dynamic,0)
    def gather_c(row, size):
        out=[]
        for j in range(jt):
            acc=None
            for o in range(TAPS):
                x=p_ref[o,j,pl.ds(row+PAD+HALF-o,size),:]
                acc=x if acc is None else acc+x
            out.append(acc)
        return out
    def own_c(i,_):
        r0=pl.multiple_of(i*CS,CS)
        out=gather_c(r0+PAD,CS)
        for j in range(jt):
            dc_ref[pl.ds(r0,CS),j*128:(j+1)*128]=out[j]
        return 0
    lax.fori_loop(0,n//CS,own_c,0)
    left=gather_c(0,PAD); right=gather_c(n+PAD,PAD)
    for j in range(jt):
        rim_ref[:,d+j*128:d+(j+1)*128]=jnp.where(side==1,left[j],right[j])
    def gather_h(row, size, j, hx, bounds, sums):
        acc=None; new=[]
        for o in range(TAPS):
            x=masked(dd_ref[j,pl.ds(row+PAD+o-HALF,size),:],bounds,o)
            b=TAPS-1-o
            term=x*taps_ref[b:b+1,j*128:(j+1)*128].astype(f32)
            acc=term if acc is None else acc+term
            new.append(jnp.sum((x*hx).reshape(size//8,8,128),axis=0))
        return acc,[s+t for s,t in zip(sums,new)]
    lhalo=jnp.where(side==1,halo_ref[half-16:half,:].astype(f32),0.0)[PAD:2*PAD,:]
    rhalo=jnp.where(side==0,halo_ref[0:16,:].astype(f32),0.0)[0:PAD,:]
    for j in range(jd):
        cols=slice(j*128,(j+1)*128)
        sums=[jnp.zeros((8,128),f32) for _ in range(TAPS)]
        la,sums=gather_h(0,PAD,j,lhalo[:,cols],doc_bounds(meta,meta[6]-PAD,(PAD,128)),sums)
        ra,sums=gather_h(n+PAD,PAD,j,rhalo[:,cols],doc_bounds(meta,meta[6]+n,(PAD,128)),sums)
        rim_ref[:,cols]=jnp.where(side==1,la,ra)
        def own_h(i,sums):
            r0=pl.multiple_of(i*CS,CS)
            acc,sums=gather_h(r0+PAD,CS,j,hid_ref[pl.ds(r0,CS),cols].astype(f32),doc_bounds(meta,meta[6]+r0,(CS,128)),sums)
            dh_ref[pl.ds(r0,CS),cols]=acc
            return sums
        sums=lax.fori_loop(0,n//CS,own_h,sums)
        for o in range(TAPS):
            b=TAPS-1-o
            gtap_ref[b*8:(b+1)*8,cols]=sums[o]
    for b in range(d//attn):
        gp_ref[b]=dot_tn(depth_ref[:,b*attn:(b+1)*attn],dck_ref[...]).astype(gp_ref.dtype)
    gp_ref[d//attn]=dot_tn(mk_ref[...],dlc_ref[...]).astype(gp_ref.dtype)

def conv_back(meta,hid,halo,dconv,cm,kern,cx,q,ck,depth,taps,wp,wck):
    n,d=hid.shape; a=q.shape[1]; sd=jax.ShapeDtypeStruct
    return pl.pallas_call(conv_back_kernel,in_specs=[SM]+[VM]*12,out_specs=[VM]*6,
        out_shape=[sd((n,a),f32),sd((n,a),f32),sd((n,d),f32),sd((PAD,d+a),f32),sd((d//a+1,a,a),bf16),sd((TAPS*8,d),f32)],
        scratch_shapes=[pltpu.VMEM((TAPS,a//128,n+4*PAD,128),f32),pltpu.VMEM((TAPS,TB,a),bf16),pltpu.VMEM((d//128,n+4*PAD,128),f32),
                        pltpu.VMEM((n,a),bf16),pltpu.VMEM((n,a),bf16),pltpu.VMEM((n,a),bf16),pltpu.VMEM((a,a),bf16)],
        cost_estimate=cost(30.0),compiler_params=pltpu.CompilerParams(vmem_limit_bytes=60*2**20),name="conv_back")(meta,hid,halo,dconv,cm,kern,cx,q,ck,depth,taps,wp,wck)

def proj_back_kernel(meta, hid_ref, dqa_ref, dqc_ref, dk_ref, dv_ref, dkv_ref, dc_ref, rim_ref, gp_ref, gtap_ref, gln_ref,
                     dp_ref, keep_ref, send_ref):
    n,d=hid_ref.shape; attn=dqa_ref.shape[1]; half=dkv_ref.shape[0]
    side=meta[7]
    shift=(1-side)*half
    def block(i,_):
        r0=pl.multiple_of(i*TB,TB)
        rows=pl.ds(r0,TB)
        inside=(r0>=shift)&(r0<shift+half)
        scale=jnp.where(inside,1.0,0.0)
        hr=pl.multiple_of(jnp.where(inside,r0-shift,0),TB)
        other=dkv_ref[pl.ds(hr,TB),:].astype(f32)*scale
        top=jnp.where((side==1)&(i==0),rim_ref[:,d:],0.0)
        bottom=jnp.where((side==0)&(i==n//TB-1),rim_ref[:,d:],0.0)
        rim=jnp.concatenate([top,jnp.zeros((TB-2*PAD,attn),f32),bottom],axis=0)
        dp_ref[rows,0:attn]=(dqa_ref[rows,:]+dqc_ref[rows,:]).astype(bf16)
        for j in range(attn//128):
            cols=slice(j*128,(j+1)*128)
            dp_ref[rows,attn+j*128:attn+(j+1)*128]=(dk_ref[rows,cols]+other[:,j*256:j*256+128]).astype(bf16)
            dp_ref[rows,2*attn+j*128:2*attn+(j+1)*128]=(dv_ref[rows,cols]+other[:,j*256+128:(j+1)*256]).astype(bf16)
        dp_ref[rows,3*attn:]=(dc_ref[rows,:]+rim).astype(bf16)
        return 0
    lax.fori_loop(0,n//TB,block,0)
    zeros=jnp.zeros((1,d),f32)
    small=[jnp.sum(gtap_ref[o*8:(o+1)*8,:],axis=0,keepdims=True) for o in range(TAPS)]
    small+=[jnp.sum(gln_ref[k*8:(k+1)*8,:],axis=0,keepdims=True) for k in range(4)]
    small=jnp.concatenate(small+[zeros]*(16-len(small)),axis=0)
    for ref,h in ((send_ref,1-side),(keep_ref,side)):
        hc=pl.ds(pl.multiple_of(h*attn,128),attn)
        for k in range(4):
            ref[k*attn:(k+1)*attn,:]=dot_tn(hid_ref[:,hc],dp_ref[:,k*attn:(k+1)*attn]).astype(ref.dtype)
        ref[4*attn:5*attn,:]=gp_ref[h]
        ref[5*attn:6*attn,:]=gp_ref[2]
        @pl.when(h==1)
        def _():
            ref[5*attn:5*attn+16,:]=small[:,:attn].astype(bf16)
            ref[5*attn+16:5*attn+32,:]=small[:,attn:].astype(bf16)

def proj_back(meta,hid,dqa,dqc,dk,dv,dkv,dc,rim,gp,gtap,gln):
    n,d=hid.shape; a=dqa.shape[1]; sd=jax.ShapeDtypeStruct
    return pl.pallas_call(proj_back_kernel,in_specs=[SM]+[VM]*11,out_specs=[VM]*3,
        out_shape=[sd((n,4*a),bf16),sd((6*a,a),bf16),sd((6*a,a),bf16)],cost_estimate=cost(9.0),
        compiler_params=pltpu.CompilerParams(vmem_limit_bytes=48*2**20),name="proj_back")(meta,hid,dqa,dqc,dk,dv,dkv,dc,rim,gp,gtap,gln)

def grad_in_kernel(meta, dp_ref, dres_ref, dh_ref, rim_ref, wq_ref, wk_ref, wv_ref, wc_ref, gi_ref):
    n,d=gi_ref.shape; attn=wq_ref.shape[1]
    side=meta[7]
    def block(i,_):
        r0=pl.multiple_of(i*TB,TB)
        rows=pl.ds(r0,TB)
        acc=dres_ref[rows,:]+dh_ref[rows,:]
        for k,w in enumerate((wq_ref,wk_ref,wv_ref,wc_ref)):
            acc=acc+dot_nt(dp_ref[rows,k*attn:(k+1)*attn],w[...])
        gi_ref[rows,:]=acc
        return 0
    lax.fori_loop(0,n//TB,block,0)
    at=pl.multiple_of((1-side)*(n-PAD),PAD)
    gi_ref[pl.ds(at,PAD),:]+=rim_ref[:,:d]

def grad_input(meta,dp,dres,dh,rim,wq,wk,wv,wc):
    n,d=dres.shape; sd=jax.ShapeDtypeStruct
    return pl.pallas_call(grad_in_kernel,in_specs=[SM]+[VM]*8,out_specs=VM,
        out_shape=sd((n,d),f32),cost_estimate=cost(9.0),
        compiler_params=pltpu.CompilerParams(vmem_limit_bytes=48*2**20),name="grad_input")(meta,dp,dres,dh,rim,wq,wk,wv,wc)

SCATTER=3
AT=16

def swap_pairs():
    return [(0,1),(1,0)]

def stage_bits(size):
    bits=[]
    b=1
    while b<size:
        bits.append(b)
        b*=2
    n=min(SCATTER,len(bits))
    first=bits[:n]
    other=first[-1:]+first[:-1]
    return list(zip(first,other)),bits[n:]

def row_pairs(rows, bits):
    return [(r*2+s,(r^bits[s])*2+s) for r in range(rows) for s in range(2)]

def comm_meta(side, row, rows):
    stages,_=stage_bits(rows)
    own=[jnp.where(side==0,(row//b0)%2,(row//b1)%2) for b0,b1 in stages]
    oth=[jnp.where(side==0,(row//b1)%2,(row//b0)%2) for b0,b1 in stages]
    c=jnp.int32(0); c2=jnp.int32(0)
    for u,v in zip(own,oth):
        c=c*2+u; c2=c2*2+v
    own=own+[jnp.int32(0)]*(3-len(own))
    return jnp.stack(own+[c,c2]).astype(jnp.int32)

def cost(us):
    return pl.CostEstimate(flops=int(us*1.0e9),bytes_accessed=0,transcendentals=0)

def fold_kernel(stage, meta, keep_ref, got_ref, k_ref, s_ref):
    h=k_ref.shape[0]; ch=96
    b=meta[AT+stage]
    def body(i,_):
        r=pl.multiple_of(i*ch,16)
        for ref,at in ((k_ref,b*h),(s_ref,(1-b)*h)):
            src=pl.multiple_of(at+r,16)
            ref[pl.ds(r,ch),:]=(keep_ref[pl.ds(src,ch),:].astype(f32)+got_ref[pl.ds(src,ch),:].astype(f32)).astype(bf16)
        return 0
    lax.fori_loop(0,h//ch,body,0)

def fold(meta, stage, keep, got):
    h=keep.shape[0]//2; sd=jax.ShapeDtypeStruct((h,keep.shape[1]),keep.dtype)
    def kernel(meta_ref, keep_ref, got_ref, k_ref, s_ref):
        fold_kernel(stage, meta_ref, keep_ref, got_ref, k_ref, s_ref)
    return pl.pallas_call(kernel,in_specs=[SM,VM,VM],out_specs=[VM,VM],out_shape=[sd,sd],cost_estimate=cost(1.0),
        compiler_params=pltpu.CompilerParams(vmem_limit_bytes=16*2**20),name="fold")(meta,keep,got)

def add_low(x,y):
    return (x.astype(f32)+y.astype(f32)).astype(bf16)

def place(meta, mine_ref, other_ref, buf_ref, sems, chunks):
    side=meta[7]
    rows=mine_ref.shape[0]//chunks
    copies=[]
    for i in range(chunks):
        for k,ref in enumerate((mine_ref,other_ref)):
            half=side if k==0 else 1-side
            at=lax.bitwise_xor(meta[AT+3+k],jnp.int32(i))
            copies.append(pltpu.make_async_copy(ref.at[pl.ds(i*rows,rows),:],
                buf_ref.at[half,pl.ds(pl.multiple_of(at*rows,16),rows),:],sems.at[i,k]))
    for c in copies:
        c.start()
    for c in copies:
        c.wait()

def unpack_a_kernel(chunks, meta, mine_ref, other_ref, gout_ref, gin_ref, gwo_ref, buf_ref, sems):
    place(meta,mine_ref,other_ref,buf_ref,sems,chunks)
    a=buf_ref.shape[2]; g,go,_=gout_ref.shape; ch=128
    per=go//a
    def body(i,_):
        r=pl.multiple_of(i*ch,ch)
        for h in range(g):
            for c in range(per):
                gout_ref[h,pl.ds(pl.multiple_of(c*a+r,ch),ch),:]=buf_ref[h,pl.ds(pl.multiple_of(c*a+r,ch),ch),:].astype(f32)
                gin_ref[h,pl.ds(r,ch),c*a:(c+1)*a]=buf_ref[h,pl.ds(pl.multiple_of((per+c)*a+r,ch),ch),:].astype(f32)
            for c in range(gwo_ref.shape[1]//a):
                gwo_ref[pl.ds(pl.multiple_of(h*a+r,ch),ch),c*a:(c+1)*a]=buf_ref[h,pl.ds(pl.multiple_of((2*per+c)*a+r,ch),ch),:].astype(f32)
        return 0
    lax.fori_loop(0,a//ch,body,0)

ANYS=pl.BlockSpec(memory_space=pl.ANY)
def unpack_a(meta, mine, other, g, gi, go, d, chunks):
    sd=jax.ShapeDtypeStruct
    def kernel(*refs):
        unpack_a_kernel(chunks,*refs)
    return pl.pallas_call(kernel,in_specs=[SM,ANYS,ANYS],out_specs=[VM]*3,
        out_shape=[sd((g,go,gi),f32),sd((g,gi,go),f32),sd((d,d),f32)],cost_estimate=cost(7.0),
        scratch_shapes=[pltpu.VMEM((2,)+mine.shape,bf16),pltpu.SemaphoreType.DMA((chunks,2))],
        compiler_params=pltpu.CompilerParams(vmem_limit_bytes=40*2**20),name="unpack_a")(meta,mine,other)

def unpack_b_kernel(chunks, meta, mine_ref, other_ref, q_ref, k_ref, v_ref, c_ref, p_ref, ck_ref, small_ref, buf_ref, sems):
    place(meta,mine_ref,other_ref,buf_ref,sems,chunks)
    a=buf_ref.shape[2]
    for h in range(2):
        for i,ref in enumerate((q_ref,k_ref,v_ref,c_ref,p_ref)):
            ref[h*a:(h+1)*a,:]=buf_ref[h,i*a:(i+1)*a,:].astype(f32)
    r=lax.broadcasted_iota(jnp.int32,(HEADS*TAPS,a),0)
    c=lax.broadcasted_iota(jnp.int32,(HEADS*TAPS,a),1)
    spread=jnp.where((c%64<TAPS)&(r==(c//64)*TAPS+c%64),1.0,0.0).astype(bf16)
    ck_ref[...]=dot_nt(buf_ref[0,5*a:6*a,:],spread)
    small_ref[:,:a]=buf_ref[1,5*a:5*a+16,:].astype(f32)
    small_ref[:,a:]=buf_ref[1,5*a+16:5*a+32,:].astype(f32)

def unpack_b(meta, mine, other, d, a, chunks):
    sd=jax.ShapeDtypeStruct
    def kernel(*refs):
        unpack_b_kernel(chunks,*refs)
    return pl.pallas_call(kernel,in_specs=[SM,ANYS,ANYS],out_specs=[VM]*7,
        out_shape=[sd((d,a),f32)]*5+[sd((a,HEADS*TAPS),f32),sd((16,d),f32)],cost_estimate=cost(4.0),
        scratch_shapes=[pltpu.VMEM((2,)+mine.shape,bf16),pltpu.SemaphoreType.DMA((chunks,2))],
        compiler_params=pltpu.CompilerParams(vmem_limit_bytes=40*2**20),name="unpack_b")(meta,mine,other)

class Reduce:
    def __init__(self, meta, keep, send, rows):
        self.meta=meta; self.rows=rows
        self.stages,self.whole=stage_bits(rows)
        self.keep=keep
        self.got=lax.ppermute(send,"seq",swap_pairs())
        self.step=0
        self.axes=("rows","seq")
    def advance(self):
        n=len(self.stages); w=len(self.whole); k=self.step; self.step+=1
        if k<n:
            self.keep,send=fold(self.meta,k,self.keep,self.got)
            self.got=lax.ppermute(send,self.axes,row_pairs(self.rows,self.stages[k]))
        elif k<n+w:
            self.keep=add_low(self.keep,self.got)
            b=self.whole[k-n]
            self.got=lax.ppermute(self.keep,self.axes,row_pairs(self.rows,(b,b)))
        elif k<2*n+w:
            self.keep=add_low(self.keep,self.got) if k==n+w else jnp.concatenate([self.keep,self.got],axis=0)
            self.got=lax.ppermute(self.keep,self.axes,row_pairs(self.rows,self.stages[2*n+w-1-k]))
        elif k==2*n+w:
            self.keep=jnp.concatenate([self.keep,self.got],axis=0)
            self.got=lax.ppermute(self.keep,"seq",swap_pairs())
        else:
            return False
        return True
    def finish(self):
        while self.advance():
            pass
        return self.keep,self.got,2**len(self.stages)

def per_device(hidden_in,doc_lengths,out_grad,w_query,w_key,w_value,w_conv_out,depth_kernel,w_point,w_conv_kernel,
               w_output,ln1_gain,ln1_bias,w_ffn_in,w_ffn_out,ln2_gain,ln2_bias):
    row_count,local,d=hidden_in.shape
    a=w_query.shape[1]
    half=local//2
    rows=lax.axis_size("rows")
    side=lax.axis_index("seq")
    row=lax.axis_index("rows")
    hid=hidden_in[0]
    meta=jnp.concatenate([make_meta(doc_lengths[0],side,local,local*2),comm_meta(side,row,rows)])
    halo=lax.ppermute(lax.dynamic_slice_in_dim(hid,(1-side)*half,half,0),"seq",swap_pairs())
    q,kw,vw,cx,depth,ck,kern,cm=pre(meta,hid,halo,w_query,w_key,w_value,w_conv_out,depth_kernel,w_point,w_conv_kernel)
    ctx,lse=attn_fwd(meta,q,kw,vw)
    ln=jnp.stack([ln1_gain,ln1_bias,ln2_gain,ln2_bias]).astype(f32)
    ho,dres,dctx,dconv,keep,send,gln=ffn(meta,hid,ctx,cm,out_grad[0],w_output,w_ffn_in,w_ffn_out,ln)
    g,gi,go=w_ffn_in.shape
    ra=Reduce(meta,keep,send,rows)
    carry=None
    for pair in range(HEADS//2):
        carry=attn_bwd(meta,pair,q,kw,vw,ctx,dctx,lse,carry)
    dqa,dk,dv,dkv=carry
    dkv=lax.ppermute(dkv,"seq",swap_pairs())
    dqc,dc,dh,rim,gp,gtap=conv_back(meta,hid,halo,dconv,cm,kern,cx,q,ck,depth,depth_kernel,w_point,w_conv_kernel)
    rim=lax.ppermute(rim,"seq",swap_pairs())
    dp,keep,send=proj_back(meta,hid,dqa,dqc,dk,dv,dkv,dc,rim,gp,gtap,gln)
    rb=Reduce(meta,keep,send,rows)
    grad_in=grad_input(meta,dp,dres,dh,rim,w_query,w_key,w_value,w_conv_out)
    mine,other,chunks=ra.finish()
    ffn_out_grad,ffn_in_grad,output_grad=unpack_a(meta,mine,other,g,gi,go,d,chunks)
    mine,other,chunks=rb.finish()
    q_grad,k_grad,v_grad,c_grad,point_grad,ck_grad,small=unpack_b(meta,mine,other,d,a,chunks)
    lng=small[KSIZE:KSIZE+4]
    return (ho[None],grad_in[None],q_grad,k_grad,v_grad,c_grad,small[:KSIZE],point_grad,ck_grad,output_grad,
            lng[0],lng[1],ffn_in_grad,ffn_out_grad,lng[2],lng[3])


def solution(mesh):
    placed=(P("rows","seq",None),P("rows",None),P("rows","seq",None))+(P(),)*14
    return jax.shard_map(per_device,mesh=mesh,in_specs=placed,
        out_specs=(P("rows","seq",None),P("rows","seq",None))+(P(),)*14,check_vma=False)
```

```python
import jax
import jax.numpy as jnp
from jax import lax
from jax.experimental import pallas as pl
from jax.experimental.pallas import tpu as pltpu
from jax.sharding import PartitionSpec as P

KSIZE = 9

HEADS=6
BLK=256
NEG=-1e30
f32=jnp.float32; bf16=jnp.bfloat16

def dot_nt(a,b):
    return lax.dot_general(a,b,(((1,),(1,)),((),())),preferred_element_type=f32)
def dot_nn(a,b):
    return lax.dot_general(a,b,(((1,),(0,)),((),())),preferred_element_type=f32)
def dot_tn(a,b):
    return lax.dot_general(a,b,(((0,),(0,)),((),())),preferred_element_type=f32)

def segs(meta, first, shape):
    pos=first+lax.broadcasted_iota(jnp.int32,shape,0)
    seg=jnp.zeros(shape,jnp.int32)
    for d in range(5):
        seg=seg+jnp.where(pos>=meta[d],1,0)
    return seg

def key_ext(meta, first, n):
    lane=lax.broadcasted_iota(jnp.int32,(n,128),1)
    seg=segs(meta,first,(n,128))
    diff=(lane>=24)&(lane<30)&(lane-24!=seg)
    return jnp.where(lane<24,-1.0,jnp.where(diff,NEG,0.0)).astype(bf16)

def fwd_kernel(meta, q_ref, k_ref, v_ref, ctx_ref, lse_ref, kx_ref, s_ref, m_ref, acc_ref):
    nkb=k_ref.shape[0]//BLK; nqb=q_ref.shape[0]//BLK; npair=HEADS//2
    for b in range(nkb):
        kx_ref[b*BLK:(b+1)*BLK,:]=key_ext(meta,meta[5]+b*BLK,BLK)
    lane=lax.broadcasted_iota(jnp.int32,(BLK,128),1)
    ones_lane=jnp.where(lane==0,1.0,0.0).astype(bf16)
    for qb in range(nqb):
        qrows=slice(qb*BLK,(qb+1)*BLK)
        seg=segs(meta,meta[6]+qb*BLK,(BLK,128))
        qext=jnp.where(lane-24==seg,1.0,0.0).astype(bf16)
        lo=meta[8+2*qb]; hi=meta[9+2*qb]
        m_ref[...]=jnp.full(m_ref.shape,NEG,f32)
        acc_ref[...]=jnp.zeros(acc_ref.shape,f32)
        def phase1(kb,_):
            r0=pl.multiple_of(kb*BLK,BLK)
            kext=kx_ref[pl.ds(r0,BLK),:]
            for j in range(npair):
                kk=jnp.concatenate([k_ref[pl.ds(r0,BLK),j*128:(j+1)*128],kext],axis=1)
                qp=q_ref[qrows,j*128:(j+1)*128]*jnp.asarray(0.125,bf16)
                for hh in range(2):
                    h=2*j+hh
                    qm=jnp.where((lane<64) if hh==0 else (lane>=64),qp,jnp.zeros_like(qp))
                    s=dot_nt(jnp.concatenate([qm,qext],axis=1),kk)
                    s_ref[h,:,pl.ds(r0,BLK)]=s
                    m_ref[h]=jnp.maximum(m_ref[h],jnp.maximum(s[:,:128],s[:,128:]))
            return 0
        lax.fori_loop(lo,hi,phase1,0)
        for h in range(HEADS):
            m_ref[h]=jnp.broadcast_to(jnp.max(m_ref[h],axis=1,keepdims=True),(BLK,128))
        def phase2(kb,_):
            r0=pl.multiple_of(kb*BLK,BLK)
            for j in range(npair):
                vv=jnp.concatenate([v_ref[pl.ds(r0,BLK),j*128:(j+1)*128],ones_lane],axis=1)
                for hh in range(2):
                    h=2*j+hh
                    mm=m_ref[h]
                    p=jnp.exp(s_ref[h,:,pl.ds(r0,BLK)]-jnp.concatenate([mm,mm],axis=1)).astype(bf16)
                    acc_ref[h]=acc_ref[h]+dot_nn(p,vv)
            return 0
        lax.fori_loop(lo,hi,phase2,0)
        lse_all=jnp.zeros((BLK,128),f32)
        for j in range(npair):
            parts=[]
            for hh in range(2):
                h=2*j+hh
                l=jnp.broadcast_to(acc_ref[h][:,128:129],(BLK,128))
                parts.append(acc_ref[h][:,:128]/l)
                lse=m_ref[h]+jnp.log(l)
                sel=(lane==h)|(lane==h+8)|(lane==h+16)
                lse_all=jnp.where(sel,lse,lse_all)
            ctx_ref[qrows,j*128:(j+1)*128]=jnp.where(lane<64,parts[0],parts[1]).astype(ctx_ref.dtype)
        lse_ref[qrows,:]=lse_all

def bwd_kernel(meta, q_ref, k_ref, v_ref, ctx_ref, dctx_ref, lse_ref, dq_ref, dko_ref, dvo_ref, dkv_ref, kx_ref, dk_ref, dv_ref):
    nkb=k_ref.shape[0]//BLK; nqb=q_ref.shape[0]//BLK; npair=HEADS//2
    width=q_ref.shape[1]
    for b in range(nkb):
        kx_ref[b*BLK:(b+1)*BLK,:]=key_ext(meta,meta[5]+b*BLK,BLK)
    dk_ref[...]=jnp.zeros(dk_ref.shape,f32)
    dv_ref[...]=jnp.zeros(dv_ref.shape,f32)
    dq_ref[...]=jnp.zeros(dq_ref.shape,f32)
    lane=lax.broadcasted_iota(jnp.int32,(BLK,128),1)
    vext=jnp.where(lane<16,-1.0,0.0).astype(bf16)
    r=lax.broadcasted_iota(jnp.int32,(width,128),0)//64
    cl=lax.broadcasted_iota(jnp.int32,(width,128),1)
    heads_of=jnp.where((cl<16)&(cl%8==r),1.0,0.0).astype(bf16)
    low=lane<64
    for qb in range(nqb):
        qrows=slice(qb*BLK,(qb+1)*BLK)
        seg=segs(meta,meta[6]+qb*BLK,(BLK,128))
        onehot=lane-24==seg
        lse=lse_ref[qrows,:]
        hi_=lse.astype(bf16).astype(f32)
        r1=lse-hi_
        mid=r1.astype(bf16).astype(f32)
        lo_=r1-mid
        split=jnp.where(lane<8,hi_,jnp.where(lane<16,mid,lo_))
        prod=ctx_ref[qrows,:].astype(f32)*dctx_ref[qrows,:].astype(f32)
        ph=prod.astype(bf16)
        plo=(prod-ph.astype(f32)).astype(bf16)
        dd=dot_nn(ph,heads_of)+dot_nn(plo,heads_of)
        dh=dd.astype(bf16).astype(f32)
        dsplit=jnp.where(lane<8,dh,dd-dh)
        qx=[];dcx=[];qms=[];dcs=[]
        for h in range(HEADS):
            j=h//2
            side=low if h%2==0 else ~low
            qp=q_ref[qrows,j*128:(j+1)*128]*jnp.asarray(0.125,bf16)
            qm=jnp.where(side,qp,jnp.zeros_like(qp))
            sel=(lane==h)|(lane==h+8)|(lane==h+16)
            qe=jnp.where(sel,split,jnp.where(onehot,1.0,0.0)).astype(bf16)
            qx.append(jnp.concatenate([qm,qe],axis=1))
            dp=dctx_ref[qrows,j*128:(j+1)*128]
            dm=jnp.where(side,dp,jnp.zeros_like(dp))
            de=jnp.where((lane==h)|(lane==h+8),dsplit,0.0).astype(bf16)
            dcx.append(jnp.concatenate([dm,de],axis=1))
            qms.append(qm);dcs.append(dm)
        lo=meta[8+2*qb]; hi=meta[9+2*qb]
        def body(kb,_):
            r0=pl.multiple_of(kb*BLK,BLK)
            kext=kx_ref[pl.ds(r0,BLK),:]
            for j in range(npair):
                cols=slice(j*128,(j+1)*128)
                kp=k_ref[pl.ds(r0,BLK),cols]
                kk=jnp.concatenate([kp,kext],axis=1)
                vv=jnp.concatenate([v_ref[pl.ds(r0,BLK),cols],vext],axis=1)
                pts=[];dss=[];ks=[]
                for hh in range(2):
                    h=2*j+hh
                    pt=jnp.exp(dot_nt(kk,qx[h]))
                    dpt=dot_nt(vv,dcx[h])
                    pts.append(pt.astype(bf16))
                    dss.append((pt*dpt).astype(bf16))
                    ks.append(jnp.where(low if hh==0 else ~low,kp,jnp.zeros_like(kp)))
                dv_ref[pl.ds(r0,BLK),cols]+=dot_nn(jnp.concatenate(pts,axis=1),jnp.concatenate(dcs[2*j:2*j+2],axis=0))
                dk_ref[pl.ds(r0,BLK),cols]+=dot_nn(jnp.concatenate(dss,axis=1),jnp.concatenate(qms[2*j:2*j+2],axis=0))
                dq_ref[qrows,cols]+=dot_tn(jnp.concatenate(dss,axis=0),jnp.concatenate(ks,axis=0))
            return 0
        lax.fori_loop(lo,hi,body,0)
        dq_ref[qrows,:]=dq_ref[qrows,:]*0.125
    n=q_ref.shape[0]; half=dkv_ref.shape[0]
    own_off=meta[7]*half; halo_off=(1-meta[7])*n
    for b in range(n//BLK):
        src=pl.multiple_of(own_off+b*BLK,BLK)
        dko_ref[b*BLK:(b+1)*BLK,:]=dk_ref[pl.ds(src,BLK),:]
        dvo_ref[b*BLK:(b+1)*BLK,:]=dv_ref[pl.ds(src,BLK),:]
    for b in range(half//BLK):
        src=pl.multiple_of(halo_off+b*BLK,BLK)
        for j in range(npair):
            dkv_ref[b*BLK:(b+1)*BLK,j*256:j*256+128]=dk_ref[pl.ds(src,BLK),j*128:(j+1)*128].astype(bf16)
            dkv_ref[b*BLK:(b+1)*BLK,j*256+128:(j+1)*256]=dv_ref[pl.ds(src,BLK),j*128:(j+1)*128].astype(bf16)

VM=pl.BlockSpec(memory_space=pltpu.VMEM)
SM=pl.BlockSpec(memory_space=pltpu.SMEM)
def attn_fwd(meta,q,k,v):
    t,w=q.shape
    return pl.pallas_call(fwd_kernel,in_specs=[SM,VM,VM,VM],out_specs=[VM,VM],
        out_shape=[jax.ShapeDtypeStruct((t,w),bf16),jax.ShapeDtypeStruct((t,128),f32)],
        scratch_shapes=[pltpu.VMEM((k.shape[0],128),bf16),pltpu.VMEM((HEADS,BLK,k.shape[0]),f32),
            pltpu.VMEM((HEADS,BLK,128),f32),pltpu.VMEM((HEADS,BLK,256),f32)],
        compiler_params=pltpu.CompilerParams(vmem_limit_bytes=30*2**20),cost_estimate=cost(15.0),name="attn_fwd")(meta,q,k,v)
def attn_bwd(meta,q,k,v,ctx,dctx,lse):
    t,w=q.shape; kn=k.shape[0]
    sd=jax.ShapeDtypeStruct
    return pl.pallas_call(bwd_kernel,in_specs=[SM]+[VM]*6,out_specs=[VM]*4,
        out_shape=[sd((t,w),f32)]*3+[sd((kn-t,2*w),bf16)],
        scratch_shapes=[pltpu.VMEM((kn,128),bf16),pltpu.VMEM((kn,w),f32),pltpu.VMEM((kn,w),f32)],cost_estimate=cost(26.0),
        compiler_params=pltpu.CompilerParams(vmem_limit_bytes=24*2**20),name="attn_bwd")(meta,q,k,v,ctx,dctx,lse)

def make_meta(lengths, side, local, full):
    ends=jnp.cumsum(lengths)
    starts=ends-lengths
    win=side*(local//2); own=side*local
    nqb=local//BLK
    b0=own+jnp.arange(nqb)*BLK
    b1=b0+BLK-1
    bounds_lo=jnp.concatenate([jnp.zeros((1,),jnp.int32),ends])
    bounds_hi=jnp.concatenate([ends,jnp.full((1,),full,jnp.int32)])
    seg0=jnp.sum((b0[:,None]>=ends[None]).astype(jnp.int32),1)
    seg1=jnp.sum((b1[:,None]>=ends[None]).astype(jnp.int32),1)
    first=jnp.sum(jnp.where(jnp.arange(6)[None]==seg0[:,None],bounds_lo[None],0),1)
    last=jnp.sum(jnp.where(jnp.arange(6)[None]==seg1[:,None],bounds_hi[None],0),1)
    lo=jnp.maximum(first-win,0)//BLK
    hi=jnp.minimum((last-win+BLK-1)//BLK,(local+local//2)//BLK)
    return jnp.concatenate([ends,win[None],own[None],side[None],jnp.stack([lo,hi],1).reshape(-1)]).astype(jnp.int32)

TB=256

def gelu_parts(z):
    a=jnp.abs(z)
    t=1.0/(1.0+a*(0.3275911*0.7071067811865476))
    e=jnp.exp(-0.5*z*z)
    poly=t*(0.127414796+t*(-0.142248368+t*(0.7107068705+t*(-0.7265760135+t*0.5307027145))))
    ht=poly*e
    phi=jnp.where(z>=0.0,1.0-ht,ht)
    return z*phi, phi+z*(e*0.3989422804014327)

def rows8(x):
    return jnp.sum(x.reshape(x.shape[0]//8,8,x.shape[1]),axis=0)

def norm_parts(z):
    mu=jnp.mean(z,axis=-1,keepdims=True)
    c=z-mu
    var=jnp.mean(c*c,axis=-1,keepdims=True)
    rstd=lax.rsqrt(var+1e-6)
    return c*rstd, rstd

def norm_back(d, gain, xhat, rstd):
    dx=d*gain
    a=jnp.mean(dx,axis=-1,keepdims=True)
    b=jnp.mean(dx*xhat,axis=-1,keepdims=True)
    return rstd*(dx-a-xhat*b)

def ffn_kernel(meta, hid_ref, ctx_ref, cm_ref, og_ref, wo_ref, win_ref, wout_ref, ln_ref,
               ho_ref, dres_ref, dctx_ref, dconv_ref, keep_ref, send_ref, gln_ref,
               act_ref, dff_ref, x1_ref, dfo_ref, datt_ref, mix_ref):
    n=hid_ref.shape[0]; d=hid_ref.shape[1]; groups=win_ref.shape[0]; gi=d//groups; go=win_ref.shape[2]
    attn=dctx_ref.shape[1]
    tile=512
    gln_ref[...]=jnp.zeros(gln_ref.shape,f32)
    def block(i,_):
        r0=pl.multiple_of(i*TB,TB)
        rows=pl.ds(r0,TB)
        g1=ln_ref[0:1,:];b1=ln_ref[1:2,:];g2=ln_ref[2:3,:];b2=ln_ref[3:4,:]
        att=dot_nn(jnp.concatenate([ctx_ref[rows,:],cm_ref[rows,:]],axis=1),wo_ref[...])
        xhat1,rstd1=norm_parts(hid_ref[rows,:].astype(f32)+att)
        first=xhat1*g1+b1
        x1=first.astype(bf16)
        for g in range(groups):
            x1_ref[g,rows,:]=x1[:,g*gi:(g+1)*gi]
        mix_ref[0,rows,:]=ctx_ref[rows,:]
        mix_ref[1,rows,:]=cm_ref[rows,:]
        outs=[]
        for g in range(groups):
            acc=None
            for c in range(go//tile):
                cols=slice(c*tile,(c+1)*tile)
                gc=slice(g*go+c*tile,g*go+(c+1)*tile)
                z=dot_nn(x1[:,g*gi:(g+1)*gi],win_ref[g,:,cols])
                a,gp=gelu_parts(z)
                ab=a.astype(bf16)
                act_ref[g,rows,cols]=ab
                dff_ref[g,rows,cols]=gp.astype(bf16)
                o=dot_nn(ab,wout_ref[g,cols,:])
                acc=o if acc is None else acc+o
            outs.append(acc)
        xhat2,rstd2=norm_parts(first+jnp.concatenate(outs,axis=1))
        pos=meta[6]+r0+lax.broadcasted_iota(jnp.int32,(TB,d),0)
        valid=pos<meta[4]
        ho_ref[rows,:]=jnp.where(valid,xhat2*g2+b2,0.0).astype(bf16)
        gn=jnp.where(valid,og_ref[rows,:].astype(f32),0.0)
        gln_ref[16:24,:]+=rows8(gn*xhat2)
        gln_ref[24:32,:]+=rows8(gn)
        dres2=norm_back(gn,g2,xhat2,rstd2)
        dfo=dres2.astype(bf16)
        for g in range(groups):
            dfo_ref[g,rows,:]=dfo[:,g*gi:(g+1)*gi]
        backs=[]
        for g in range(groups):
            acc=None
            for c in range(go//tile):
                cols=slice(c*tile,(c+1)*tile)
                gc=slice(g*go+c*tile,g*go+(c+1)*tile)
                da=dot_nt(dfo[:,g*gi:(g+1)*gi],wout_ref[g,cols,:])
                dh=(da*dff_ref[g,rows,cols].astype(f32)).astype(bf16)
                dff_ref[g,rows,cols]=dh
                o=dot_nt(dh,win_ref[g,:,cols])
                acc=o if acc is None else acc+o
            backs.append(acc)
        dfirst=dres2+jnp.concatenate(backs,axis=1)
        gln_ref[0:8,:]+=rows8(dfirst*xhat1)
        gln_ref[8:16,:]+=rows8(dfirst)
        dres1=norm_back(dfirst,g1,xhat1,rstd1)
        dres_ref[rows,:]=dres1
        datt=dres1.astype(bf16)
        datt_ref[rows,:]=datt
        dm=dot_nt(datt,wo_ref[...])
        dctx_ref[rows,:]=dm[:,:attn].astype(bf16)
        dconv_ref[rows,:]=dm[:,attn:]
        return 0
    lax.fori_loop(0,n//TB,block,0)
    side=meta[7]
    for ref,g in ((send_ref,1-side),(keep_ref,side)):
        at=0
        for c in range(go//gi):
            ref[at*gi:(at+1)*gi,:]=dot_tn(act_ref[g,:,c*gi:(c+1)*gi],dfo_ref[g]).astype(ref.dtype)
            at+=1
        for c in range(go//gi):
            ref[at*gi:(at+1)*gi,:]=dot_tn(x1_ref[g],dff_ref[g,:,c*gi:(c+1)*gi]).astype(ref.dtype)
            at+=1
        for c in range(d//attn):
            ref[at*gi:(at+1)*gi,:]=dot_tn(mix_ref[g],datt_ref[:,c*attn:(c+1)*attn]).astype(ref.dtype)
            at+=1

def ffn(meta,hid,ctx,cm,og,wo,win,wout,ln):
    n,d=hid.shape; g,gi,go=win.shape; attn=ctx.shape[1]
    sd=jax.ShapeDtypeStruct
    return pl.pallas_call(ffn_kernel,in_specs=[SM]+[VM]*8,out_specs=[VM]*7,
        out_shape=[sd((n,d),bf16),sd((n,d),f32),sd((n,attn),bf16),sd((n,attn),f32),
                   sd((2*go+d,attn),bf16),sd((2*go+d,attn),bf16),sd((32,d),f32)],
        scratch_shapes=[pltpu.VMEM((g,n,go),bf16),pltpu.VMEM((g,n,go),bf16),pltpu.VMEM((g,n,gi),bf16),
                        pltpu.VMEM((g,n,gi),bf16),pltpu.VMEM((n,d),bf16),pltpu.VMEM((2,n,attn),bf16)],
        cost_estimate=cost(40.0),compiler_params=pltpu.CompilerParams(vmem_limit_bytes=40*2**20),name="ffn")(meta,hid,ctx,cm,og,wo,win,wout,ln)

TAPS=9
HALF=4
PAD=8
TB=256
CH=64
CS=32

def doc_bounds(meta, first, shape):
    pos=first+lax.broadcasted_iota(jnp.int32,shape,0)
    nxt=jnp.full(shape,2**30,jnp.int32)
    prv=jnp.full(shape,-2**30,jnp.int32)
    for d in range(5):
        e=meta[d]
        nxt=jnp.minimum(nxt,jnp.where(e>pos,e,2**30))
        prv=jnp.maximum(prv,jnp.where(e<=pos,e,-2**30))
    return nxt-pos, pos-prv

def tap_mask(bounds, o):
    rem,age=bounds
    if o>HALF:
        return rem>(o-HALF)
    return age>=(HALF-o)

def masked(x, bounds, o):
    if o==HALF:
        return x
    return jnp.where(tap_mask(bounds,o),x,0.0)

def tap_onehot(rows, cols, o):
    r=lax.broadcasted_iota(jnp.int32,(rows,cols),0)
    c=lax.broadcasted_iota(jnp.int32,(rows,cols),1)
    return jnp.where(r==(c//64)*TAPS+o,1.0,0.0).astype(bf16)

def pre_kernel(meta, hid_ref, halo_ref, wq_hbm, wk_hbm, wv_hbm, wc_hbm, taps_ref, wp_hbm, wck_ref,
               q_ref, kw_ref, vw_ref, cx_ref, depth_ref, ck_ref, kern_hbm, cm_ref,
               hx_ref, wx_ref, lx_ref, w_ref, kern_ref, sems):
    loads=[pltpu.make_async_copy(w,w_ref.at[k],sems.at[k]) for k,w in enumerate((wc_hbm,wq_hbm,wk_hbm,wv_hbm,wp_hbm))]
    for x in loads:
        x.start()
    wc_ref,wq_ref,wk_ref,wv_ref,wp_ref=(w_ref.at[k] for k in range(5))
    n,d=hid_ref.shape; half=halo_ref.shape[0]; attn=q_ref.shape[1]
    side=meta[7]
    own_off=side*half; halo_off=(1-side)*n
    jt=attn//128; jd=d//128
    for o in range(TAPS):
        wx_ref[:,o*attn:(o+1)*attn]=dot_nn(wck_ref[...],tap_onehot(HEADS*TAPS,attn,o)).astype(bf16)
    left=jnp.where(side==1,halo_ref[half-16:half,:].astype(f32),0.0)
    right=jnp.where(side==0,halo_ref[0:16,:].astype(f32),0.0)
    rims=jnp.concatenate([left,right],axis=0).astype(bf16)
    for x in loads:
        x.wait()
    crim=dot_nn(rims,wc_ref[...]).astype(bf16).astype(f32)
    for j in range(jd):
        hx_ref[j,0:PAD,:]=left[PAD:2*PAD,j*128:(j+1)*128]
        hx_ref[j,n+PAD:n+2*PAD,:]=right[0:PAD,j*128:(j+1)*128]
    for j in range(jt):
        cx_ref[j,0:PAD,:]=crim[PAD:2*PAD,j*128:(j+1)*128]
        cx_ref[j,n+PAD:n+2*PAD,:]=crim[16:16+PAD,j*128:(j+1)*128]
    def project(i,_):
        r0=pl.multiple_of(i*TB,TB)
        x=hid_ref[pl.ds(r0,TB),:]
        q_ref[pl.ds(r0,TB),:]=dot_nn(x,wq_ref[...]).astype(bf16)
        ow=pl.multiple_of(own_off+r0,TB)
        kw_ref[pl.ds(ow,TB),:]=dot_nn(x,wk_ref[...]).astype(bf16)
        vw_ref[pl.ds(ow,TB),:]=dot_nn(x,wv_ref[...]).astype(bf16)
        c=dot_nn(x,wc_ref[...]).astype(bf16).astype(f32)
        rp=pl.multiple_of(r0+PAD,PAD)
        for j in range(jt):
            cx_ref[j,pl.ds(rp,TB),:]=c[:,j*128:(j+1)*128]
        xf=x.astype(f32)
        for j in range(jd):
            hx_ref[j,pl.ds(rp,TB),:]=xf[:,j*128:(j+1)*128]
        return 0
    lax.fori_loop(0,n//TB,project,0)
    def project_halo(i,_):
        r0=pl.multiple_of(i*TB,TB)
        x=halo_ref[pl.ds(r0,TB),:]
        ow=pl.multiple_of(halo_off+r0,TB)
        kw_ref[pl.ds(ow,TB),:]=dot_nn(x,wk_ref[...]).astype(bf16)
        vw_ref[pl.ds(ow,TB),:]=dot_nn(x,wv_ref[...]).astype(bf16)
        return 0
    lax.fori_loop(0,half//TB,project_halo,0)
    def depthwise(i,_):
        r0=pl.multiple_of(i*CH,CH)
        bounds=doc_bounds(meta,meta[6]+r0,(CH,128))
        for j in range(jd):
            acc=None
            for o in range(TAPS):
                x=hx_ref[j,pl.ds(r0+PAD+o-HALF,CH),:]
                term=masked(x*taps_ref[o:o+1,j*128:(j+1)*128].astype(f32),bounds,o)
                acc=term if acc is None else acc+term
            depth_ref[pl.ds(r0,CH),j*128:(j+1)*128]=acc.astype(bf16)
        return 0
    lax.fori_loop(0,n//CH,depthwise,0)
    def dynamic(r0):
        ck=dot_nn(depth_ref[pl.ds(r0,TB),:],wp_ref[...])
        ck_ref[pl.ds(r0,TB),:]=ck
        mk=(ck*q_ref[pl.ds(r0,TB),:].astype(f32)).astype(bf16)
        for o in range(TAPS):
            lx_ref[o]=dot_nn(mk,wx_ref[:,o*attn:(o+1)*attn])
        def soft(s,_):
            s0=pl.multiple_of(s*CS,CS)
            rows=pl.ds(s0,CS)
            t0=pl.multiple_of(r0+s0,CS)
            bounds=doc_bounds(meta,meta[6]+t0,(CS,128))
            for j in range(jt):
                cols=slice(j*128,(j+1)*128)
                ls=[lx_ref[o,rows,cols] for o in range(TAPS)]
                m=ls[0]
                for o in range(1,TAPS):
                    m=jnp.maximum(m,ls[o])
                es=[jnp.exp(l-m) for l in ls]
                tot=es[0]
                for o in range(1,TAPS):
                    tot=tot+es[o]
                inv=1.0/tot
                acc=None
                for o in range(TAPS):
                    k=es[o]*inv
                    kern_ref[o,pl.ds(t0,CS),cols]=k.astype(bf16)
                    term=masked(k*cx_ref[j,pl.ds(t0+PAD+o-HALF,CS),:],bounds,o)
                    acc=term if acc is None else acc+term
                cm_ref[pl.ds(t0,CS),cols]=acc.astype(bf16)
            return 0
        lax.fori_loop(0,TB//CS,soft,0)
    stores=[]
    for b in range(n//TB):
        dynamic(b*TB)
        x=pltpu.make_async_copy(kern_ref.at[:,pl.ds(b*TB,TB),:],kern_hbm.at[:,pl.ds(b*TB,TB),:],sems.at[5+b])
        x.start()
        stores.append(x)
    for x in stores:
        x.wait()

def pre(meta,hid,halo,wq,wk,wv,wc,taps,wp,wck):
    n,d=hid.shape; half=halo.shape[0]; a=wq.shape[1]; sd=jax.ShapeDtypeStruct
    anys=pl.BlockSpec(memory_space=pltpu.HBM)
    return pl.pallas_call(pre_kernel,in_specs=[SM,VM,VM,anys,anys,anys,anys,VM,anys,VM],out_specs=[VM]*6+[anys,VM],
        out_shape=[sd((n,a),bf16),sd((n+half,a),bf16),sd((n+half,a),bf16),sd((a//128,n+2*PAD,128),f32),
                   sd((n,d),bf16),sd((n,a),f32),sd((TAPS,n,a),bf16),sd((n,a),bf16)],
        scratch_shapes=[pltpu.VMEM((d//128,n+2*PAD,128),f32),pltpu.VMEM((a,TAPS*a),bf16),pltpu.VMEM((TAPS,TB,a),f32),
                        pltpu.VMEM((5,d,a),bf16),pltpu.VMEM((TAPS,n,a),bf16),pltpu.SemaphoreType.DMA((5+n//TB,))],
        cost_estimate=cost(30.0),compiler_params=pltpu.CompilerParams(vmem_limit_bytes=40*2**20),name="pre")(meta,hid,halo,wq,wk,wv,wc,taps,wp,wck)

def conv_back_kernel(meta, dconv_ref, cm_ref, kern_ref, cx_ref, q_ref, ck_ref, depth_ref,
                     wp_ref, wck_ref,
                     dqc_ref, dc_ref, dda_ref, ddb_ref, rimc_ref, gp_ref,
                     p_ref, pr_ref, dlc_ref, mk_ref, dck_ref, wcx_ref, dep_ref):
    d=depth_ref.shape[1]; attn,n=q_ref.shape[1],dc_ref.shape[0]
    i=pl.program_id(0)
    side=meta[7]; jt=attn//128; jd=d//128; hd=jd//2
    dds=[(dda_ref,j) if j<hd else (ddb_ref,j-hd) for j in range(jd)]
    @pl.when(i==0)
    def _():
        zero=jnp.zeros((2*PAD,128),f32)
        for j in range(jt):
            for o in range(TAPS):
                p_ref[o,j,0:2*PAD,:]=zero
                p_ref[o,j,n+2*PAD:n+4*PAD,:]=zero
        for ref,j in dds:
            ref[j,0:2*PAD,:]=zero
            ref[j,n+2*PAD:n+4*PAD,:]=zero
        r=lax.broadcasted_iota(jnp.int32,(HEADS*TAPS,attn),0)
        c=lax.broadcasted_iota(jnp.int32,(HEADS*TAPS,attn),1)
        spread=jnp.where((c%64<TAPS)&(r==(c//64)*TAPS+c%64),1.0,0.0).astype(bf16)
        wcx_ref[...]=dot_nn(wck_ref[...],spread).astype(bf16)
    def ones_block(w):
        return jnp.where(lax.broadcasted_iota(jnp.int32,(w,w),0)//64==lax.broadcasted_iota(jnp.int32,(w,w),1)//64,1.0,0.0).astype(bf16)
    ones256=ones_block(256); ones128=ones_block(128)
    lane=lax.broadcasted_iota(jnp.int32,(TB,attn),1)%64
    def dynamic():
        r0=pl.multiple_of(i*TB,TB)
        rows=pl.ds(r0,TB)
        def products(s,_):
            s0=pl.multiple_of(s*CS,CS)
            t0=pl.multiple_of(r0+s0,CS)
            bounds=doc_bounds(meta,meta[6]+t0,(CS,128))
            for j in range(jt):
                cols=slice(j*128,(j+1)*128)
                g=dconv_ref[pl.ds(s0,CS),cols]
                cm=cm_ref[pl.ds(s0,CS),cols].astype(f32)
                for o in range(TAPS):
                    cs=masked(cx_ref[j,pl.ds(t0+PAD+o-HALF,CS),:],bounds,o)
                    pr_ref[o,pl.ds(s0,CS),cols]=(g*(cs-cm)).astype(bf16)
                    p_ref[o,j,pl.ds(t0+2*PAD,CS),:]=masked(kern_ref[o,pl.ds(s0,CS),cols].astype(f32)*g,bounds,o)
            return 0
        lax.fori_loop(0,TB//CS,products,0)
        dl=jnp.zeros((TB,attn),f32)
        for o in range(TAPS):
            pr=pr_ref[o]
            dk=jnp.concatenate([dot_nn(pr[:,:256],ones256),dot_nn(pr[:,256:],ones128)],axis=1)
            dl=jnp.where(lane==o,kern_ref[o].astype(f32)*dk,dl)
        dlb=dl.astype(bf16)
        dlc_ref[rows,:]=dlb
        dmk=dot_nt(dlb,wcx_ref[...])
        dep_ref[rows,:]=depth_ref[...]
        q=q_ref[...].astype(f32)
        ck=ck_ref[...]
        mk_ref[rows,:]=(ck*q).astype(bf16)
        dqc_ref[...]=dmk*ck
        dck=(dmk*q).astype(bf16)
        dck_ref[rows,:]=dck
        dd=dot_nt(dck,wp_ref[...])
        rp=pl.multiple_of(r0+2*PAD,PAD)
        for j in range(jd):
            dds[j][0][dds[j][1],pl.ds(rp,TB),:]=dd[:,j*128:(j+1)*128]
    dynamic()
    @pl.when(i==pl.num_programs(0)-1)
    def _():
        def gather_c(row, size):
            out=[]
            for j in range(jt):
                acc=None
                for o in range(TAPS):
                    x=p_ref[o,j,pl.ds(row+PAD+HALF-o,size),:]
                    acc=x if acc is None else acc+x
                out.append(acc)
            return out
        def own_c(i,_):
            r0=pl.multiple_of(i*CS,CS)
            out=gather_c(r0+PAD,CS)
            for j in range(jt):
                dc_ref[pl.ds(r0,CS),j*128:(j+1)*128]=out[j]
            return 0
        lax.fori_loop(0,n//CS,own_c,0)
        left=gather_c(0,PAD); right=gather_c(n+PAD,PAD)
        for j in range(jt):
            rimc_ref[:,j*128:(j+1)*128]=jnp.where(side==1,left[j],right[j])
        for b in range(d//attn):
            gp_ref[b]=dot_tn(dep_ref[:,b*attn:(b+1)*attn],dck_ref[...]).astype(gp_ref.dtype)
        gp_ref[d//attn]=dot_tn(mk_ref[...],dlc_ref[...]).astype(gp_ref.dtype)

def taps_back_kernel(meta, hid_ref, halo_ref, dd_ref, taps_ref, dh_ref, rim_ref, gtap_ref):
    n,d=hid_ref.shape; half=halo_ref.shape[0]
    side=meta[7]; jd=d//128
    def gather_h(row, size, j, hx, bounds, sums):
        acc=None; new=[]
        for o in range(TAPS):
            x=masked(dd_ref[j,pl.ds(row+PAD+o-HALF,size),:],bounds,o)
            b=TAPS-1-o
            term=x*taps_ref[b:b+1,j*128:(j+1)*128].astype(f32)
            acc=term if acc is None else acc+term
            new.append(jnp.sum((x*hx).reshape(size//8,8,128),axis=0))
        return acc,[s+t for s,t in zip(sums,new)]
    lhalo=jnp.where(side==1,halo_ref[half-16:half,:].astype(f32),0.0)[PAD:2*PAD,:]
    rhalo=jnp.where(side==0,halo_ref[0:16,:].astype(f32),0.0)[0:PAD,:]
    for j in range(jd):
        cols=slice(j*128,(j+1)*128)
        sums=[jnp.zeros((8,128),f32) for _ in range(TAPS)]
        la,sums=gather_h(0,PAD,j,lhalo[:,cols],doc_bounds(meta,meta[6]-PAD,(PAD,128)),sums)
        ra,sums=gather_h(n+PAD,PAD,j,rhalo[:,cols],doc_bounds(meta,meta[6]+n,(PAD,128)),sums)
        rim_ref[:,cols]=jnp.where(side==1,la,ra)
        def own_h(i,sums):
            r0=pl.multiple_of(i*CS,CS)
            acc,sums=gather_h(r0+PAD,CS,j,hid_ref[pl.ds(r0,CS),cols].astype(f32),doc_bounds(meta,meta[6]+r0,(CS,128)),sums)
            dh_ref[pl.ds(r0,CS),cols]=acc
            return sums
        sums=lax.fori_loop(0,n//CS,own_h,sums)
        for o in range(TAPS):
            b=TAPS-1-o
            gtap_ref[b*8:(b+1)*8,cols]=sums[o]

def conv_back(meta,dconv,cm,kern,cx,q,ck,depth,wp,wck):
    n,d=depth.shape; a=q.shape[1]; sd=jax.ShapeDtypeStruct
    def row(w):
        return pl.BlockSpec((TB,w),lambda i:(i,0))
    def whole(*shape):
        return pl.BlockSpec(shape,lambda i:(0,)*len(shape))
    half=(d//256,n+4*PAD,128)
    return pl.pallas_call(conv_back_kernel,grid=(n//TB,),
        in_specs=[SM,row(a),row(a),pl.BlockSpec((TAPS,TB,a),lambda i:(0,i,0)),VM,row(a),row(a),row(d),VM,VM],
        out_specs=[row(a),whole(n,a),whole(*half),whole(*half),whole(PAD,a),whole(d//a+1,a,a)],
        out_shape=[sd((n,a),f32),sd((n,a),f32),sd(half,f32),sd(half,f32),sd((PAD,a),f32),sd((d//a+1,a,a),bf16)],
        scratch_shapes=[pltpu.VMEM((TAPS,a//128,n+4*PAD,128),f32),pltpu.VMEM((TAPS,TB,a),bf16),
                        pltpu.VMEM((n,a),bf16),pltpu.VMEM((n,a),bf16),pltpu.VMEM((n,a),bf16),pltpu.VMEM((a,a),bf16),pltpu.VMEM((n,d),bf16)],
        cost_estimate=cost(20.0),compiler_params=pltpu.CompilerParams(vmem_limit_bytes=48*2**20),name="conv_back")(meta,dconv,cm,kern,cx,q,ck,depth,wp,wck)

def taps_back(meta,part,hid,halo,dd,taps):
    n=hid.shape[0]; d=dd.shape[0]*128; sd=jax.ShapeDtypeStruct
    def col(rows):
        return pl.BlockSpec((rows,d),lambda i:(0,part))
    def whole(*shape):
        return pl.BlockSpec(shape,lambda i:(0,)*len(shape))
    return pl.pallas_call(taps_back_kernel,grid=(1,),in_specs=[SM,col(n),col(halo.shape[0]),whole(*dd.shape),col(TAPS)],
        out_specs=[whole(n,d),whole(PAD,d),whole(TAPS*8,d)],
        out_shape=[sd((n,d),f32),sd((PAD,d),f32),sd((TAPS*8,d),f32)],
        cost_estimate=cost(6.0),compiler_params=pltpu.CompilerParams(vmem_limit_bytes=24*2**20),name="taps_back")(meta,hid,halo,dd,taps)

def proj_back_kernel(meta, hid_ref, dqa_ref, dqc_ref, dk_ref, dv_ref, dkv_ref, dc_ref, rimc_ref, gp_ref, gta_ref, gtb_ref, gln_ref,
                     dp_ref, keep_ref, send_ref):
    n,d=hid_ref.shape; attn=dqa_ref.shape[1]; half=dkv_ref.shape[0]
    side=meta[7]
    shift=(1-side)*half
    def block(i,_):
        r0=pl.multiple_of(i*TB,TB)
        rows=pl.ds(r0,TB)
        inside=(r0>=shift)&(r0<shift+half)
        scale=jnp.where(inside,1.0,0.0)
        hr=pl.multiple_of(jnp.where(inside,r0-shift,0),TB)
        other=dkv_ref[pl.ds(hr,TB),:].astype(f32)*scale
        top=jnp.where((side==1)&(i==0),rimc_ref[...],0.0)
        bottom=jnp.where((side==0)&(i==n//TB-1),rimc_ref[...],0.0)
        rim=jnp.concatenate([top,jnp.zeros((TB-2*PAD,attn),f32),bottom],axis=0)
        dp_ref[rows,0:attn]=(dqa_ref[rows,:]+dqc_ref[rows,:]).astype(bf16)
        for j in range(attn//128):
            cols=slice(j*128,(j+1)*128)
            dp_ref[rows,attn+j*128:attn+(j+1)*128]=(dk_ref[rows,cols]+other[:,j*256:j*256+128]).astype(bf16)
            dp_ref[rows,2*attn+j*128:2*attn+(j+1)*128]=(dv_ref[rows,cols]+other[:,j*256+128:(j+1)*256]).astype(bf16)
        dp_ref[rows,3*attn:]=(dc_ref[rows,:]+rim).astype(bf16)
        return 0
    lax.fori_loop(0,n//TB,block,0)
    zeros=jnp.zeros((1,d),f32)
    small=[jnp.concatenate([jnp.sum(t[o*8:(o+1)*8,:],axis=0,keepdims=True) for t in (gta_ref,gtb_ref)],axis=1) for o in range(TAPS)]
    small+=[jnp.sum(gln_ref[k*8:(k+1)*8,:],axis=0,keepdims=True) for k in range(4)]
    small=jnp.concatenate(small+[zeros]*(16-len(small)),axis=0)
    for ref,h in ((send_ref,1-side),(keep_ref,side)):
        hc=pl.ds(pl.multiple_of(h*attn,128),attn)
        for k in range(4):
            ref[k*attn:(k+1)*attn,:]=dot_tn(hid_ref[:,hc],dp_ref[:,k*attn:(k+1)*attn]).astype(ref.dtype)
        ref[4*attn:5*attn,:]=gp_ref[h]
        ref[5*attn:6*attn,:]=gp_ref[2]
        @pl.when(h==1)
        def _():
            ref[5*attn:5*attn+16,:]=small[:,:attn].astype(bf16)
            ref[5*attn+16:5*attn+32,:]=small[:,attn:].astype(bf16)

def proj_back(meta,hid,dqa,dqc,dk,dv,dkv,dc,rimc,gp,gta,gtb,gln):
    n,d=hid.shape; a=dqa.shape[1]; sd=jax.ShapeDtypeStruct
    return pl.pallas_call(proj_back_kernel,in_specs=[SM]+[VM]*12,out_specs=[VM]*3,
        out_shape=[sd((n,4*a),bf16),sd((6*a,a),bf16),sd((6*a,a),bf16)],cost_estimate=cost(9.0),
        compiler_params=pltpu.CompilerParams(vmem_limit_bytes=16*2**20),name="proj_back")(meta,hid,dqa,dqc,dk,dv,dkv,dc,rimc,gp,gta,gtb,gln)

def grad_in_kernel(meta, dp_ref, dres_ref, dha_ref, dhb_ref, rima_ref, rimb_ref, wq_ref, wk_ref, wv_ref, wc_ref, gi_ref):
    n,d=gi_ref.shape; attn=wq_ref.shape[1]
    side=meta[7]
    def block(i,_):
        r0=pl.multiple_of(i*TB,TB)
        rows=pl.ds(r0,TB)
        acc=dres_ref[rows,:]+jnp.concatenate([dha_ref[rows,:],dhb_ref[rows,:]],axis=1)
        for k,w in enumerate((wq_ref,wk_ref,wv_ref,wc_ref)):
            acc=acc+dot_nt(dp_ref[rows,k*attn:(k+1)*attn],w[...])
        gi_ref[rows,:]=acc
        return 0
    lax.fori_loop(0,n//TB,block,0)
    at=pl.multiple_of((1-side)*(n-PAD),PAD)
    gi_ref[pl.ds(at,PAD),:]+=jnp.concatenate([rima_ref[...],rimb_ref[...]],axis=1)

def grad_input(meta,dp,dres,dha,dhb,rima,rimb,wq,wk,wv,wc):
    n,d=dres.shape; sd=jax.ShapeDtypeStruct
    return pl.pallas_call(grad_in_kernel,in_specs=[SM]+[VM]*10,out_specs=VM,
        out_shape=sd((n,d),f32),cost_estimate=cost(9.0),
        compiler_params=pltpu.CompilerParams(vmem_limit_bytes=16*2**20),name="grad_input")(meta,dp,dres,dha,dhb,rima,rimb,wq,wk,wv,wc)

AT=16

def swap_pairs():
    return [(0,1),(1,0)]

def stage_bits(size, scatter):
    bits=[]
    b=1
    while b<size:
        bits.append(b)
        b*=2
    lead=bits[:3]
    other=lead[-1:]+lead[:-1]+bits[3:]
    n=min(scatter,len(bits))
    return list(zip(bits,other))[:n],bits[n:]

def row_pairs(rows, bits):
    return [(r*2+s,(r^bits[s])*2+s) for r in range(rows) for s in range(2)]

def comm_meta(side, row, rows):
    stages,_=stage_bits(rows,4)
    own=[jnp.where(side==0,(row//b0)%2,(row//b1)%2) for b0,b1 in stages]
    oth=[jnp.where(side==0,(row//b1)%2,(row//b0)%2) for b0,b1 in stages]
    c=jnp.int32(0); c2=jnp.int32(0)
    for u,v in list(zip(own,oth))[:3]:
        c=c*2+u; c2=c2*2+v
    own=own+[jnp.int32(0)]*(4-len(own))
    return jnp.stack(own+[c,c2]).astype(jnp.int32)

def cost(us):
    return pl.CostEstimate(flops=int(us*1.0e9),bytes_accessed=0,transcendentals=0)

def fold_kernel(stage, meta, keep_ref, got_ref, k_ref, s_ref):
    h=k_ref.shape[0]; ch=48
    b=meta[AT+stage]
    def body(i,_):
        r=pl.multiple_of(i*ch,16)
        for ref,at in ((k_ref,b*h),(s_ref,(1-b)*h)):
            src=pl.multiple_of(at+r,16)
            ref[pl.ds(r,ch),:]=(keep_ref[pl.ds(src,ch),:].astype(f32)+got_ref[pl.ds(src,ch),:].astype(f32)).astype(bf16)
        return 0
    lax.fori_loop(0,h//ch,body,0)

def fold(meta, stage, keep, got):
    h=keep.shape[0]//2; sd=jax.ShapeDtypeStruct((h,keep.shape[1]),keep.dtype)
    def kernel(meta_ref, keep_ref, got_ref, k_ref, s_ref):
        fold_kernel(stage, meta_ref, keep_ref, got_ref, k_ref, s_ref)
    return pl.pallas_call(kernel,in_specs=[SM,VM,VM],out_specs=[VM,VM],out_shape=[sd,sd],cost_estimate=cost(1.0),
        compiler_params=pltpu.CompilerParams(vmem_limit_bytes=16*2**20),name="fold")(meta,keep,got)

def add_low(x,y):
    return (x.astype(f32)+y.astype(f32)).astype(bf16)

def place(meta, mine_ref, other_ref, buf_ref, sems, chunks):
    side=meta[7]
    rows=mine_ref.shape[0]//chunks
    copies=[]
    for i in range(chunks):
        for k,ref in enumerate((mine_ref,other_ref)):
            half=side if k==0 else 1-side
            at=lax.bitwise_xor(meta[AT+4+k],jnp.int32(i))
            copies.append(pltpu.make_async_copy(ref.at[pl.ds(i*rows,rows),:],
                buf_ref.at[half,pl.ds(pl.multiple_of(at*rows,16),rows),:],sems.at[i,k]))
    for c in copies:
        c.start()
    for c in copies:
        c.wait()

def unpack_a_kernel(chunks, meta, mine_ref, other_ref, gout_ref, gin_ref, gwo_ref, buf_ref, sems):
    place(meta,mine_ref,other_ref,buf_ref,sems,chunks)
    a=buf_ref.shape[2]; g,go,_=gout_ref.shape; ch=128
    per=go//a
    def body(i,_):
        r=pl.multiple_of(i*ch,ch)
        for h in range(g):
            for c in range(per):
                gout_ref[h,pl.ds(pl.multiple_of(c*a+r,ch),ch),:]=buf_ref[h,pl.ds(pl.multiple_of(c*a+r,ch),ch),:].astype(f32)
                gin_ref[h,pl.ds(r,ch),c*a:(c+1)*a]=buf_ref[h,pl.ds(pl.multiple_of((per+c)*a+r,ch),ch),:].astype(f32)
            for c in range(gwo_ref.shape[1]//a):
                gwo_ref[pl.ds(pl.multiple_of(h*a+r,ch),ch),c*a:(c+1)*a]=buf_ref[h,pl.ds(pl.multiple_of((2*per+c)*a+r,ch),ch),:].astype(f32)
        return 0
    lax.fori_loop(0,a//ch,body,0)

ANYS=pl.BlockSpec(memory_space=pl.ANY)
def unpack_a(meta, mine, other, g, gi, go, d, chunks):
    sd=jax.ShapeDtypeStruct
    def kernel(*refs):
        unpack_a_kernel(chunks,*refs)
    return pl.pallas_call(kernel,in_specs=[SM,ANYS,ANYS],out_specs=[VM]*3,
        out_shape=[sd((g,go,gi),f32),sd((g,gi,go),f32),sd((d,d),f32)],cost_estimate=cost(8.0),
        scratch_shapes=[pltpu.VMEM((2,)+mine.shape,bf16),pltpu.SemaphoreType.DMA((chunks,2))],
        compiler_params=pltpu.CompilerParams(vmem_limit_bytes=20*2**20),name="unpack_a")(meta,mine,other)

def unpack_b_kernel(chunks, which, meta, part_ref, q_ref, k_ref, v_ref, c_ref, p_ref, ck_ref, small_ref, buf_ref, sems, outs):
    a=buf_ref.shape[1]; rows=part_ref.shape[0]//chunks
    h=meta[7] if which==0 else 1-meta[7]
    copies=[]
    for i in range(chunks):
        at=lax.bitwise_xor(meta[AT+4+which],jnp.int32(i))
        copies.append(pltpu.make_async_copy(part_ref.at[pl.ds(i*rows,rows),:],
            buf_ref.at[pl.ds(pl.multiple_of(at*rows,16),rows),:],sems.at[i]))
    for x in copies:
        x.start()
    for x in copies:
        x.wait()
    backs=[]
    for i,ref in enumerate((q_ref,k_ref,v_ref,c_ref,p_ref)):
        outs[i]=buf_ref[i*a:(i+1)*a,:].astype(f32)
        x=pltpu.make_async_copy(outs.at[i],ref.at[pl.ds(pl.multiple_of(h*a,128),a),:],sems.at[chunks+i])
        x.start()
        backs.append(x)
    r=lax.broadcasted_iota(jnp.int32,(HEADS*TAPS,a),0)
    c=lax.broadcasted_iota(jnp.int32,(HEADS*TAPS,a),1)
    spread=jnp.where((c%64<TAPS)&(r==(c//64)*TAPS+c%64),1.0,0.0).astype(bf16)
    ck_ref[...]=dot_nt(buf_ref[5*a:6*a,:],spread)
    small_ref[:,:a]=buf_ref[5*a:5*a+16,:].astype(f32)
    small_ref[:,a:]=buf_ref[5*a+16:5*a+32,:].astype(f32)
    for x in backs:
        x.wait()

def unpack_b(meta, which, part, d, a, chunks, carry):
    sd=jax.ShapeDtypeStruct
    def kernel(meta_ref, part_ref, *refs):
        unpack_b_kernel(chunks,which,meta_ref,part_ref,*refs[-10:])
    carry=() if carry is None else tuple(carry)
    return pl.pallas_call(kernel,in_specs=[SM,ANYS]+[ANYS]*len(carry),out_specs=[ANYS]*5+[VM]*2,
        out_shape=[sd((d,a),f32)]*5+[sd((a,HEADS*TAPS),f32),sd((16,d),f32)],cost_estimate=cost(4.0),
        input_output_aliases={2+i:i for i in range(len(carry))},
        scratch_shapes=[pltpu.VMEM(part.shape,bf16),pltpu.SemaphoreType.DMA((chunks+5,)),pltpu.VMEM((5,a,a),f32)],
        compiler_params=pltpu.CompilerParams(vmem_limit_bytes=12*2**20),name="unpack_b")(meta,part,*carry)

class Reduce:
    def __init__(self, meta, keep, send, rows, scatter):
        self.meta=meta; self.rows=rows
        self.stages,self.whole=stage_bits(rows,scatter)
        self.keep=keep
        self.got=lax.ppermute(send,"seq",swap_pairs())
        self.step=0
        self.axes=("rows","seq")
    def advance(self):
        n=len(self.stages); w=len(self.whole); k=self.step; self.step+=1
        self.last=k==2*n+w
        if k<n:
            self.keep,send=fold(self.meta,k,self.keep,self.got)
            self.got=lax.ppermute(send,self.axes,row_pairs(self.rows,self.stages[k]))
        elif k<n+w:
            self.keep=add_low(self.keep,self.got)
            b=self.whole[k-n]
            self.got=lax.ppermute(self.keep,self.axes,row_pairs(self.rows,(b,b)))
        elif k==n+w+n+1:
            self.other=self.got
            self.got=None
        else:
            self.keep=add_low(self.keep,self.got) if k==n+w else jnp.concatenate([self.keep,self.got],axis=0)
            m=2*n+w-1-k
            if m>=0:
                self.got=lax.ppermute(self.keep,self.axes,row_pairs(self.rows,self.stages[m]))
            else:
                self.got=lax.ppermute(self.keep,"seq",swap_pairs())
    def after(self, arrays):
        self.got,arrays=lax.optimization_barrier((self.got,tuple(arrays)))
        self.advance()
        self.keep,arrays=lax.optimization_barrier((self.keep,arrays))
        return arrays
    def follow(self, other):
        self.got,other.keep=lax.optimization_barrier((self.got,other.keep))
        self.advance()
    def finish(self):
        while self.got is not None:
            self.advance()
        return self.keep,self.other,2**len(self.stages)

def per_device(hidden_in,doc_lengths,out_grad,w_query,w_key,w_value,w_conv_out,depth_kernel,w_point,w_conv_kernel,
               w_output,ln1_gain,ln1_bias,w_ffn_in,w_ffn_out,ln2_gain,ln2_bias):
    row_count,local,d=hidden_in.shape
    a=w_query.shape[1]
    half=local//2
    rows=lax.axis_size("rows")
    side=lax.axis_index("seq")
    row=lax.axis_index("rows")
    hid=hidden_in[0]
    meta=jnp.concatenate([make_meta(doc_lengths[0],side,local,local*2),comm_meta(side,row,rows)])
    halo=lax.ppermute(lax.dynamic_slice_in_dim(hid,(1-side)*half,half,0),"seq",swap_pairs())
    q,kw,vw,cx,depth,ck,kern,cm=pre(meta,hid,halo,w_query,w_key,w_value,w_conv_out,depth_kernel,w_point,w_conv_kernel)
    ctx,lse=attn_fwd(meta,q,kw,vw)
    ln=jnp.stack([ln1_gain,ln1_bias,ln2_gain,ln2_bias]).astype(f32)
    ho,dres,dctx,dconv,keep,send,gln=ffn(meta,hid,ctx,cm,out_grad[0],w_output,w_ffn_in,w_ffn_out,ln)
    g,gi,go=w_ffn_in.shape
    ra=Reduce(meta,keep,send,rows,3)
    dqc,dc,dda,ddb,rimc,gp=conv_back(meta,dconv,cm,kern,cx,q,ck,depth,w_point,w_conv_kernel)
    rimc=lax.ppermute(rimc,"seq",swap_pairs())
    dctx,dqc,dda=ra.after((dctx,dqc,dda))
    dqa,dk,dv,dkv=attn_bwd(meta,q,kw,vw,ctx,dctx,lse)
    dkv=lax.ppermute(dkv,"seq",swap_pairs())
    dda,dqa=ra.after((dda,dqa))
    dha,rima,gta=taps_back(meta,0,hid,halo,dda,depth_kernel)
    ddb,dha=ra.after((ddb,dha))
    dhb,rimb,gtb=taps_back(meta,1,hid,halo,ddb,depth_kernel)
    rima=lax.ppermute(rima,"seq",swap_pairs())
    rimb=lax.ppermute(rimb,"seq",swap_pairs())
    dqc,dhb=ra.after((dqc,dhb))
    dp,keep,send=proj_back(meta,hid,dqa,dqc,dk,dv,dkv,dc,rimc,gp,gta,gtb,gln)
    rb=Reduce(meta,keep,send,rows,3)
    grad_in=grad_input(meta,dp,dres,dha,dhb,rima,rimb,w_query,w_key,w_value,w_conv_out)
    (grad_in,)=rb.after((grad_in,))
    while True:
        ra.follow(rb)
        if ra.got is None:
            break
        rb.follow(ra)
    mine,other,chunks=ra.finish()
    ffn_out_grad,ffn_in_grad,output_grad=unpack_a(meta,mine,other,g,gi,go,d,chunks)
    ffn_in_grad,ffn_out_grad,output_grad=rb.after((ffn_in_grad,ffn_out_grad,output_grad))
    while not rb.last:
        rb.advance()
    first=unpack_b(meta,0,rb.keep,d,a,chunks,None)
    first,got=lax.optimization_barrier((tuple(first),rb.got))
    second=unpack_b(meta,1,got,d,a,chunks,first[:5])
    q_grad,k_grad,v_grad,c_grad,point_grad=second[:5]
    ck_grad=jnp.where(side==0,first[5],second[5])
    small=jnp.where(side==1,first[6],second[6])
    lng=small[KSIZE:KSIZE+4]
    return (ho[None],grad_in[None],q_grad,k_grad,v_grad,c_grad,small[:KSIZE],point_grad,ck_grad,output_grad,
            lng[0],lng[1],ffn_in_grad,ffn_out_grad,lng[2],lng[3])


def solution(mesh):
    placed=(P("rows","seq",None),P("rows",None),P("rows","seq",None))+(P(),)*14
    return jax.shard_map(per_device,mesh=mesh,in_specs=placed,
        out_specs=(P("rows","seq",None),P("rows","seq",None))+(P(),)*14,check_vma=False)
```

```python
import jax
import jax.numpy as jnp
from jax import lax
from jax.experimental import pallas as pl
from jax.experimental.pallas import tpu as pltpu
from jax.sharding import PartitionSpec as P

KSIZE = 9

HEADS=6
BLK=256
NEG=-1e30
f32=jnp.float32; bf16=jnp.bfloat16

def dot_nt(a,b):
    return lax.dot_general(a,b,(((1,),(1,)),((),())),preferred_element_type=f32)
def dot_nn(a,b):
    return lax.dot_general(a,b,(((1,),(0,)),((),())),preferred_element_type=f32)
def dot_tn(a,b):
    return lax.dot_general(a,b,(((0,),(0,)),((),())),preferred_element_type=f32)

def segs(meta, first, shape):
    pos=first+lax.broadcasted_iota(jnp.int32,shape,0)
    seg=jnp.zeros(shape,jnp.int32)
    for d in range(5):
        seg=seg+jnp.where(pos>=meta[d],1,0)
    return seg

def key_ext(meta, first, n):
    lane=lax.broadcasted_iota(jnp.int32,(n,128),1)
    seg=segs(meta,first,(n,128))
    diff=(lane>=24)&(lane<30)&(lane-24!=seg)
    return jnp.where(lane<24,-1.0,jnp.where(diff,NEG,0.0)).astype(bf16)

def fwd_kernel(meta, q_ref, k_ref, v_ref, ctx_ref, lse_ref, kx_ref, s_ref, m_ref, acc_ref):
    nkb=k_ref.shape[0]//BLK; nqb=q_ref.shape[0]//BLK; npair=HEADS//2
    for b in range(nkb):
        kx_ref[b*BLK:(b+1)*BLK,:]=key_ext(meta,meta[5]+b*BLK,BLK)
    lane=lax.broadcasted_iota(jnp.int32,(BLK,128),1)
    ones_lane=jnp.where(lane==0,1.0,0.0).astype(bf16)
    for qb in range(nqb):
        qrows=slice(qb*BLK,(qb+1)*BLK)
        seg=segs(meta,meta[6]+qb*BLK,(BLK,128))
        qext=jnp.where(lane-24==seg,1.0,0.0).astype(bf16)
        lo=meta[8+2*qb]; hi=meta[9+2*qb]
        m_ref[...]=jnp.full(m_ref.shape,NEG,f32)
        acc_ref[...]=jnp.zeros(acc_ref.shape,f32)
        def phase1(kb,_):
            r0=pl.multiple_of(kb*BLK,BLK)
            kext=kx_ref[pl.ds(r0,BLK),:]
            for j in range(npair):
                kk=jnp.concatenate([k_ref[pl.ds(r0,BLK),j*128:(j+1)*128],kext],axis=1)
                qp=q_ref[qrows,j*128:(j+1)*128]*jnp.asarray(0.125,bf16)
                for hh in range(2):
                    h=2*j+hh
                    qm=jnp.where((lane<64) if hh==0 else (lane>=64),qp,jnp.zeros_like(qp))
                    s=dot_nt(jnp.concatenate([qm,qext],axis=1),kk)
                    s_ref[h,:,pl.ds(r0,BLK)]=s
                    m_ref[h]=jnp.maximum(m_ref[h],jnp.maximum(s[:,:128],s[:,128:]))
            return 0
        lax.fori_loop(lo,hi,phase1,0)
        for h in range(HEADS):
            m_ref[h]=jnp.broadcast_to(jnp.max(m_ref[h],axis=1,keepdims=True),(BLK,128))
        def phase2(kb,_):
            r0=pl.multiple_of(kb*BLK,BLK)
            for j in range(npair):
                vv=jnp.concatenate([v_ref[pl.ds(r0,BLK),j*128:(j+1)*128],ones_lane],axis=1)
                for hh in range(2):
                    h=2*j+hh
                    mm=m_ref[h]
                    p=jnp.exp(s_ref[h,:,pl.ds(r0,BLK)]-jnp.concatenate([mm,mm],axis=1)).astype(bf16)
                    acc_ref[h]=acc_ref[h]+dot_nn(p,vv)
            return 0
        lax.fori_loop(lo,hi,phase2,0)
        lse_all=jnp.zeros((BLK,128),f32)
        for j in range(npair):
            parts=[]
            for hh in range(2):
                h=2*j+hh
                l=jnp.broadcast_to(acc_ref[h][:,128:129],(BLK,128))
                parts.append(acc_ref[h][:,:128]/l)
                lse=m_ref[h]+jnp.log(l)
                sel=(lane==h)|(lane==h+8)|(lane==h+16)
                lse_all=jnp.where(sel,lse,lse_all)
            ctx_ref[qrows,j*128:(j+1)*128]=jnp.where(lane<64,parts[0],parts[1]).astype(ctx_ref.dtype)
        lse_ref[qrows,:]=lse_all

def bwd_kernel(head, meta, q_ref, k_ref, v_ref, ctx_ref, dctx_ref, lse_ref, dq_ref, dko_ref, dvo_ref, dkv_ref, kx_ref, dk_ref, dv_ref):
    nkb=k_ref.shape[0]//BLK; nqb=q_ref.shape[0]//BLK; npair=q_ref.shape[1]//128
    width=q_ref.shape[1]
    for b in range(nkb):
        kx_ref[b*BLK:(b+1)*BLK,:]=key_ext(meta,meta[5]+b*BLK,BLK)
    dk_ref[...]=jnp.zeros(dk_ref.shape,f32)
    dv_ref[...]=jnp.zeros(dv_ref.shape,f32)
    dq_ref[...]=jnp.zeros(dq_ref.shape,f32)
    lane=lax.broadcasted_iota(jnp.int32,(BLK,128),1)
    vext=jnp.where(lane<16,-1.0,0.0).astype(bf16)
    r=head+lax.broadcasted_iota(jnp.int32,(width,128),0)//64
    cl=lax.broadcasted_iota(jnp.int32,(width,128),1)
    heads_of=jnp.where((cl<16)&(cl%8==r),1.0,0.0).astype(bf16)
    low=lane<64
    for qb in range(nqb):
        qrows=slice(qb*BLK,(qb+1)*BLK)
        seg=segs(meta,meta[6]+qb*BLK,(BLK,128))
        onehot=lane-24==seg
        lse=lse_ref[qrows,:]
        hi_=lse.astype(bf16).astype(f32)
        r1=lse-hi_
        mid=r1.astype(bf16).astype(f32)
        lo_=r1-mid
        split=jnp.where(lane<8,hi_,jnp.where(lane<16,mid,lo_))
        prod=ctx_ref[qrows,:].astype(f32)*dctx_ref[qrows,:].astype(f32)
        ph=prod.astype(bf16)
        plo=(prod-ph.astype(f32)).astype(bf16)
        dd=dot_nn(ph,heads_of)+dot_nn(plo,heads_of)
        dh=dd.astype(bf16).astype(f32)
        dsplit=jnp.where(lane<8,dh,dd-dh)
        qx=[];dcx=[];qms=[];dcs=[]
        for h in range(head,head+2*npair):
            j=(h-head)//2
            side=low if h%2==0 else ~low
            qp=q_ref[qrows,j*128:(j+1)*128]*jnp.asarray(0.125,bf16)
            qm=jnp.where(side,qp,jnp.zeros_like(qp))
            sel=(lane==h)|(lane==h+8)|(lane==h+16)
            qe=jnp.where(sel,split,jnp.where(onehot,1.0,0.0)).astype(bf16)
            qx.append(jnp.concatenate([qm,qe],axis=1))
            dp=dctx_ref[qrows,j*128:(j+1)*128]
            dm=jnp.where(side,dp,jnp.zeros_like(dp))
            de=jnp.where((lane==h)|(lane==h+8),dsplit,0.0).astype(bf16)
            dcx.append(jnp.concatenate([dm,de],axis=1))
            qms.append(qm);dcs.append(dm)
        lo=meta[8+2*qb]; hi=meta[9+2*qb]
        def body(kb,_):
            r0=pl.multiple_of(kb*BLK,BLK)
            kext=kx_ref[pl.ds(r0,BLK),:]
            for j in range(npair):
                cols=slice(j*128,(j+1)*128)
                kp=k_ref[pl.ds(r0,BLK),cols]
                kk=jnp.concatenate([kp,kext],axis=1)
                vv=jnp.concatenate([v_ref[pl.ds(r0,BLK),cols],vext],axis=1)
                pts=[];dss=[];ks=[]
                for hh in range(2):
                    h=2*j+hh
                    pt=jnp.exp(dot_nt(kk,qx[h]))
                    dpt=dot_nt(vv,dcx[h])
                    pts.append(pt.astype(bf16))
                    dss.append((pt*dpt).astype(bf16))
                    ks.append(jnp.where(low if hh==0 else ~low,kp,jnp.zeros_like(kp)))
                dv_ref[pl.ds(r0,BLK),cols]+=dot_nn(jnp.concatenate(pts,axis=1),jnp.concatenate(dcs[2*j:2*j+2],axis=0))
                dk_ref[pl.ds(r0,BLK),cols]+=dot_nn(jnp.concatenate(dss,axis=1),jnp.concatenate(qms[2*j:2*j+2],axis=0))
                dq_ref[qrows,cols]+=dot_tn(jnp.concatenate(dss,axis=0),jnp.concatenate(ks,axis=0))
            return 0
        lax.fori_loop(lo,hi,body,0)
        dq_ref[qrows,:]=dq_ref[qrows,:]*0.125
    n=q_ref.shape[0]; half=dkv_ref.shape[0]
    own_off=meta[7]*half; halo_off=(1-meta[7])*n
    for b in range(n//BLK):
        src=pl.multiple_of(own_off+b*BLK,BLK)
        dko_ref[b*BLK:(b+1)*BLK,:]=dk_ref[pl.ds(src,BLK),:]
        dvo_ref[b*BLK:(b+1)*BLK,:]=dv_ref[pl.ds(src,BLK),:]
    for b in range(half//BLK):
        src=pl.multiple_of(halo_off+b*BLK,BLK)
        for j in range(npair):
            dkv_ref[b*BLK:(b+1)*BLK,j*256:j*256+128]=dk_ref[pl.ds(src,BLK),j*128:(j+1)*128].astype(bf16)
            dkv_ref[b*BLK:(b+1)*BLK,j*256+128:(j+1)*256]=dv_ref[pl.ds(src,BLK),j*128:(j+1)*128].astype(bf16)

VM=pl.BlockSpec(memory_space=pltpu.VMEM)
SM=pl.BlockSpec(memory_space=pltpu.SMEM)
def attn_fwd(meta,q,k,v):
    t,w=q.shape
    return pl.pallas_call(fwd_kernel,in_specs=[SM,VM,VM,VM],out_specs=[VM,VM],
        out_shape=[jax.ShapeDtypeStruct((t,w),bf16),jax.ShapeDtypeStruct((t,128),f32)],
        scratch_shapes=[pltpu.VMEM((k.shape[0],128),bf16),pltpu.VMEM((HEADS,BLK,k.shape[0]),f32),
            pltpu.VMEM((HEADS,BLK,128),f32),pltpu.VMEM((HEADS,BLK,256),f32)],
        compiler_params=pltpu.CompilerParams(vmem_limit_bytes=30*2**20),cost_estimate=cost(15.0),name="attn_fwd")(meta,q,k,v)
def attn_bwd(meta,first,pairs,q,k,v,ctx,dctx,lse,carry):
    t,w=q.shape; kn=k.shape[0]; wide=128*pairs
    sd=jax.ShapeDtypeStruct
    def col(n,width):
        return pl.BlockSpec((n,width),lambda i:(0,first//pairs))
    def kernel(*refs):
        bwd_kernel(2*first,*refs[:7],*refs[-7:])
    carry=() if carry is None else tuple(carry)
    return pl.pallas_call(kernel,grid=(1,),
        in_specs=[SM,col(t,wide),col(kn,wide),col(kn,wide),col(t,wide),col(t,wide),pl.BlockSpec((t,128),lambda i:(0,0))]+[pl.BlockSpec(memory_space=pl.ANY)]*len(carry),
        out_specs=[col(t,wide)]*3+[col(kn-t,2*wide)],
        out_shape=[sd((t,w),f32)]*3+[sd((kn-t,2*w),bf16)],
        scratch_shapes=[pltpu.VMEM((kn,128),bf16),pltpu.VMEM((kn,wide),f32),pltpu.VMEM((kn,wide),f32)],
        input_output_aliases={7+i:i for i in range(len(carry))},cost_estimate=cost(9.0*pairs),
        compiler_params=pltpu.CompilerParams(vmem_limit_bytes=(16+4*pairs)*2**20),name="attn_bwd")(meta,q,k,v,ctx,dctx,lse,*carry)

def make_meta(lengths, side, local, full):
    ends=jnp.cumsum(lengths)
    starts=ends-lengths
    win=side*(local//2); own=side*local
    nqb=local//BLK
    b0=own+jnp.arange(nqb)*BLK
    b1=b0+BLK-1
    bounds_lo=jnp.concatenate([jnp.zeros((1,),jnp.int32),ends])
    bounds_hi=jnp.concatenate([ends,jnp.full((1,),full,jnp.int32)])
    seg0=jnp.sum((b0[:,None]>=ends[None]).astype(jnp.int32),1)
    seg1=jnp.sum((b1[:,None]>=ends[None]).astype(jnp.int32),1)
    first=jnp.sum(jnp.where(jnp.arange(6)[None]==seg0[:,None],bounds_lo[None],0),1)
    last=jnp.sum(jnp.where(jnp.arange(6)[None]==seg1[:,None],bounds_hi[None],0),1)
    lo=jnp.maximum(first-win,0)//BLK
    hi=jnp.minimum((last-win+BLK-1)//BLK,(local+local//2)//BLK)
    return jnp.concatenate([ends,win[None],own[None],side[None],jnp.stack([lo,hi],1).reshape(-1)]).astype(jnp.int32)

TB=256

def gelu_parts(z):
    a=jnp.abs(z)
    t=1.0/(1.0+a*(0.3275911*0.7071067811865476))
    e=jnp.exp(-0.5*z*z)
    poly=t*(0.127414796+t*(-0.142248368+t*(0.7107068705+t*(-0.7265760135+t*0.5307027145))))
    ht=poly*e
    phi=jnp.where(z>=0.0,1.0-ht,ht)
    return z*phi, phi+z*(e*0.3989422804014327)

def rows8(x):
    return jnp.sum(x.reshape(x.shape[0]//8,8,x.shape[1]),axis=0)

def norm_parts(z):
    mu=jnp.mean(z,axis=-1,keepdims=True)
    c=z-mu
    var=jnp.mean(c*c,axis=-1,keepdims=True)
    rstd=lax.rsqrt(var+1e-6)
    return c*rstd, rstd

def norm_back(d, gain, xhat, rstd):
    dx=d*gain
    a=jnp.mean(dx,axis=-1,keepdims=True)
    b=jnp.mean(dx*xhat,axis=-1,keepdims=True)
    return rstd*(dx-a-xhat*b)

def ffn_kernel(meta, hid_ref, ctx_ref, cm_ref, og_ref, wo_ref, win_ref, wout_ref, ln_ref,
               ho_ref, dres_ref, dctx_ref, dconv_ref, keep_ref, send_ref, gln_ref,
               act_ref, dff_ref, x1_ref, dfo_ref, datt_ref, mix_ref):
    n=hid_ref.shape[0]; d=hid_ref.shape[1]; groups=win_ref.shape[0]; gi=d//groups; go=win_ref.shape[2]
    attn=dctx_ref.shape[1]
    tile=512
    gln_ref[...]=jnp.zeros(gln_ref.shape,f32)
    def block(i,_):
        r0=pl.multiple_of(i*TB,TB)
        rows=pl.ds(r0,TB)
        g1=ln_ref[0:1,:];b1=ln_ref[1:2,:];g2=ln_ref[2:3,:];b2=ln_ref[3:4,:]
        att=dot_nn(jnp.concatenate([ctx_ref[rows,:],cm_ref[rows,:]],axis=1),wo_ref[...])
        xhat1,rstd1=norm_parts(hid_ref[rows,:].astype(f32)+att)
        first=xhat1*g1+b1
        x1=first.astype(bf16)
        for g in range(groups):
            x1_ref[g,rows,:]=x1[:,g*gi:(g+1)*gi]
        mix_ref[0,rows,:]=ctx_ref[rows,:]
        mix_ref[1,rows,:]=cm_ref[rows,:]
        tiles=[(g,c) for g in range(groups) for c in range(go//tile)]
        def up(g,c):
            return dot_nn(x1[:,g*gi:(g+1)*gi],win_ref[g,:,c*tile:(c+1)*tile])
        outs=[None]*groups
        ahead=up(*tiles[0])
        for t,(g,c) in enumerate(tiles):
            z=ahead
            if t+1<len(tiles):
                ahead=up(*tiles[t+1])
            cols=slice(c*tile,(c+1)*tile)
            a,gp=gelu_parts(z)
            ab=a.astype(bf16)
            act_ref[g,rows,cols]=ab
            dff_ref[g,rows,cols]=gp.astype(bf16)
            o=dot_nn(ab,wout_ref[g,cols,:])
            outs[g]=o if outs[g] is None else outs[g]+o
        xhat2,rstd2=norm_parts(first+jnp.concatenate(outs,axis=1))
        pos=meta[6]+r0+lax.broadcasted_iota(jnp.int32,(TB,d),0)
        valid=pos<meta[4]
        ho_ref[rows,:]=jnp.where(valid,xhat2*g2+b2,0.0).astype(bf16)
        gn=jnp.where(valid,og_ref[rows,:].astype(f32),0.0)
        gln_ref[16:24,:]+=rows8(gn*xhat2)
        gln_ref[24:32,:]+=rows8(gn)
        dres2=norm_back(gn,g2,xhat2,rstd2)
        dfo=dres2.astype(bf16)
        for g in range(groups):
            dfo_ref[g,rows,:]=dfo[:,g*gi:(g+1)*gi]
        def down(g,c):
            return dot_nt(dfo[:,g*gi:(g+1)*gi],wout_ref[g,c*tile:(c+1)*tile,:])
        backs=[None]*groups
        ahead=down(*tiles[0])
        for t,(g,c) in enumerate(tiles):
            da=ahead
            if t+1<len(tiles):
                ahead=down(*tiles[t+1])
            cols=slice(c*tile,(c+1)*tile)
            dh=(da*dff_ref[g,rows,cols].astype(f32)).astype(bf16)
            dff_ref[g,rows,cols]=dh
            o=dot_nt(dh,win_ref[g,:,cols])
            backs[g]=o if backs[g] is None else backs[g]+o
        dfirst=dres2+jnp.concatenate(backs,axis=1)
        gln_ref[0:8,:]+=rows8(dfirst*xhat1)
        gln_ref[8:16,:]+=rows8(dfirst)
        dres1=norm_back(dfirst,g1,xhat1,rstd1)
        dres_ref[rows,:]=dres1
        datt=dres1.astype(bf16)
        datt_ref[rows,:]=datt
        dm=dot_nt(datt,wo_ref[...])
        dctx_ref[rows,:]=dm[:,:attn].astype(bf16)
        dconv_ref[rows,:]=dm[:,attn:]
        return 0
    lax.fori_loop(0,n//TB,block,0)
    side=meta[7]
    for ref,g in ((send_ref,1-side),(keep_ref,side)):
        at=0
        for c in range(go//gi):
            ref[at*gi:(at+1)*gi,:]=dot_tn(act_ref[g,:,c*gi:(c+1)*gi],dfo_ref[g]).astype(ref.dtype)
            at+=1
        wide=dot_tn(x1_ref[g],dff_ref[g]).astype(ref.dtype)
        for c in range(go//gi):
            ref[at*gi:(at+1)*gi,:]=wide[:,c*gi:(c+1)*gi]
            at+=1
        for c in range(d//attn):
            ref[at*gi:(at+1)*gi,:]=dot_tn(mix_ref[g],datt_ref[:,c*attn:(c+1)*attn]).astype(ref.dtype)
            at+=1

def ffn(meta,hid,ctx,cm,og,wo,win,wout,ln):
    n,d=hid.shape; g,gi,go=win.shape; attn=ctx.shape[1]
    sd=jax.ShapeDtypeStruct
    return pl.pallas_call(ffn_kernel,in_specs=[SM]+[VM]*8,out_specs=[VM]*7,
        out_shape=[sd((n,d),bf16),sd((n,d),f32),sd((n,attn),bf16),sd((n,attn),f32),
                   sd((2*go+d,attn),bf16),sd((2*go+d,attn),bf16),sd((32,d),f32)],
        scratch_shapes=[pltpu.VMEM((g,n,go),bf16),pltpu.VMEM((g,n,go),bf16),pltpu.VMEM((g,n,gi),bf16),
                        pltpu.VMEM((g,n,gi),bf16),pltpu.VMEM((n,d),bf16),pltpu.VMEM((2,n,attn),bf16)],
        cost_estimate=cost(40.0),compiler_params=pltpu.CompilerParams(vmem_limit_bytes=40*2**20),name="ffn")(meta,hid,ctx,cm,og,wo,win,wout,ln)

TAPS=9
HALF=4
PAD=8
TB=256
CH=64
CS=32

def doc_bounds(meta, first, shape):
    pos=first+lax.broadcasted_iota(jnp.int32,shape,0)
    nxt=jnp.full(shape,2**30,jnp.int32)
    prv=jnp.full(shape,-2**30,jnp.int32)
    for d in range(5):
        e=meta[d]
        nxt=jnp.minimum(nxt,jnp.where(e>pos,e,2**30))
        prv=jnp.maximum(prv,jnp.where(e<=pos,e,-2**30))
    return nxt-pos, pos-prv

def tap_mask(bounds, o):
    rem,age=bounds
    if o>HALF:
        return rem>(o-HALF)
    return age>=(HALF-o)

def masked(x, bounds, o):
    if o==HALF:
        return x
    return jnp.where(tap_mask(bounds,o),x,0.0)

def tap_onehot(rows, cols, o):
    r=lax.broadcasted_iota(jnp.int32,(rows,cols),0)
    c=lax.broadcasted_iota(jnp.int32,(rows,cols),1)
    return jnp.where(r==(c//64)*TAPS+o,1.0,0.0).astype(bf16)

def pre_kernel(meta, hid_ref, halo_ref, wq_ref, wk_ref, wv_ref, wc_ref, taps_ref, wp_ref, wck_ref,
               q_ref, kw_ref, vw_ref, cx_ref, depth_ref, ck_ref, kern_hbm, cm_ref,
               hx_ref, wx_ref, lx_ref, kern_ref, sems):
    n,d=hid_ref.shape; half=halo_ref.shape[0]; attn=q_ref.shape[1]
    side=meta[7]
    own_off=side*half; halo_off=(1-side)*n
    jt=attn//128; jd=d//128
    for o in range(TAPS):
        wx_ref[:,o*attn:(o+1)*attn]=dot_nn(wck_ref[...],tap_onehot(HEADS*TAPS,attn,o)).astype(bf16)
    left=jnp.where(side==1,halo_ref[half-16:half,:].astype(f32),0.0)
    right=jnp.where(side==0,halo_ref[0:16,:].astype(f32),0.0)
    rims=jnp.concatenate([left,right],axis=0).astype(bf16)
    crim=dot_nn(rims,wc_ref[...]).astype(bf16).astype(f32)
    for j in range(jd):
        hx_ref[j,0:PAD,:]=left[PAD:2*PAD,j*128:(j+1)*128]
        hx_ref[j,n+PAD:n+2*PAD,:]=right[0:PAD,j*128:(j+1)*128]
    for j in range(jt):
        cx_ref[j,0:PAD,:]=crim[PAD:2*PAD,j*128:(j+1)*128]
        cx_ref[j,n+PAD:n+2*PAD,:]=crim[16:16+PAD,j*128:(j+1)*128]
    def project(i,_):
        r0=pl.multiple_of(i*TB,TB)
        x=hid_ref[pl.ds(r0,TB),:]
        q_ref[pl.ds(r0,TB),:]=dot_nn(x,wq_ref[...]).astype(bf16)
        ow=pl.multiple_of(own_off+r0,TB)
        kw_ref[pl.ds(ow,TB),:]=dot_nn(x,wk_ref[...]).astype(bf16)
        vw_ref[pl.ds(ow,TB),:]=dot_nn(x,wv_ref[...]).astype(bf16)
        c=dot_nn(x,wc_ref[...]).astype(bf16).astype(f32)
        rp=pl.multiple_of(r0+PAD,PAD)
        for j in range(jt):
            cx_ref[j,pl.ds(rp,TB),:]=c[:,j*128:(j+1)*128]
        xf=x.astype(f32)
        for j in range(jd):
            hx_ref[j,pl.ds(rp,TB),:]=xf[:,j*128:(j+1)*128]
        return 0
    lax.fori_loop(0,n//TB,project,0)
    def project_halo(i,_):
        r0=pl.multiple_of(i*TB,TB)
        x=halo_ref[pl.ds(r0,TB),:]
        ow=pl.multiple_of(halo_off+r0,TB)
        kw_ref[pl.ds(ow,TB),:]=dot_nn(x,wk_ref[...]).astype(bf16)
        vw_ref[pl.ds(ow,TB),:]=dot_nn(x,wv_ref[...]).astype(bf16)
        return 0
    lax.fori_loop(0,half//TB,project_halo,0)
    def depthwise(i,_):
        r0=pl.multiple_of(i*CH,CH)
        bounds=doc_bounds(meta,meta[6]+r0,(CH,128))
        for j in range(jd):
            acc=None
            for o in range(TAPS):
                x=hx_ref[j,pl.ds(r0+PAD+o-HALF,CH),:]
                term=masked(x*taps_ref[o:o+1,j*128:(j+1)*128].astype(f32),bounds,o)
                acc=term if acc is None else acc+term
            depth_ref[pl.ds(r0,CH),j*128:(j+1)*128]=acc.astype(bf16)
        return 0
    lax.fori_loop(0,n//CH,depthwise,0)
    def dynamic(r0):
        ck=dot_nn(depth_ref[pl.ds(r0,TB),:],wp_ref[...])
        ck_ref[pl.ds(r0,TB),:]=ck
        mk=(ck*q_ref[pl.ds(r0,TB),:].astype(f32)).astype(bf16)
        for o in range(TAPS):
            lx_ref[o]=dot_nn(mk,wx_ref[:,o*attn:(o+1)*attn])
        def soft(s,_):
            s0=pl.multiple_of(s*CS,CS)
            rows=pl.ds(s0,CS)
            t0=pl.multiple_of(r0+s0,CS)
            bounds=doc_bounds(meta,meta[6]+t0,(CS,128))
            for j in range(jt):
                cols=slice(j*128,(j+1)*128)
                ls=[lx_ref[o,rows,cols] for o in range(TAPS)]
                m=ls[0]
                for o in range(1,TAPS):
                    m=jnp.maximum(m,ls[o])
                es=[jnp.exp(l-m) for l in ls]
                tot=es[0]
                for o in range(1,TAPS):
                    tot=tot+es[o]
                inv=1.0/tot
                acc=None
                for o in range(TAPS):
                    k=es[o]*inv
                    kern_ref[o,pl.ds(t0,CS),cols]=k.astype(bf16)
                    term=masked(k*cx_ref[j,pl.ds(t0+PAD+o-HALF,CS),:],bounds,o)
                    acc=term if acc is None else acc+term
                cm_ref[pl.ds(t0,CS),cols]=acc.astype(bf16)
            return 0
        lax.fori_loop(0,TB//CS,soft,0)
    stores=[]
    for b in range(n//TB):
        dynamic(b*TB)
        x=pltpu.make_async_copy(kern_ref.at[:,pl.ds(b*TB,TB),:],kern_hbm.at[:,pl.ds(b*TB,TB),:],sems.at[b])
        x.start()
        stores.append(x)
    for x in stores:
        x.wait()

def pre(meta,hid,halo,wq,wk,wv,wc,taps,wp,wck):
    n,d=hid.shape; half=halo.shape[0]; a=wq.shape[1]; sd=jax.ShapeDtypeStruct
    anys=pl.BlockSpec(memory_space=pl.ANY)
    def whole(*shape):
        return pl.BlockSpec(shape,lambda i:(0,)*len(shape))
    proj=whole(d,a)
    return pl.pallas_call(pre_kernel,grid=(1,),in_specs=[SM,whole(n,d),VM,proj,proj,proj,proj,VM,proj,VM],out_specs=[VM]*6+[anys,VM],
        out_shape=[sd((n,a),bf16),sd((n+half,a),bf16),sd((n+half,a),bf16),sd((a//128,n+2*PAD,128),f32),
                   sd((n,d),bf16),sd((n,a),f32),sd((TAPS,n,a),bf16),sd((n,a),bf16)],
        scratch_shapes=[pltpu.VMEM((d//128,n+2*PAD,128),f32),pltpu.VMEM((a,TAPS*a),bf16),pltpu.VMEM((TAPS,TB,a),f32),
                        pltpu.VMEM((TAPS,n,a),bf16),pltpu.SemaphoreType.DMA((n//TB,))],
        cost_estimate=cost(30.0),compiler_params=pltpu.CompilerParams(vmem_limit_bytes=40*2**20),name="pre")(meta,hid,halo,wq,wk,wv,wc,taps,wp,wck)

def conv_back_kernel(meta, dconv_ref, cm_ref, kern_ref, cx_ref, q_ref, ck_ref, depth_ref,
                     wp_ref, wck_ref,
                     dqc_ref, dc_ref, dda_ref, ddb_ref, rimc_ref, gp_ref,
                     p_ref, pr_ref, dlc_ref, mk_ref, dck_ref, wcx_ref, dep_ref):
    d=depth_ref.shape[1]; attn,n=q_ref.shape[1],dc_ref.shape[0]
    i=pl.program_id(0)
    side=meta[7]; jt=attn//128; jd=d//128; hd=jd//2
    dds=[(dda_ref,j) if j<hd else (ddb_ref,j-hd) for j in range(jd)]
    @pl.when(i==0)
    def _():
        zero=jnp.zeros((2*PAD,128),f32)
        for j in range(jt):
            for o in range(TAPS):
                p_ref[o,j,0:2*PAD,:]=zero
                p_ref[o,j,n+2*PAD:n+4*PAD,:]=zero
        for ref,j in dds:
            ref[j,0:2*PAD,:]=zero
            ref[j,n+2*PAD:n+4*PAD,:]=zero
        r=lax.broadcasted_iota(jnp.int32,(HEADS*TAPS,attn),0)
        c=lax.broadcasted_iota(jnp.int32,(HEADS*TAPS,attn),1)
        spread=jnp.where((c%64<TAPS)&(r==(c//64)*TAPS+c%64),1.0,0.0).astype(bf16)
        wcx_ref[...]=dot_nn(wck_ref[...],spread).astype(bf16)
    def ones_block(w):
        return jnp.where(lax.broadcasted_iota(jnp.int32,(w,w),0)//64==lax.broadcasted_iota(jnp.int32,(w,w),1)//64,1.0,0.0).astype(bf16)
    ones256=ones_block(256); ones128=ones_block(128)
    lane=lax.broadcasted_iota(jnp.int32,(TB,attn),1)%64
    def dynamic():
        r0=pl.multiple_of(i*TB,TB)
        rows=pl.ds(r0,TB)
        def products(s,_):
            s0=pl.multiple_of(s*CS,CS)
            t0=pl.multiple_of(r0+s0,CS)
            bounds=doc_bounds(meta,meta[6]+t0,(CS,128))
            for j in range(jt):
                cols=slice(j*128,(j+1)*128)
                g=dconv_ref[pl.ds(s0,CS),cols]
                cm=cm_ref[pl.ds(s0,CS),cols].astype(f32)
                for o in range(TAPS):
                    cs=masked(cx_ref[j,pl.ds(t0+PAD+o-HALF,CS),:],bounds,o)
                    pr_ref[o,pl.ds(s0,CS),cols]=(g*(cs-cm)).astype(bf16)
                    p_ref[o,j,pl.ds(t0+2*PAD,CS),:]=masked(kern_ref[o,pl.ds(s0,CS),cols].astype(f32)*g,bounds,o)
            return 0
        lax.fori_loop(0,TB//CS,products,0)
        dl=jnp.zeros((TB,attn),f32)
        for o in range(TAPS):
            pr=pr_ref[o]
            dk=jnp.concatenate([dot_nn(pr[:,:256],ones256),dot_nn(pr[:,256:],ones128)],axis=1)
            dl=jnp.where(lane==o,kern_ref[o].astype(f32)*dk,dl)
        dlb=dl.astype(bf16)
        dlc_ref[rows,:]=dlb
        dmk=dot_nt(dlb,wcx_ref[...])
        dep_ref[rows,:]=depth_ref[...]
        q=q_ref[...].astype(f32)
        ck=ck_ref[...]
        mk_ref[rows,:]=(ck*q).astype(bf16)
        dqc_ref[...]=dmk*ck
        dck=(dmk*q).astype(bf16)
        dck_ref[rows,:]=dck
        dd=dot_nt(dck,wp_ref[...])
        rp=pl.multiple_of(r0+2*PAD,PAD)
        for j in range(jd):
            dds[j][0][dds[j][1],pl.ds(rp,TB),:]=dd[:,j*128:(j+1)*128]
    dynamic()
    @pl.when(i==pl.num_programs(0)-1)
    def _():
        def gather_c(row, size):
            out=[]
            for j in range(jt):
                acc=None
                for o in range(TAPS):
                    x=p_ref[o,j,pl.ds(row+PAD+HALF-o,size),:]
                    acc=x if acc is None else acc+x
                out.append(acc)
            return out
        def own_c(i,_):
            r0=pl.multiple_of(i*CS,CS)
            out=gather_c(r0+PAD,CS)
            for j in range(jt):
                dc_ref[pl.ds(r0,CS),j*128:(j+1)*128]=out[j]
            return 0
        lax.fori_loop(0,n//CS,own_c,0)
        left=gather_c(0,PAD); right=gather_c(n+PAD,PAD)
        for j in range(jt):
            rimc_ref[:,j*128:(j+1)*128]=jnp.where(side==1,left[j],right[j])
        for b in range(d//attn):
            gp_ref[b]=dot_tn(dep_ref[:,b*attn:(b+1)*attn],dck_ref[...]).astype(gp_ref.dtype)
        gp_ref[d//attn]=dot_tn(mk_ref[...],dlc_ref[...]).astype(gp_ref.dtype)

def taps_back_kernel(meta, hid_ref, halo_ref, dd_ref, taps_ref, dh_ref, rim_ref, gtap_ref):
    n,d=hid_ref.shape; half=halo_ref.shape[0]
    side=meta[7]; jd=d//128
    def gather_h(row, size, j, hx, bounds, sums):
        acc=None; new=[]
        for o in range(TAPS):
            x=masked(dd_ref[j,pl.ds(row+PAD+o-HALF,size),:],bounds,o)
            b=TAPS-1-o
            term=x*taps_ref[b:b+1,j*128:(j+1)*128].astype(f32)
            acc=term if acc is None else acc+term
            new.append(jnp.sum((x*hx).reshape(size//8,8,128),axis=0))
        return acc,[s+t for s,t in zip(sums,new)]
    lhalo=jnp.where(side==1,halo_ref[half-16:half,:].astype(f32),0.0)[PAD:2*PAD,:]
    rhalo=jnp.where(side==0,halo_ref[0:16,:].astype(f32),0.0)[0:PAD,:]
    for j in range(jd):
        cols=slice(j*128,(j+1)*128)
        sums=[jnp.zeros((8,128),f32) for _ in range(TAPS)]
        la,sums=gather_h(0,PAD,j,lhalo[:,cols],doc_bounds(meta,meta[6]-PAD,(PAD,128)),sums)
        ra,sums=gather_h(n+PAD,PAD,j,rhalo[:,cols],doc_bounds(meta,meta[6]+n,(PAD,128)),sums)
        rim_ref[:,cols]=jnp.where(side==1,la,ra)
        def own_h(i,sums):
            r0=pl.multiple_of(i*CS,CS)
            acc,sums=gather_h(r0+PAD,CS,j,hid_ref[pl.ds(r0,CS),cols].astype(f32),doc_bounds(meta,meta[6]+r0,(CS,128)),sums)
            dh_ref[pl.ds(r0,CS),cols]=acc
            return sums
        sums=lax.fori_loop(0,n//CS,own_h,sums)
        for o in range(TAPS):
            b=TAPS-1-o
            gtap_ref[b*8:(b+1)*8,cols]=sums[o]

def conv_back(meta,dconv,cm,kern,cx,q,ck,depth,wp,wck):
    n,d=depth.shape; a=q.shape[1]; sd=jax.ShapeDtypeStruct
    def row(w):
        return pl.BlockSpec((TB,w),lambda i:(i,0))
    def whole(*shape):
        return pl.BlockSpec(shape,lambda i:(0,)*len(shape))
    half=(d//256,n+4*PAD,128)
    return pl.pallas_call(conv_back_kernel,grid=(n//TB,),
        in_specs=[SM,row(a),row(a),pl.BlockSpec((TAPS,TB,a),lambda i:(0,i,0)),VM,row(a),row(a),row(d),VM,VM],
        out_specs=[row(a),whole(n,a),whole(*half),whole(*half),whole(PAD,a),whole(d//a+1,a,a)],
        out_shape=[sd((n,a),f32),sd((n,a),f32),sd(half,f32),sd(half,f32),sd((PAD,a),f32),sd((d//a+1,a,a),bf16)],
        scratch_shapes=[pltpu.VMEM((TAPS,a//128,n+4*PAD,128),f32),pltpu.VMEM((TAPS,TB,a),bf16),
                        pltpu.VMEM((n,a),bf16),pltpu.VMEM((n,a),bf16),pltpu.VMEM((n,a),bf16),pltpu.VMEM((a,a),bf16),pltpu.VMEM((n,d),bf16)],
        cost_estimate=cost(20.0),compiler_params=pltpu.CompilerParams(vmem_limit_bytes=48*2**20),name="conv_back")(meta,dconv,cm,kern,cx,q,ck,depth,wp,wck)

def taps_back(meta,part,hid,halo,dd,taps):
    n=hid.shape[0]; d=dd.shape[0]*128; sd=jax.ShapeDtypeStruct
    def col(rows):
        return pl.BlockSpec((rows,d),lambda i:(0,part))
    def whole(*shape):
        return pl.BlockSpec(shape,lambda i:(0,)*len(shape))
    return pl.pallas_call(taps_back_kernel,grid=(1,),in_specs=[SM,col(n),col(halo.shape[0]),whole(*dd.shape),col(TAPS)],
        out_specs=[whole(n,d),whole(PAD,d),whole(TAPS*8,d)],
        out_shape=[sd((n,d),f32),sd((PAD,d),f32),sd((TAPS*8,d),f32)],
        cost_estimate=cost(6.0),compiler_params=pltpu.CompilerParams(vmem_limit_bytes=24*2**20),name="taps_back")(meta,hid,halo,dd,taps)

def proj_back_kernel(meta, hid_ref, dqa_ref, dqc_ref, dk_ref, dv_ref, dkv_ref, dc_ref, rimc_ref, gp_ref, gta_ref, gtb_ref, gln_ref,
                     dp_ref, keep_ref, send_ref):
    n,d=hid_ref.shape; attn=dqa_ref.shape[1]; half=dkv_ref.shape[0]
    side=meta[7]
    shift=(1-side)*half
    def block(i,_):
        r0=pl.multiple_of(i*TB,TB)
        rows=pl.ds(r0,TB)
        inside=(r0>=shift)&(r0<shift+half)
        scale=jnp.where(inside,1.0,0.0)
        hr=pl.multiple_of(jnp.where(inside,r0-shift,0),TB)
        other=dkv_ref[pl.ds(hr,TB),:].astype(f32)*scale
        top=jnp.where((side==1)&(i==0),rimc_ref[...],0.0)
        bottom=jnp.where((side==0)&(i==n//TB-1),rimc_ref[...],0.0)
        rim=jnp.concatenate([top,jnp.zeros((TB-2*PAD,attn),f32),bottom],axis=0)
        dp_ref[rows,0:attn]=(dqa_ref[rows,:]+dqc_ref[rows,:]).astype(bf16)
        for j in range(attn//128):
            cols=slice(j*128,(j+1)*128)
            dp_ref[rows,attn+j*128:attn+(j+1)*128]=(dk_ref[rows,cols]+other[:,j*256:j*256+128]).astype(bf16)
            dp_ref[rows,2*attn+j*128:2*attn+(j+1)*128]=(dv_ref[rows,cols]+other[:,j*256+128:(j+1)*256]).astype(bf16)
        dp_ref[rows,3*attn:]=(dc_ref[rows,:]+rim).astype(bf16)
        return 0
    lax.fori_loop(0,n//TB,block,0)
    zeros=jnp.zeros((1,d),f32)
    small=[jnp.concatenate([jnp.sum(t[o*8:(o+1)*8,:],axis=0,keepdims=True) for t in (gta_ref,gtb_ref)],axis=1) for o in range(TAPS)]
    small+=[jnp.sum(gln_ref[k*8:(k+1)*8,:],axis=0,keepdims=True) for k in range(4)]
    small=jnp.concatenate(small+[zeros]*(16-len(small)),axis=0)
    for ref,h in ((send_ref,1-side),(keep_ref,side)):
        hc=pl.ds(pl.multiple_of(h*attn,128),attn)
        for k in range(4):
            ref[k*attn:(k+1)*attn,:]=dot_tn(hid_ref[:,hc],dp_ref[:,k*attn:(k+1)*attn]).astype(ref.dtype)
        ref[4*attn:5*attn,:]=gp_ref[h]
        ref[5*attn:6*attn,:]=gp_ref[2]
        @pl.when(h==1)
        def _():
            ref[5*attn:5*attn+16,:]=small[:,:attn].astype(bf16)
            ref[5*attn+16:5*attn+32,:]=small[:,attn:].astype(bf16)

def proj_back(meta,hid,dqa,dqc,dk,dv,dkv,dc,rimc,gp,gta,gtb,gln):
    n,d=hid.shape; a=dqa.shape[1]; sd=jax.ShapeDtypeStruct
    return pl.pallas_call(proj_back_kernel,in_specs=[SM]+[VM]*12,out_specs=[VM]*3,
        out_shape=[sd((n,4*a),bf16),sd((6*a,a),bf16),sd((6*a,a),bf16)],cost_estimate=cost(9.0),
        compiler_params=pltpu.CompilerParams(vmem_limit_bytes=16*2**20),name="proj_back")(meta,hid,dqa,dqc,dk,dv,dkv,dc,rimc,gp,gta,gtb,gln)

def grad_in_kernel(meta, dp_ref, dres_ref, dha_ref, dhb_ref, rima_ref, rimb_ref, wq_ref, wk_ref, wv_ref, wc_ref, gi_ref):
    n,d=gi_ref.shape; attn=wq_ref.shape[1]
    side=meta[7]
    def block(i,_):
        r0=pl.multiple_of(i*TB,TB)
        rows=pl.ds(r0,TB)
        acc=dres_ref[rows,:]+jnp.concatenate([dha_ref[rows,:],dhb_ref[rows,:]],axis=1)
        for k,w in enumerate((wq_ref,wk_ref,wv_ref,wc_ref)):
            acc=acc+dot_nt(dp_ref[rows,k*attn:(k+1)*attn],w[...])
        gi_ref[rows,:]=acc
        return 0
    lax.fori_loop(0,n//TB,block,0)
    at=pl.multiple_of((1-side)*(n-PAD),PAD)
    gi_ref[pl.ds(at,PAD),:]+=jnp.concatenate([rima_ref[...],rimb_ref[...]],axis=1)

def grad_input(meta,dp,dres,dha,dhb,rima,rimb,wq,wk,wv,wc):
    n,d=dres.shape; sd=jax.ShapeDtypeStruct
    return pl.pallas_call(grad_in_kernel,in_specs=[SM]+[VM]*10,out_specs=VM,
        out_shape=sd((n,d),f32),cost_estimate=cost(9.0),
        compiler_params=pltpu.CompilerParams(vmem_limit_bytes=16*2**20),name="grad_input")(meta,dp,dres,dha,dhb,rima,rimb,wq,wk,wv,wc)

AT=16

def swap_pairs():
    return [(0,1),(1,0)]

def stage_bits(size, scatter):
    bits=[]
    b=1
    while b<size:
        bits.append(b)
        b*=2
    lead=bits[:3]
    other=lead[-1:]+lead[:-1]+bits[3:]
    n=min(scatter,len(bits))
    return list(zip(bits,other))[:n],bits[n:]

def row_pairs(rows, bits):
    return [(r*2+s,(r^bits[s])*2+s) for r in range(rows) for s in range(2)]

def comm_meta(side, row, rows):
    stages,_=stage_bits(rows,4)
    own=[jnp.where(side==0,(row//b0)%2,(row//b1)%2) for b0,b1 in stages]
    oth=[jnp.where(side==0,(row//b1)%2,(row//b0)%2) for b0,b1 in stages]
    c=jnp.int32(0); c2=jnp.int32(0)
    for u,v in list(zip(own,oth))[:3]:
        c=c*2+u; c2=c2*2+v
    own=own+[jnp.int32(0)]*(4-len(own))
    return jnp.stack(own+[c,c2]).astype(jnp.int32)

def cost(us):
    return pl.CostEstimate(flops=int(us*1.0e9),bytes_accessed=0,transcendentals=0)

def fold_kernel(stage, meta, keep_ref, got_ref, k_ref, s_ref):
    h=k_ref.shape[0]; ch=48
    b=meta[AT+stage]
    def body(i,_):
        r=pl.multiple_of(i*ch,16)
        for ref,at in ((k_ref,b*h),(s_ref,(1-b)*h)):
            src=pl.multiple_of(at+r,16)
            ref[pl.ds(r,ch),:]=(keep_ref[pl.ds(src,ch),:].astype(f32)+got_ref[pl.ds(src,ch),:].astype(f32)).astype(bf16)
        return 0
    lax.fori_loop(0,h//ch,body,0)

def fold(meta, stage, keep, got):
    h=keep.shape[0]//2; sd=jax.ShapeDtypeStruct((h,keep.shape[1]),keep.dtype)
    def kernel(meta_ref, keep_ref, got_ref, k_ref, s_ref):
        fold_kernel(stage, meta_ref, keep_ref, got_ref, k_ref, s_ref)
    return pl.pallas_call(kernel,in_specs=[SM,VM,VM],out_specs=[VM,VM],out_shape=[sd,sd],cost_estimate=cost(1.0),
        compiler_params=pltpu.CompilerParams(vmem_limit_bytes=16*2**20),name="fold")(meta,keep,got)

def add_low(x,y):
    return (x.astype(f32)+y.astype(f32)).astype(bf16)

def place(meta, mine_ref, other_ref, buf_ref, sems, chunks):
    side=meta[7]
    rows=mine_ref.shape[0]//chunks
    copies=[]
    for i in range(chunks):
        for k,ref in enumerate((mine_ref,other_ref)):
            half=side if k==0 else 1-side
            at=lax.bitwise_xor(meta[AT+4+k],jnp.int32(i))
            copies.append(pltpu.make_async_copy(ref.at[pl.ds(i*rows,rows),:],
                buf_ref.at[half,pl.ds(pl.multiple_of(at*rows,16),rows),:],sems.at[i,k]))
    for c in copies:
        c.start()
    for c in copies:
        c.wait()

def unpack_a_kernel(chunks, meta, mine_ref, other_ref, gout_ref, gin_ref, gwo_ref, buf_ref, sems):
    place(meta,mine_ref,other_ref,buf_ref,sems,chunks)
    a=buf_ref.shape[2]; g,go,_=gout_ref.shape; ch=128
    per=go//a
    def body(i,_):
        r=pl.multiple_of(i*ch,ch)
        for h in range(g):
            for c in range(per):
                gout_ref[h,pl.ds(pl.multiple_of(c*a+r,ch),ch),:]=buf_ref[h,pl.ds(pl.multiple_of(c*a+r,ch),ch),:].astype(f32)
                gin_ref[h,pl.ds(r,ch),c*a:(c+1)*a]=buf_ref[h,pl.ds(pl.multiple_of((per+c)*a+r,ch),ch),:].astype(f32)
            for c in range(gwo_ref.shape[1]//a):
                gwo_ref[pl.ds(pl.multiple_of(h*a+r,ch),ch),c*a:(c+1)*a]=buf_ref[h,pl.ds(pl.multiple_of((2*per+c)*a+r,ch),ch),:].astype(f32)
        return 0
    lax.fori_loop(0,a//ch,body,0)

ANYS=pl.BlockSpec(memory_space=pl.ANY)
def unpack_a(meta, mine, other, g, gi, go, d, chunks):
    sd=jax.ShapeDtypeStruct
    def kernel(*refs):
        unpack_a_kernel(chunks,*refs)
    return pl.pallas_call(kernel,in_specs=[SM,ANYS,ANYS],out_specs=[VM]*3,
        out_shape=[sd((g,go,gi),f32),sd((g,gi,go),f32),sd((d,d),f32)],cost_estimate=cost(8.0),
        scratch_shapes=[pltpu.VMEM((2,)+mine.shape,bf16),pltpu.SemaphoreType.DMA((chunks,2))],
        compiler_params=pltpu.CompilerParams(vmem_limit_bytes=20*2**20),name="unpack_a")(meta,mine,other)

def unpack_b_kernel(chunks, which, meta, part_ref, q_ref, k_ref, v_ref, c_ref, p_ref, ck_ref, small_ref, buf_ref, sems, outs):
    a=buf_ref.shape[1]; rows=part_ref.shape[0]//chunks
    h=meta[7] if which==0 else 1-meta[7]
    copies=[]
    for i in range(chunks):
        at=lax.bitwise_xor(meta[AT+4+which],jnp.int32(i))
        copies.append(pltpu.make_async_copy(part_ref.at[pl.ds(i*rows,rows),:],
            buf_ref.at[pl.ds(pl.multiple_of(at*rows,16),rows),:],sems.at[i]))
    for x in copies:
        x.start()
    for x in copies:
        x.wait()
    backs=[]
    for i,ref in enumerate((q_ref,k_ref,v_ref,c_ref,p_ref)):
        outs[i]=buf_ref[i*a:(i+1)*a,:].astype(f32)
        x=pltpu.make_async_copy(outs.at[i],ref.at[pl.ds(pl.multiple_of(h*a,128),a),:],sems.at[chunks+i])
        x.start()
        backs.append(x)
    r=lax.broadcasted_iota(jnp.int32,(HEADS*TAPS,a),0)
    c=lax.broadcasted_iota(jnp.int32,(HEADS*TAPS,a),1)
    spread=jnp.where((c%64<TAPS)&(r==(c//64)*TAPS+c%64),1.0,0.0).astype(bf16)
    ck_ref[...]=dot_nt(buf_ref[5*a:6*a,:],spread)
    small_ref[:,:a]=buf_ref[5*a:5*a+16,:].astype(f32)
    small_ref[:,a:]=buf_ref[5*a+16:5*a+32,:].astype(f32)
    for x in backs:
        x.wait()

def unpack_b(meta, which, part, d, a, chunks, carry):
    sd=jax.ShapeDtypeStruct
    def kernel(meta_ref, part_ref, *refs):
        unpack_b_kernel(chunks,which,meta_ref,part_ref,*refs[-10:])
    carry=() if carry is None else tuple(carry)
    return pl.pallas_call(kernel,in_specs=[SM,ANYS]+[ANYS]*len(carry),out_specs=[ANYS]*5+[VM]*2,
        out_shape=[sd((d,a),f32)]*5+[sd((a,HEADS*TAPS),f32),sd((16,d),f32)],cost_estimate=cost(4.0),
        input_output_aliases={2+i:i for i in range(len(carry))},
        scratch_shapes=[pltpu.VMEM(part.shape,bf16),pltpu.SemaphoreType.DMA((chunks+5,)),pltpu.VMEM((5,a,a),f32)],
        compiler_params=pltpu.CompilerParams(vmem_limit_bytes=12*2**20),name="unpack_b")(meta,part,*carry)

class Reduce:
    def __init__(self, meta, keep, send, rows, scatter):
        self.meta=meta; self.rows=rows
        self.stages,self.whole=stage_bits(rows,scatter)
        self.keep=keep
        self.got=lax.ppermute(send,"seq",swap_pairs())
        self.step=0
        self.axes=("rows","seq")
    def advance(self):
        n=len(self.stages); w=len(self.whole); k=self.step; self.step+=1
        self.last=k==2*n+w
        if k<n:
            self.keep,send=fold(self.meta,k,self.keep,self.got)
            self.got=lax.ppermute(send,self.axes,row_pairs(self.rows,self.stages[k]))
        elif k<n+w:
            self.keep=add_low(self.keep,self.got)
            b=self.whole[k-n]
            self.got=lax.ppermute(self.keep,self.axes,row_pairs(self.rows,(b,b)))
        elif k==n+w+n+1:
            self.other=self.got
            self.got=None
        else:
            self.keep=add_low(self.keep,self.got) if k==n+w else jnp.concatenate([self.keep,self.got],axis=0)
            m=2*n+w-1-k
            if m>=0:
                self.got=lax.ppermute(self.keep,self.axes,row_pairs(self.rows,self.stages[m]))
            else:
                self.got=lax.ppermute(self.keep,"seq",swap_pairs())
    def after(self, arrays):
        self.got,arrays=lax.optimization_barrier((self.got,tuple(arrays)))
        self.advance()
        self.keep,arrays=lax.optimization_barrier((self.keep,arrays))
        return arrays
    def follow(self, other):
        self.got,other.keep=lax.optimization_barrier((self.got,other.keep))
        self.advance()
    def finish(self):
        while self.got is not None:
            self.advance()
        return self.keep,self.other,2**len(self.stages)

def per_device(hidden_in,doc_lengths,out_grad,w_query,w_key,w_value,w_conv_out,depth_kernel,w_point,w_conv_kernel,
               w_output,ln1_gain,ln1_bias,w_ffn_in,w_ffn_out,ln2_gain,ln2_bias):
    row_count,local,d=hidden_in.shape
    a=w_query.shape[1]
    half=local//2
    rows=lax.axis_size("rows")
    side=lax.axis_index("seq")
    row=lax.axis_index("rows")
    hid=hidden_in[0]
    meta=jnp.concatenate([make_meta(doc_lengths[0],side,local,local*2),comm_meta(side,row,rows)])
    halo=lax.ppermute(lax.dynamic_slice_in_dim(hid,(1-side)*half,half,0),"seq",swap_pairs())
    q,kw,vw,cx,depth,ck,kern,cm=pre(meta,hid,halo,w_query,w_key,w_value,w_conv_out,depth_kernel,w_point,w_conv_kernel)
    ctx,lse=attn_fwd(meta,q,kw,vw)
    ln=jnp.stack([ln1_gain,ln1_bias,ln2_gain,ln2_bias]).astype(f32)
    ho,dres,dctx,dconv,keep,send,gln=ffn(meta,hid,ctx,cm,out_grad[0],w_output,w_ffn_in,w_ffn_out,ln)
    g,gi,go=w_ffn_in.shape
    ra=Reduce(meta,keep,send,rows,3)
    carry=attn_bwd(meta,2,1,q,kw,vw,ctx,dctx,lse,None)
    out=ra.after(tuple(carry)+(dconv,))
    carry,dconv=out[:4],out[4]
    dqc,dc,dda,ddb,rimc,gp=conv_back(meta,dconv,cm,kern,cx,q,ck,depth,w_point,w_conv_kernel)
    rimc=lax.ppermute(rimc,"seq",swap_pairs())
    out=ra.after(tuple(carry)+(dqc,dda))
    carry,dqc,dda=out[:4],out[4],out[5]
    dqa,dk,dv,dkv=attn_bwd(meta,0,2,q,kw,vw,ctx,dctx,lse,carry)
    dkv=lax.ppermute(dkv,"seq",swap_pairs())
    dda,dqa=ra.after((dda,dqa))
    dha,rima,gta=taps_back(meta,0,hid,halo,dda,depth_kernel)
    ddb,dha=ra.after((ddb,dha))
    dhb,rimb,gtb=taps_back(meta,1,hid,halo,ddb,depth_kernel)
    rima=lax.ppermute(rima,"seq",swap_pairs())
    rimb=lax.ppermute(rimb,"seq",swap_pairs())
    dp,keep,send=proj_back(meta,hid,dqa,dqc,dk,dv,dkv,dc,rimc,gp,gta,gtb,gln)
    rb=Reduce(meta,keep,send,rows,3)
    grad_in=grad_input(meta,dp,dres,dha,dhb,rima,rimb,w_query,w_key,w_value,w_conv_out)
    (grad_in,)=rb.after((grad_in,))
    for one,two in ((rb,ra),(ra,rb),(rb,ra),(ra,rb),(rb,ra),(ra,rb),(rb,ra),(rb,ra),(ra,rb),(rb,ra),(ra,rb)):
        one.follow(two)
    mine,other,chunks=ra.finish()
    ffn_out_grad,ffn_in_grad,output_grad=unpack_a(meta,mine,other,g,gi,go,d,chunks)
    ffn_in_grad,ffn_out_grad,output_grad=rb.after((ffn_in_grad,ffn_out_grad,output_grad))
    while not rb.last:
        rb.advance()
    first=unpack_b(meta,0,rb.keep,d,a,chunks,None)
    first,got=lax.optimization_barrier((tuple(first),rb.got))
    second=unpack_b(meta,1,got,d,a,chunks,first[:5])
    q_grad,k_grad,v_grad,c_grad,point_grad=second[:5]
    ck_grad=jnp.where(side==0,first[5],second[5])
    small=jnp.where(side==1,first[6],second[6])
    lng=small[KSIZE:KSIZE+4]
    return (ho[None],grad_in[None],q_grad,k_grad,v_grad,c_grad,small[:KSIZE],point_grad,ck_grad,output_grad,
            lng[0],lng[1],ffn_in_grad,ffn_out_grad,lng[2],lng[3])


def solution(mesh):
    placed=(P("rows","seq",None),P("rows",None),P("rows","seq",None))+(P(),)*14
    return jax.shard_map(per_device,mesh=mesh,in_specs=placed,
        out_specs=(P("rows","seq",None),P("rows","seq",None))+(P(),)*14,check_vma=False)
```

```python
import jax
import jax.numpy as jnp
from jax import lax
from jax.experimental import pallas as pl
from jax.experimental.pallas import tpu as pltpu
from jax.sharding import PartitionSpec as P

KSIZE = 9

HEADS=6
BLK=256
NEG=-1e30
f32=jnp.float32; bf16=jnp.bfloat16

def dot_nt(a,b):
    return lax.dot_general(a,b,(((1,),(1,)),((),())),preferred_element_type=f32)
def dot_nn(a,b):
    return lax.dot_general(a,b,(((1,),(0,)),((),())),preferred_element_type=f32)
def dot_tn(a,b):
    return lax.dot_general(a,b,(((0,),(0,)),((),())),preferred_element_type=f32)

def segs(meta, first, shape):
    pos=first+lax.broadcasted_iota(jnp.int32,shape,0)
    seg=jnp.zeros(shape,jnp.int32)
    for d in range(5):
        seg=seg+jnp.where(pos>=meta[d],1,0)
    return seg

def key_ext(meta, first, n):
    lane=lax.broadcasted_iota(jnp.int32,(n,128),1)
    seg=segs(meta,first,(n,128))
    diff=(lane>=24)&(lane<30)&(lane-24!=seg)
    return jnp.where(lane<24,-1.0,jnp.where(diff,NEG,0.0)).astype(bf16)

def fwd_kernel(meta, q_ref, k_ref, v_ref, ctx_ref, lse_ref, kx_ref, s_ref, m_ref, acc_ref):
    nkb=k_ref.shape[0]//BLK; nqb=q_ref.shape[0]//BLK; npair=HEADS//2
    for b in range(nkb):
        kx_ref[b*BLK:(b+1)*BLK,:]=key_ext(meta,meta[5]+b*BLK,BLK)
    lane=lax.broadcasted_iota(jnp.int32,(BLK,128),1)
    ones_lane=jnp.where(lane==0,1.0,0.0).astype(bf16)
    for qb in range(nqb):
        qrows=slice(qb*BLK,(qb+1)*BLK)
        seg=segs(meta,meta[6]+qb*BLK,(BLK,128))
        qext=jnp.where(lane-24==seg,1.0,0.0).astype(bf16)
        lo=meta[8+2*qb]; hi=meta[9+2*qb]
        m_ref[...]=jnp.full(m_ref.shape,NEG,f32)
        acc_ref[...]=jnp.zeros(acc_ref.shape,f32)
        def phase1(kb,_):
            r0=pl.multiple_of(kb*BLK,BLK)
            kext=kx_ref[pl.ds(r0,BLK),:]
            for j in range(npair):
                kk=jnp.concatenate([k_ref[pl.ds(r0,BLK),j*128:(j+1)*128],kext],axis=1)
                qp=q_ref[qrows,j*128:(j+1)*128]*jnp.asarray(0.125,bf16)
                for hh in range(2):
                    h=2*j+hh
                    qm=jnp.where((lane<64) if hh==0 else (lane>=64),qp,jnp.zeros_like(qp))
                    s=dot_nt(jnp.concatenate([qm,qext],axis=1),kk)
                    s_ref[h,:,pl.ds(r0,BLK)]=s
                    m_ref[h]=jnp.maximum(m_ref[h],jnp.maximum(s[:,:128],s[:,128:]))
            return 0
        lax.fori_loop(lo,hi,phase1,0)
        for h in range(HEADS):
            m_ref[h]=jnp.broadcast_to(jnp.max(m_ref[h],axis=1,keepdims=True),(BLK,128))
        def phase2(kb,_):
            r0=pl.multiple_of(kb*BLK,BLK)
            for j in range(npair):
                vv=jnp.concatenate([v_ref[pl.ds(r0,BLK),j*128:(j+1)*128],ones_lane],axis=1)
                for hh in range(2):
                    h=2*j+hh
                    mm=m_ref[h]
                    p=jnp.exp(s_ref[h,:,pl.ds(r0,BLK)]-jnp.concatenate([mm,mm],axis=1)).astype(bf16)
                    acc_ref[h]=acc_ref[h]+dot_nn(p,vv)
            return 0
        lax.fori_loop(lo,hi,phase2,0)
        lse_all=jnp.zeros((BLK,128),f32)
        for j in range(npair):
            parts=[]
            for hh in range(2):
                h=2*j+hh
                l=jnp.broadcast_to(acc_ref[h][:,128:129],(BLK,128))
                parts.append(acc_ref[h][:,:128]/l)
                lse=m_ref[h]+jnp.log(l)
                sel=(lane==h)|(lane==h+8)|(lane==h+16)
                lse_all=jnp.where(sel,lse,lse_all)
            ctx_ref[qrows,j*128:(j+1)*128]=jnp.where(lane<64,parts[0],parts[1]).astype(ctx_ref.dtype)
        lse_ref[qrows,:]=lse_all

def bwd_kernel(head, meta, q_ref, k_ref, v_ref, ctx_ref, dctx_ref, lse_ref, dq_ref, dko_ref, dvo_ref, dkv_ref, kx_ref, dk_ref, dv_ref):
    nkb=k_ref.shape[0]//BLK; nqb=q_ref.shape[0]//BLK; npair=q_ref.shape[1]//128
    width=q_ref.shape[1]
    for b in range(nkb):
        kx_ref[b*BLK:(b+1)*BLK,:]=key_ext(meta,meta[5]+b*BLK,BLK)
    dk_ref[...]=jnp.zeros(dk_ref.shape,f32)
    dv_ref[...]=jnp.zeros(dv_ref.shape,f32)
    dq_ref[...]=jnp.zeros(dq_ref.shape,f32)
    lane=lax.broadcasted_iota(jnp.int32,(BLK,128),1)
    vext=jnp.where(lane<16,-1.0,0.0).astype(bf16)
    r=head+lax.broadcasted_iota(jnp.int32,(width,128),0)//64
    cl=lax.broadcasted_iota(jnp.int32,(width,128),1)
    heads_of=jnp.where((cl<16)&(cl%8==r),1.0,0.0).astype(bf16)
    low=lane<64
    for qb in range(nqb):
        qrows=slice(qb*BLK,(qb+1)*BLK)
        seg=segs(meta,meta[6]+qb*BLK,(BLK,128))
        onehot=lane-24==seg
        lse=lse_ref[qrows,:]
        hi_=lse.astype(bf16).astype(f32)
        r1=lse-hi_
        mid=r1.astype(bf16).astype(f32)
        lo_=r1-mid
        split=jnp.where(lane<8,hi_,jnp.where(lane<16,mid,lo_))
        prod=ctx_ref[qrows,:].astype(f32)*dctx_ref[qrows,:].astype(f32)
        ph=prod.astype(bf16)
        plo=(prod-ph.astype(f32)).astype(bf16)
        dd=dot_nn(ph,heads_of)+dot_nn(plo,heads_of)
        dh=dd.astype(bf16).astype(f32)
        dsplit=jnp.where(lane<8,dh,dd-dh)
        qx=[];dcx=[];qms=[];dcs=[]
        for h in range(head,head+2*npair):
            j=(h-head)//2
            side=low if h%2==0 else ~low
            qp=q_ref[qrows,j*128:(j+1)*128]*jnp.asarray(0.125,bf16)
            qm=jnp.where(side,qp,jnp.zeros_like(qp))
            sel=(lane==h)|(lane==h+8)|(lane==h+16)
            qe=jnp.where(sel,split,jnp.where(onehot,1.0,0.0)).astype(bf16)
            qx.append(jnp.concatenate([qm,qe],axis=1))
            dp=dctx_ref[qrows,j*128:(j+1)*128]
            dm=jnp.where(side,dp,jnp.zeros_like(dp))
            de=jnp.where((lane==h)|(lane==h+8),dsplit,0.0).astype(bf16)
            dcx.append(jnp.concatenate([dm,de],axis=1))
            qms.append(qm);dcs.append(dm)
        lo=meta[8+2*qb]; hi=meta[9+2*qb]
        def body(kb,_):
            r0=pl.multiple_of(kb*BLK,BLK)
            kext=kx_ref[pl.ds(r0,BLK),:]
            for j in range(npair):
                cols=slice(j*128,(j+1)*128)
                kp=k_ref[pl.ds(r0,BLK),cols]
                kk=jnp.concatenate([kp,kext],axis=1)
                vv=jnp.concatenate([v_ref[pl.ds(r0,BLK),cols],vext],axis=1)
                pts=[];dss=[];ks=[]
                for hh in range(2):
                    h=2*j+hh
                    pt=jnp.exp(dot_nt(kk,qx[h]))
                    dpt=dot_nt(vv,dcx[h])
                    pts.append(pt.astype(bf16))
                    dss.append((pt*dpt).astype(bf16))
                    ks.append(jnp.where(low if hh==0 else ~low,kp,jnp.zeros_like(kp)))
                dv_ref[pl.ds(r0,BLK),cols]+=dot_nn(jnp.concatenate(pts,axis=1),jnp.concatenate(dcs[2*j:2*j+2],axis=0))
                dk_ref[pl.ds(r0,BLK),cols]+=dot_nn(jnp.concatenate(dss,axis=1),jnp.concatenate(qms[2*j:2*j+2],axis=0))
                dq_ref[qrows,cols]+=dot_tn(jnp.concatenate(dss,axis=0),jnp.concatenate(ks,axis=0))
            return 0
        lax.fori_loop(lo,hi,body,0)
        dq_ref[qrows,:]=dq_ref[qrows,:]*0.125
    n=q_ref.shape[0]; half=dkv_ref.shape[0]
    own_off=meta[7]*half; halo_off=(1-meta[7])*n
    for b in range(n//BLK):
        src=pl.multiple_of(own_off+b*BLK,BLK)
        dko_ref[b*BLK:(b+1)*BLK,:]=dk_ref[pl.ds(src,BLK),:]
        dvo_ref[b*BLK:(b+1)*BLK,:]=dv_ref[pl.ds(src,BLK),:]
    for b in range(half//BLK):
        src=pl.multiple_of(halo_off+b*BLK,BLK)
        for j in range(npair):
            dkv_ref[b*BLK:(b+1)*BLK,j*256:j*256+128]=dk_ref[pl.ds(src,BLK),j*128:(j+1)*128].astype(bf16)
            dkv_ref[b*BLK:(b+1)*BLK,j*256+128:(j+1)*256]=dv_ref[pl.ds(src,BLK),j*128:(j+1)*128].astype(bf16)

VM=pl.BlockSpec(memory_space=pltpu.VMEM)
SM=pl.BlockSpec(memory_space=pltpu.SMEM)
def attn_fwd(meta,q,k,v):
    t,w=q.shape
    return pl.pallas_call(fwd_kernel,in_specs=[SM,VM,VM,VM],out_specs=[VM,VM],
        out_shape=[jax.ShapeDtypeStruct((t,w),bf16),jax.ShapeDtypeStruct((t,128),f32)],
        scratch_shapes=[pltpu.VMEM((k.shape[0],128),bf16),pltpu.VMEM((HEADS,BLK,k.shape[0]),f32),
            pltpu.VMEM((HEADS,BLK,128),f32),pltpu.VMEM((HEADS,BLK,256),f32)],
        compiler_params=pltpu.CompilerParams(vmem_limit_bytes=30*2**20),cost_estimate=cost(15.0),name="attn_fwd")(meta,q,k,v)
def attn_bwd(meta,first,pairs,q,k,v,ctx,dctx,lse,carry):
    t,w=q.shape; kn=k.shape[0]; wide=128*pairs
    sd=jax.ShapeDtypeStruct
    def col(n,width):
        return pl.BlockSpec((n,width),lambda i:(0,first//pairs))
    def kernel(*refs):
        bwd_kernel(2*first,*refs[:7],*refs[-7:])
    carry=() if carry is None else tuple(carry)
    return pl.pallas_call(kernel,grid=(1,),
        in_specs=[SM,col(t,wide),col(kn,wide),col(kn,wide),col(t,wide),col(t,wide),pl.BlockSpec((t,128),lambda i:(0,0))]+[pl.BlockSpec(memory_space=pl.ANY)]*len(carry),
        out_specs=[col(t,wide)]*3+[col(kn-t,2*wide)],
        out_shape=[sd((t,w),f32)]*3+[sd((kn-t,2*w),bf16)],
        scratch_shapes=[pltpu.VMEM((kn,128),bf16),pltpu.VMEM((kn,wide),f32),pltpu.VMEM((kn,wide),f32)],
        input_output_aliases={7+i:i for i in range(len(carry))},cost_estimate=cost(9.0*pairs),
        compiler_params=pltpu.CompilerParams(vmem_limit_bytes=(16+4*pairs)*2**20),name="attn_bwd")(meta,q,k,v,ctx,dctx,lse,*carry)

def make_meta(lengths, side, local, full):
    ends=jnp.cumsum(lengths)
    starts=ends-lengths
    win=side*(local//2); own=side*local
    nqb=local//BLK
    b0=own+jnp.arange(nqb)*BLK
    b1=b0+BLK-1
    bounds_lo=jnp.concatenate([jnp.zeros((1,),jnp.int32),ends])
    bounds_hi=jnp.concatenate([ends,jnp.full((1,),full,jnp.int32)])
    seg0=jnp.sum((b0[:,None]>=ends[None]).astype(jnp.int32),1)
    seg1=jnp.sum((b1[:,None]>=ends[None]).astype(jnp.int32),1)
    first=jnp.sum(jnp.where(jnp.arange(6)[None]==seg0[:,None],bounds_lo[None],0),1)
    last=jnp.sum(jnp.where(jnp.arange(6)[None]==seg1[:,None],bounds_hi[None],0),1)
    lo=jnp.maximum(first-win,0)//BLK
    hi=jnp.minimum((last-win+BLK-1)//BLK,(local+local//2)//BLK)
    return jnp.concatenate([ends,win[None],own[None],side[None],jnp.stack([lo,hi],1).reshape(-1)]).astype(jnp.int32)


TB=256

def gelu_parts(z):
    a=jnp.abs(z)
    t=1.0/(1.0+a*(0.3275911*0.7071067811865476))
    e=jnp.exp(-0.5*z*z)
    poly=t*(0.127414796+t*(-0.142248368+t*(0.7107068705+t*(-0.7265760135+t*0.5307027145))))
    ht=poly*e
    phi=jnp.where(z>=0.0,1.0-ht,ht)
    return z*phi, phi+z*(e*0.3989422804014327)

def rows8(x):
    return jnp.sum(x.reshape(x.shape[0]//8,8,x.shape[1]),axis=0)

def norm_parts(z):
    mu=jnp.mean(z,axis=-1,keepdims=True)
    c=z-mu
    var=jnp.mean(c*c,axis=-1,keepdims=True)
    rstd=lax.rsqrt(var+1e-6)
    return c*rstd, rstd

def norm_back(d, gain, xhat, rstd):
    dx=d*gain
    a=jnp.mean(dx,axis=-1,keepdims=True)
    b=jnp.mean(dx*xhat,axis=-1,keepdims=True)
    return rstd*(dx-a-xhat*b)

def ffn_kernel(meta, hid_ref, ctx_ref, cm_ref, og_ref, wo_ref, win_ref, wout_ref, ln_ref,
               ho_ref, dres_ref, dctx_ref, dconv_ref, keep_ref, send_ref, gln_ref,
               act_ref, dff_ref, x1_ref, dfo_ref, datt_ref, mix_ref):
    n=hid_ref.shape[0]; d=hid_ref.shape[1]; groups=win_ref.shape[0]; gi=d//groups; go=win_ref.shape[2]
    attn=dctx_ref.shape[1]
    tile=512
    gln_ref[...]=jnp.zeros(gln_ref.shape,f32)
    def block(i,_):
        r0=pl.multiple_of(i*TB,TB)
        rows=pl.ds(r0,TB)
        g1=ln_ref[0:1,:];b1=ln_ref[1:2,:];g2=ln_ref[2:3,:];b2=ln_ref[3:4,:]
        att=dot_nn(jnp.concatenate([ctx_ref[rows,:],cm_ref[rows,:]],axis=1),wo_ref[...])
        xhat1,rstd1=norm_parts(hid_ref[rows,:].astype(f32)+att)
        first=xhat1*g1+b1
        x1=first.astype(bf16)
        for g in range(groups):
            x1_ref[g,rows,:]=x1[:,g*gi:(g+1)*gi]
        mix_ref[0,rows,:]=ctx_ref[rows,:]
        mix_ref[1,rows,:]=cm_ref[rows,:]
        tiles=[(g,c) for g in range(groups) for c in range(go//tile)]
        def up(g,c):
            return dot_nn(x1[:,g*gi:(g+1)*gi],win_ref[g,:,c*tile:(c+1)*tile])
        outs=[None]*groups
        ahead=up(*tiles[0])
        for t,(g,c) in enumerate(tiles):
            z=ahead
            if t+1<len(tiles):
                ahead=up(*tiles[t+1])
            cols=slice(c*tile,(c+1)*tile)
            a,gp=gelu_parts(z)
            ab=a.astype(bf16)
            act_ref[g,rows,cols]=ab
            dff_ref[g,rows,cols]=gp.astype(bf16)
            o=dot_nn(ab,wout_ref[g,cols,:])
            outs[g]=o if outs[g] is None else outs[g]+o
        xhat2,rstd2=norm_parts(first+jnp.concatenate(outs,axis=1))
        pos=meta[6]+r0+lax.broadcasted_iota(jnp.int32,(TB,d),0)
        valid=pos<meta[4]
        ho_ref[rows,:]=jnp.where(valid,xhat2*g2+b2,0.0).astype(bf16)
        gn=jnp.where(valid,og_ref[rows,:].astype(f32),0.0)
        gln_ref[16:24,:]+=rows8(gn*xhat2)
        gln_ref[24:32,:]+=rows8(gn)
        dres2=norm_back(gn,g2,xhat2,rstd2)
        dfo=dres2.astype(bf16)
        for g in range(groups):
            dfo_ref[g,rows,:]=dfo[:,g*gi:(g+1)*gi]
        def down(g,c):
            return dot_nt(dfo[:,g*gi:(g+1)*gi],wout_ref[g,c*tile:(c+1)*tile,:])
        backs=[None]*groups
        ahead=down(*tiles[0])
        for t,(g,c) in enumerate(tiles):
            da=ahead
            if t+1<len(tiles):
                ahead=down(*tiles[t+1])
            cols=slice(c*tile,(c+1)*tile)
            dh=(da*dff_ref[g,rows,cols].astype(f32)).astype(bf16)
            dff_ref[g,rows,cols]=dh
            o=dot_nt(dh,win_ref[g,:,cols])
            backs[g]=o if backs[g] is None else backs[g]+o
        dfirst=dres2+jnp.concatenate(backs,axis=1)
        gln_ref[0:8,:]+=rows8(dfirst*xhat1)
        gln_ref[8:16,:]+=rows8(dfirst)
        dres1=norm_back(dfirst,g1,xhat1,rstd1)
        dres_ref[rows,:]=dres1
        datt=dres1.astype(bf16)
        datt_ref[rows,:]=datt
        dm=dot_nt(datt,wo_ref[...])
        dctx_ref[rows,:]=dm[:,:attn].astype(bf16)
        dconv_ref[rows,:]=dm[:,attn:]
        return 0
    lax.fori_loop(0,n//TB,block,0)
    side=meta[7]
    for ref,g in ((send_ref,1-side),(keep_ref,side)):
        at=0
        for c in range(go//gi):
            ref[at*gi:(at+1)*gi,:]=dot_tn(act_ref[g,:,c*gi:(c+1)*gi],dfo_ref[g]).astype(ref.dtype)
            at+=1
        wide=dot_tn(x1_ref[g],dff_ref[g]).astype(ref.dtype)
        for c in range(go//gi):
            ref[at*gi:(at+1)*gi,:]=wide[:,c*gi:(c+1)*gi]
            at+=1
        for c in range(d//attn):
            ref[at*gi:(at+1)*gi,:]=dot_tn(mix_ref[g],datt_ref[:,c*attn:(c+1)*attn]).astype(ref.dtype)
            at+=1

def ffn(meta,hid,ctx,cm,og,wo,win,wout,ln):
    n,d=hid.shape; g,gi,go=win.shape; attn=ctx.shape[1]
    sd=jax.ShapeDtypeStruct
    return pl.pallas_call(ffn_kernel,in_specs=[SM]+[VM]*8,out_specs=[VM]*7,
        out_shape=[sd((n,d),bf16),sd((n,d),f32),sd((n,attn),bf16),sd((n,attn),f32),
                   sd((2*go+d,attn),bf16),sd((2*go+d,attn),bf16),sd((32,d),f32)],
        scratch_shapes=[pltpu.VMEM((g,n,go),bf16),pltpu.VMEM((g,n,go),bf16),pltpu.VMEM((g,n,gi),bf16),
                        pltpu.VMEM((g,n,gi),bf16),pltpu.VMEM((n,d),bf16),pltpu.VMEM((2,n,attn),bf16)],
        cost_estimate=cost(40.0),compiler_params=pltpu.CompilerParams(vmem_limit_bytes=40*2**20),name="ffn")(meta,hid,ctx,cm,og,wo,win,wout,ln)

TAPS=9
HALF=4
PAD=8
TB=256
CH=64
CS=32
LAST=128

def doc_bounds(meta, first, shape):
    pos=first+lax.broadcasted_iota(jnp.int32,shape,0)
    nxt=jnp.full(shape,2**30,jnp.int32)
    prv=jnp.full(shape,-2**30,jnp.int32)
    for d in range(5):
        e=meta[d]
        nxt=jnp.minimum(nxt,jnp.where(e>pos,e,2**30))
        prv=jnp.maximum(prv,jnp.where(e<=pos,e,-2**30))
    return nxt-pos, pos-prv

def tap_mask(bounds, o):
    rem,age=bounds
    if o>HALF:
        return rem>(o-HALF)
    return age>=(HALF-o)

def masked(x, bounds, o):
    if o==HALF:
        return x
    return jnp.where(tap_mask(bounds,o),x,0.0)

def tap_onehot(rows, cols, o):
    r=lax.broadcasted_iota(jnp.int32,(rows,cols),0)
    c=lax.broadcasted_iota(jnp.int32,(rows,cols),1)
    return jnp.where(r==(c//64)*TAPS+o,1.0,0.0).astype(bf16)

def pre_kernel(meta, hid_ref, halo_ref, wq_ref, wk_ref, wv_ref, wc_ref, taps_ref, wp_ref, wck_ref,
               q_ref, kw_ref, vw_ref, cx_ref, depth_ref, ck_ref, kern_hbm, cm_ref,
               hx_ref, wx_ref, lx_ref, kern_ref, sems):
    n,d=hid_ref.shape; half=halo_ref.shape[0]; attn=q_ref.shape[1]
    side=meta[7]
    own_off=side*half; halo_off=(1-side)*n
    jt=attn//128; jd=d//128
    for o in range(TAPS):
        wx_ref[:,o*attn:(o+1)*attn]=dot_nn(wck_ref[...],tap_onehot(HEADS*TAPS,attn,o)).astype(bf16)
    left=jnp.where(side==1,halo_ref[half-16:half,:].astype(f32),0.0)
    right=jnp.where(side==0,halo_ref[0:16,:].astype(f32),0.0)
    rims=jnp.concatenate([left,right],axis=0).astype(bf16)
    crim=dot_nn(rims,wc_ref[...]).astype(bf16).astype(f32)
    for j in range(jd):
        hx_ref[j,0:PAD,:]=left[PAD:2*PAD,j*128:(j+1)*128]
        hx_ref[j,n+PAD:n+2*PAD,:]=right[0:PAD,j*128:(j+1)*128]
    for j in range(jt):
        cx_ref[j,0:PAD,:]=crim[PAD:2*PAD,j*128:(j+1)*128]
        cx_ref[j,n+PAD:n+2*PAD,:]=crim[16:16+PAD,j*128:(j+1)*128]
    def project(i,_):
        r0=pl.multiple_of(i*TB,TB)
        x=hid_ref[pl.ds(r0,TB),:]
        q_ref[pl.ds(r0,TB),:]=dot_nn(x,wq_ref[...]).astype(bf16)
        ow=pl.multiple_of(own_off+r0,TB)
        kw_ref[pl.ds(ow,TB),:]=dot_nn(x,wk_ref[...]).astype(bf16)
        vw_ref[pl.ds(ow,TB),:]=dot_nn(x,wv_ref[...]).astype(bf16)
        c=dot_nn(x,wc_ref[...]).astype(bf16).astype(f32)
        rp=pl.multiple_of(r0+PAD,PAD)
        for j in range(jt):
            cx_ref[j,pl.ds(rp,TB),:]=c[:,j*128:(j+1)*128]
        xf=x.astype(f32)
        for j in range(jd):
            hx_ref[j,pl.ds(rp,TB),:]=xf[:,j*128:(j+1)*128]
        return 0
    lax.fori_loop(0,n//TB,project,0)
    def project_halo(i,_):
        r0=pl.multiple_of(i*TB,TB)
        x=halo_ref[pl.ds(r0,TB),:]
        ow=pl.multiple_of(halo_off+r0,TB)
        kw_ref[pl.ds(ow,TB),:]=dot_nn(x,wk_ref[...]).astype(bf16)
        vw_ref[pl.ds(ow,TB),:]=dot_nn(x,wv_ref[...]).astype(bf16)
        return 0
    lax.fori_loop(0,half//TB,project_halo,0)
    def depthwise(i,_):
        r0=pl.multiple_of(i*CH,CH)
        bounds=doc_bounds(meta,meta[6]+r0,(CH,128))
        for j in range(jd):
            acc=None
            for o in range(TAPS):
                x=hx_ref[j,pl.ds(r0+PAD+o-HALF,CH),:]
                term=masked(x*taps_ref[o:o+1,j*128:(j+1)*128].astype(f32),bounds,o)
                acc=term if acc is None else acc+term
            depth_ref[pl.ds(r0,CH),j*128:(j+1)*128]=acc.astype(bf16)
        return 0
    lax.fori_loop(0,n//CH,depthwise,0)
    def dynamic(r0):
        ck=dot_nn(depth_ref[pl.ds(r0,TB),:],wp_ref[...])
        ck_ref[pl.ds(r0,TB),:]=ck
        mk=(ck*q_ref[pl.ds(r0,TB),:].astype(f32)).astype(bf16)
        for o in range(TAPS):
            lx_ref[o]=dot_nn(mk,wx_ref[:,o*attn:(o+1)*attn])
        def soft(s,_):
            s0=pl.multiple_of(s*CS,CS)
            rows=pl.ds(s0,CS)
            t0=pl.multiple_of(r0+s0,CS)
            bounds=doc_bounds(meta,meta[6]+t0,(CS,128))
            for j in range(jt):
                cols=slice(j*128,(j+1)*128)
                ls=[lx_ref[o,rows,cols] for o in range(TAPS)]
                m=ls[0]
                for o in range(1,TAPS):
                    m=jnp.maximum(m,ls[o])
                es=[jnp.exp(l-m) for l in ls]
                tot=es[0]
                for o in range(1,TAPS):
                    tot=tot+es[o]
                inv=1.0/tot
                acc=None
                for o in range(TAPS):
                    k=es[o]*inv
                    kern_ref[o,pl.ds(t0,CS),cols]=k.astype(bf16)
                    term=masked(k*cx_ref[j,pl.ds(t0+PAD+o-HALF,CS),:],bounds,o)
                    acc=term if acc is None else acc+term
                cm_ref[pl.ds(t0,CS),cols]=acc.astype(bf16)
            return 0
        lax.fori_loop(0,TB//CS,soft,0)
    stores=[]
    for b in range(n//TB):
        dynamic(b*TB)
        x=pltpu.make_async_copy(kern_ref.at[:,pl.ds(b*TB,TB),:],kern_hbm.at[:,pl.ds(b*TB,TB),:],sems.at[b])
        x.start()
        stores.append(x)
    for x in stores:
        x.wait()

def pre(meta,hid,halo,wq,wk,wv,wc,taps,wp,wck):
    n,d=hid.shape; half=halo.shape[0]; a=wq.shape[1]; sd=jax.ShapeDtypeStruct
    anys=pl.BlockSpec(memory_space=pl.ANY)
    def whole(*shape):
        return pl.BlockSpec(shape,lambda i:(0,)*len(shape))
    proj=whole(d,a)
    return pl.pallas_call(pre_kernel,grid=(1,),in_specs=[SM,whole(n,d),VM,proj,proj,proj,proj,VM,proj,VM],out_specs=[VM]*6+[anys,VM],
        out_shape=[sd((n,a),bf16),sd((n+half,a),bf16),sd((n+half,a),bf16),sd((a//128,n+2*PAD,128),f32),
                   sd((n,d),bf16),sd((n,a),f32),sd((TAPS,n,a),bf16),sd((n,a),bf16)],
        scratch_shapes=[pltpu.VMEM((d//128,n+2*PAD,128),f32),pltpu.VMEM((a,TAPS*a),bf16),pltpu.VMEM((TAPS,TB,a),f32),
                        pltpu.VMEM((TAPS,n,a),bf16),pltpu.SemaphoreType.DMA((n//TB,))],
        cost_estimate=cost(30.0),compiler_params=pltpu.CompilerParams(vmem_limit_bytes=40*2**20),name="pre")(meta,hid,halo,wq,wk,wv,wc,taps,wp,wck)

def conv_back_kernel(meta, dconv_ref, cm_ref, kern_ref, cx_ref, q_ref, ck_ref, depth_ref,
                     wp_ref, wck_ref,
                     dqc_ref, dc_ref, dda_ref, ddb_ref, rimc_ref, gp_ref,
                     p_ref, pr_ref, dlc_ref, mk_ref, dck_ref, wcx_ref, dep_ref):
    d=depth_ref.shape[1]; attn,n=q_ref.shape[1],dc_ref.shape[0]
    i=pl.program_id(0)
    side=meta[7]; jt=attn//128; jd=d//128; hd=jd//2
    dds=[(dda_ref,j) if j<hd else (ddb_ref,j-hd) for j in range(jd)]
    @pl.when(i==0)
    def _():
        zero=jnp.zeros((2*PAD,128),f32)
        for j in range(jt):
            for o in range(TAPS):
                p_ref[o,j,0:2*PAD,:]=zero
                p_ref[o,j,n+2*PAD:n+4*PAD,:]=zero
        for ref,j in dds:
            ref[j,0:2*PAD,:]=zero
            ref[j,n+2*PAD:n+4*PAD,:]=zero
        r=lax.broadcasted_iota(jnp.int32,(HEADS*TAPS,attn),0)
        c=lax.broadcasted_iota(jnp.int32,(HEADS*TAPS,attn),1)
        spread=jnp.where((c%64<TAPS)&(r==(c//64)*TAPS+c%64),1.0,0.0).astype(bf16)
        wcx_ref[...]=dot_nn(wck_ref[...],spread).astype(bf16)
    def ones_block(w):
        return jnp.where(lax.broadcasted_iota(jnp.int32,(w,w),0)//64==lax.broadcasted_iota(jnp.int32,(w,w),1)//64,1.0,0.0).astype(bf16)
    ones256=ones_block(256); ones128=ones_block(128)
    lane=lax.broadcasted_iota(jnp.int32,(TB,attn),1)%64
    def dynamic():
        r0=pl.multiple_of(i*TB,TB)
        rows=pl.ds(r0,TB)
        def products(s,_):
            s0=pl.multiple_of(s*CS,CS)
            t0=pl.multiple_of(r0+s0,CS)
            bounds=doc_bounds(meta,meta[6]+t0,(CS,128))
            for j in range(jt):
                cols=slice(j*128,(j+1)*128)
                g=dconv_ref[pl.ds(s0,CS),cols]
                cm=cm_ref[pl.ds(s0,CS),cols].astype(f32)
                for o in range(TAPS):
                    cs=masked(cx_ref[j,pl.ds(t0+PAD+o-HALF,CS),:],bounds,o)
                    pr_ref[o,pl.ds(s0,CS),cols]=(g*(cs-cm)).astype(bf16)
                    p_ref[o,j,pl.ds(t0+2*PAD,CS),:]=masked(kern_ref[o,pl.ds(s0,CS),cols].astype(f32)*g,bounds,o)
            return 0
        lax.fori_loop(0,TB//CS,products,0)
        dl=jnp.zeros((TB,attn),f32)
        for o in range(TAPS):
            pr=pr_ref[o]
            dk=jnp.concatenate([dot_nn(pr[:,:256],ones256),dot_nn(pr[:,256:],ones128)],axis=1)
            dl=jnp.where(lane==o,kern_ref[o].astype(f32)*dk,dl)
        dlb=dl.astype(bf16)
        dlc_ref[rows,:]=dlb
        dmk=dot_nt(dlb,wcx_ref[...])
        dep_ref[rows,:]=depth_ref[...]
        q=q_ref[...].astype(f32)
        ck=ck_ref[...]
        mk_ref[rows,:]=(ck*q).astype(bf16)
        dqc_ref[...]=dmk*ck
        dck=(dmk*q).astype(bf16)
        dck_ref[rows,:]=dck
        dd=dot_nt(dck,wp_ref[...])
        rp=pl.multiple_of(r0+2*PAD,PAD)
        for j in range(jd):
            dds[j][0][dds[j][1],pl.ds(rp,TB),:]=dd[:,j*128:(j+1)*128]
    dynamic()
    @pl.when(i==pl.num_programs(0)-1)
    def _():
        def gather_c(row, size):
            out=[]
            for j in range(jt):
                acc=None
                for o in range(TAPS):
                    x=p_ref[o,j,pl.ds(row+PAD+HALF-o,size),:]
                    acc=x if acc is None else acc+x
                out.append(acc)
            return out
        def own_c(i,_):
            r0=pl.multiple_of(i*CS,CS)
            out=gather_c(r0+PAD,CS)
            for j in range(jt):
                dc_ref[pl.ds(r0,CS),j*128:(j+1)*128]=out[j]
            return 0
        lax.fori_loop(0,n//CS,own_c,0)
        left=gather_c(0,PAD); right=gather_c(n+PAD,PAD)
        for j in range(jt):
            rimc_ref[:,j*128:(j+1)*128]=jnp.where(side==1,left[j],right[j])
        for b in range(d//attn):
            gp_ref[b]=dot_tn(dep_ref[:,b*attn:(b+1)*attn],dck_ref[...]).astype(gp_ref.dtype)
        gp_ref[d//attn]=dot_tn(dlc_ref[...],mk_ref[...]).astype(gp_ref.dtype)

def taps_back_kernel(meta, hid_ref, halo_ref, dd_ref, taps_ref, dh_ref, rim_ref, gtap_ref):
    n,d=hid_ref.shape; half=halo_ref.shape[0]
    side=meta[7]; jd=d//128
    def gather_h(row, size, j, hx, bounds, sums):
        acc=None; new=[]
        for o in range(TAPS):
            x=masked(dd_ref[j,pl.ds(row+PAD+o-HALF,size),:],bounds,o)
            b=TAPS-1-o
            term=x*taps_ref[b:b+1,j*128:(j+1)*128].astype(f32)
            acc=term if acc is None else acc+term
            new.append(jnp.sum((x*hx).reshape(size//8,8,128),axis=0))
        return acc,[s+t for s,t in zip(sums,new)]
    lhalo=jnp.where(side==1,halo_ref[half-16:half,:].astype(f32),0.0)[PAD:2*PAD,:]
    rhalo=jnp.where(side==0,halo_ref[0:16,:].astype(f32),0.0)[0:PAD,:]
    for j in range(jd):
        cols=slice(j*128,(j+1)*128)
        sums=[jnp.zeros((8,128),f32) for _ in range(TAPS)]
        la,sums=gather_h(0,PAD,j,lhalo[:,cols],doc_bounds(meta,meta[6]-PAD,(PAD,128)),sums)
        ra,sums=gather_h(n+PAD,PAD,j,rhalo[:,cols],doc_bounds(meta,meta[6]+n,(PAD,128)),sums)
        rim_ref[:,cols]=jnp.where(side==1,la,ra)
        def own_h(i,sums):
            r0=pl.multiple_of(i*CS,CS)
            acc,sums=gather_h(r0+PAD,CS,j,hid_ref[pl.ds(r0,CS),cols].astype(f32),doc_bounds(meta,meta[6]+r0,(CS,128)),sums)
            dh_ref[pl.ds(r0,CS),cols]=acc
            return sums
        sums=lax.fori_loop(0,n//CS,own_h,sums)
        for o in range(TAPS):
            b=TAPS-1-o
            gtap_ref[b*8:(b+1)*8,cols]=sums[o]

def conv_back(meta,dconv,cm,kern,cx,q,ck,depth,wp,wck):
    n,d=depth.shape; a=q.shape[1]; sd=jax.ShapeDtypeStruct
    def row(w):
        return pl.BlockSpec((TB,w),lambda i:(i,0))
    def whole(*shape):
        return pl.BlockSpec(shape,lambda i:(0,)*len(shape))
    half=(d//256,n+4*PAD,128)
    return pl.pallas_call(conv_back_kernel,grid=(n//TB,),
        in_specs=[SM,row(a),row(a),pl.BlockSpec((TAPS,TB,a),lambda i:(0,i,0)),VM,row(a),row(a),row(d),VM,VM],
        out_specs=[row(a),whole(n,a),whole(*half),whole(*half),whole(PAD,a),whole(d//a+1,a,a)],
        out_shape=[sd((n,a),f32),sd((n,a),f32),sd(half,f32),sd(half,f32),sd((PAD,a),f32),sd((d//a+1,a,a),bf16)],
        scratch_shapes=[pltpu.VMEM((TAPS,a//128,n+4*PAD,128),f32),pltpu.VMEM((TAPS,TB,a),bf16),
                        pltpu.VMEM((n,a),bf16),pltpu.VMEM((n,a),bf16),pltpu.VMEM((n,a),bf16),pltpu.VMEM((a,a),bf16),pltpu.VMEM((n,d),bf16)],
        cost_estimate=cost(20.0),compiler_params=pltpu.CompilerParams(vmem_limit_bytes=48*2**20),name="conv_back")(meta,dconv,cm,kern,cx,q,ck,depth,wp,wck)

def taps_back(meta,part,hid,halo,dd,taps):
    n=hid.shape[0]; d=dd.shape[0]*128; sd=jax.ShapeDtypeStruct
    def col(rows):
        return pl.BlockSpec((rows,d),lambda i:(0,part))
    def whole(*shape):
        return pl.BlockSpec(shape,lambda i:(0,)*len(shape))
    return pl.pallas_call(taps_back_kernel,grid=(1,),in_specs=[SM,col(n),col(halo.shape[0]),whole(*dd.shape),col(TAPS)],
        out_specs=[whole(n,d),whole(PAD,d),whole(TAPS*8,d)],
        out_shape=[sd((n,d),f32),sd((PAD,d),f32),sd((TAPS*8,d),f32)],
        cost_estimate=cost(6.0),compiler_params=pltpu.CompilerParams(vmem_limit_bytes=24*2**20),name="taps_back")(meta,hid,halo,dd,taps)

def proj_back_kernel(meta, hid_ref, dqa_ref, dqc_ref, dk_ref, dv_ref, dkv_ref, dc_ref, rimc_ref, gp_ref, gta_ref, gtb_ref, gln_ref,
                     dp_ref, keep_ref, send_ref):
    n,d=hid_ref.shape; attn=dqa_ref.shape[1]; half=dkv_ref.shape[0]
    side=meta[7]
    shift=(1-side)*half
    def block(i,_):
        r0=pl.multiple_of(i*TB,TB)
        rows=pl.ds(r0,TB)
        inside=(r0>=shift)&(r0<shift+half)
        scale=jnp.where(inside,1.0,0.0)
        hr=pl.multiple_of(jnp.where(inside,r0-shift,0),TB)
        other=dkv_ref[pl.ds(hr,TB),:].astype(f32)*scale
        top=jnp.where((side==1)&(i==0),rimc_ref[...],0.0)
        bottom=jnp.where((side==0)&(i==n//TB-1),rimc_ref[...],0.0)
        rim=jnp.concatenate([top,jnp.zeros((TB-2*PAD,attn),f32),bottom],axis=0)
        dp_ref[rows,0:attn]=(dqa_ref[rows,:]+dqc_ref[rows,:]).astype(bf16)
        for j in range(attn//128):
            cols=slice(j*128,(j+1)*128)
            dp_ref[rows,attn+j*128:attn+(j+1)*128]=(dk_ref[rows,cols]+other[:,j*256:j*256+128]).astype(bf16)
            dp_ref[rows,2*attn+j*128:2*attn+(j+1)*128]=(dv_ref[rows,cols]+other[:,j*256+128:(j+1)*256]).astype(bf16)
        dp_ref[rows,3*attn:]=(dc_ref[rows,:]+rim).astype(bf16)
        return 0
    lax.fori_loop(0,n//TB,block,0)
    zeros=jnp.zeros((1,d),f32)
    small=[jnp.concatenate([jnp.sum(t[o*8:(o+1)*8,:],axis=0,keepdims=True) for t in (gta_ref,gtb_ref)],axis=1) for o in range(TAPS)]
    small+=[jnp.sum(gln_ref[k*8:(k+1)*8,:],axis=0,keepdims=True) for k in range(4)]
    small=jnp.concatenate(small+[zeros]*(16-len(small)),axis=0)
    for ref,h in ((send_ref,1-side),(keep_ref,side)):
        hc=pl.ds(pl.multiple_of(h*attn,128),attn)
        for k in range(4):
            ref[k*attn:(k+1)*attn,:]=dot_tn(hid_ref[:,hc],dp_ref[:,k*attn:(k+1)*attn]).astype(ref.dtype)
        ref[4*attn:5*attn,:]=gp_ref[h]
        @pl.when(h==0)
        def _():
            for k in range(HEADS):
                ref[5*attn+16*k:5*attn+16*(k+1),:]=gp_ref[2,64*k:64*k+16,:]
            ref[5*attn+16*HEADS:5*attn+LAST,:]=jnp.zeros((LAST-16*HEADS,attn),bf16)
        @pl.when(h==1)
        def _():
            ref[5*attn:5*attn+16,:]=small[:,:attn].astype(bf16)
            ref[5*attn+16:5*attn+32,:]=small[:,attn:].astype(bf16)
            ref[5*attn+32:5*attn+LAST,:]=jnp.zeros((LAST-32,attn),bf16)

def proj_back(meta,hid,dqa,dqc,dk,dv,dkv,dc,rimc,gp,gta,gtb,gln):
    n,d=hid.shape; a=dqa.shape[1]; sd=jax.ShapeDtypeStruct
    return pl.pallas_call(proj_back_kernel,in_specs=[SM]+[VM]*12,out_specs=[VM]*3,
        out_shape=[sd((n,4*a),bf16),sd((5*a+LAST,a),bf16),sd((5*a+LAST,a),bf16)],cost_estimate=cost(9.0),
        compiler_params=pltpu.CompilerParams(vmem_limit_bytes=16*2**20),name="proj_back")(meta,hid,dqa,dqc,dk,dv,dkv,dc,rimc,gp,gta,gtb,gln)

def grad_in_kernel(meta, dp_ref, dres_ref, dha_ref, dhb_ref, rima_ref, rimb_ref, wq_ref, wk_ref, wv_ref, wc_ref, gi_ref):
    n,d=gi_ref.shape; attn=wq_ref.shape[1]
    side=meta[7]
    def block(i,_):
        r0=pl.multiple_of(i*TB,TB)
        rows=pl.ds(r0,TB)
        acc=dres_ref[rows,:]+jnp.concatenate([dha_ref[rows,:],dhb_ref[rows,:]],axis=1)
        for k,w in enumerate((wq_ref,wk_ref,wv_ref,wc_ref)):
            acc=acc+dot_nt(dp_ref[rows,k*attn:(k+1)*attn],w[...])
        gi_ref[rows,:]=acc
        return 0
    lax.fori_loop(0,n//TB,block,0)
    at=pl.multiple_of((1-side)*(n-PAD),PAD)
    gi_ref[pl.ds(at,PAD),:]+=jnp.concatenate([rima_ref[...],rimb_ref[...]],axis=1)

def grad_input(meta,dp,dres,dha,dhb,rima,rimb,wq,wk,wv,wc):
    n,d=dres.shape; sd=jax.ShapeDtypeStruct
    return pl.pallas_call(grad_in_kernel,in_specs=[SM]+[VM]*10,out_specs=VM,
        out_shape=sd((n,d),f32),cost_estimate=cost(9.0),
        compiler_params=pltpu.CompilerParams(vmem_limit_bytes=16*2**20),name="grad_input")(meta,dp,dres,dha,dhb,rima,rimb,wq,wk,wv,wc)

AT=16

def swap_pairs():
    return [(0,1),(1,0)]

def stage_bits(size, scatter):
    bits=[]
    b=1
    while b<size:
        bits.append(b)
        b*=2
    lead=bits[:3]
    other=lead[-1:]+lead[:-1]+bits[3:]
    n=min(scatter,len(bits))
    return list(zip(bits,other))[:n],bits[n:]

def row_pairs(rows, bits):
    return [(r*2+s,(r^bits[s])*2+s) for r in range(rows) for s in range(2)]

def comm_meta(side, row, rows):
    stages,_=stage_bits(rows,4)
    own=[jnp.where(side==0,(row//b0)%2,(row//b1)%2) for b0,b1 in stages]
    oth=[jnp.where(side==0,(row//b1)%2,(row//b0)%2) for b0,b1 in stages]
    c=jnp.int32(0); c2=jnp.int32(0)
    for u,v in list(zip(own,oth))[:3]:
        c=c*2+u; c2=c2*2+v
    own=own+[jnp.int32(0)]*(4-len(own))
    return jnp.stack(own+[c,c2]).astype(jnp.int32)

def cost(us):
    return pl.CostEstimate(flops=int(us*1.0e9),bytes_accessed=0,transcendentals=0)

def fold_kernel(stage, meta, keep_ref, got_ref, k_ref, s_ref):
    h=k_ref.shape[0]; ch=64 if k_ref.shape[0]%64==0 else 48
    b=meta[AT+stage]
    def body(i,_):
        r=pl.multiple_of(i*ch,16)
        for ref,at in ((k_ref,b*h),(s_ref,(1-b)*h)):
            src=pl.multiple_of(at+r,16)
            ref[pl.ds(r,ch),:]=(keep_ref[pl.ds(src,ch),:].astype(f32)+got_ref[pl.ds(src,ch),:].astype(f32)).astype(bf16)
        return 0
    lax.fori_loop(0,h//ch,body,0)

def fold(meta, stage, keep, got):
    h=keep.shape[0]//2; sd=jax.ShapeDtypeStruct((h,keep.shape[1]),keep.dtype)
    def kernel(meta_ref, keep_ref, got_ref, k_ref, s_ref):
        fold_kernel(stage, meta_ref, keep_ref, got_ref, k_ref, s_ref)
    return pl.pallas_call(kernel,in_specs=[SM,VM,VM],out_specs=[VM,VM],out_shape=[sd,sd],cost_estimate=cost(1.0),
        compiler_params=pltpu.CompilerParams(vmem_limit_bytes=16*2**20),name="fold")(meta,keep,got)

def add_low(x,y):
    return (x.astype(f32)+y.astype(f32)).astype(bf16)

def place(meta, mine_ref, other_ref, buf_ref, sems, chunks):
    side=meta[7]
    rows=mine_ref.shape[0]//chunks
    copies=[]
    for i in range(chunks):
        for k,ref in enumerate((mine_ref,other_ref)):
            half=side if k==0 else 1-side
            at=lax.bitwise_xor(meta[AT+4+k],jnp.int32(i))
            copies.append(pltpu.make_async_copy(ref.at[pl.ds(i*rows,rows),:],
                buf_ref.at[half,pl.ds(pl.multiple_of(at*rows,16),rows),:],sems.at[i,k]))
    for c in copies:
        c.start()
    for c in copies:
        c.wait()

def unpack_a_kernel(chunks, meta, mine_ref, other_ref, gout_ref, gin_ref, gwo_ref, buf_ref, sems):
    place(meta,mine_ref,other_ref,buf_ref,sems,chunks)
    a=buf_ref.shape[2]; g,go,_=gout_ref.shape; ch=128
    per=go//a
    def body(i,_):
        r=pl.multiple_of(i*ch,ch)
        for h in range(g):
            for c in range(per):
                gout_ref[h,pl.ds(pl.multiple_of(c*a+r,ch),ch),:]=buf_ref[h,pl.ds(pl.multiple_of(c*a+r,ch),ch),:].astype(f32)
                gin_ref[h,pl.ds(r,ch),c*a:(c+1)*a]=buf_ref[h,pl.ds(pl.multiple_of((per+c)*a+r,ch),ch),:].astype(f32)
            for c in range(gwo_ref.shape[1]//a):
                gwo_ref[pl.ds(pl.multiple_of(h*a+r,ch),ch),c*a:(c+1)*a]=buf_ref[h,pl.ds(pl.multiple_of((2*per+c)*a+r,ch),ch),:].astype(f32)
        return 0
    lax.fori_loop(0,a//ch,body,0)

ANYS=pl.BlockSpec(memory_space=pl.ANY)
def unpack_a(meta, mine, other, g, gi, go, d, chunks):
    sd=jax.ShapeDtypeStruct
    def kernel(*refs):
        unpack_a_kernel(chunks,*refs)
    return pl.pallas_call(kernel,in_specs=[SM,ANYS,ANYS],out_specs=[VM]*3,
        out_shape=[sd((g,go,gi),f32),sd((g,gi,go),f32),sd((d,d),f32)],cost_estimate=cost(8.0),
        scratch_shapes=[pltpu.VMEM((2,)+mine.shape,bf16),pltpu.SemaphoreType.DMA((chunks,2))],
        compiler_params=pltpu.CompilerParams(vmem_limit_bytes=20*2**20),name="unpack_a")(meta,mine,other)

def unpack_b_kernel(chunks, which, meta, part_ref, q_ref, k_ref, v_ref, c_ref, p_ref, ck_ref, small_ref, buf_ref, sems, outs):
    a=buf_ref.shape[1]; rows=part_ref.shape[0]//chunks
    h=meta[7] if which==0 else 1-meta[7]
    copies=[]
    for i in range(chunks):
        at=lax.bitwise_xor(meta[AT+4+which],jnp.int32(i))
        copies.append(pltpu.make_async_copy(part_ref.at[pl.ds(i*rows,rows),:],
            buf_ref.at[pl.ds(pl.multiple_of(at*rows,16),rows),:],sems.at[i]))
    for x in copies:
        x.start()
    for x in copies:
        x.wait()
    backs=[]
    for i,ref in enumerate((q_ref,k_ref,v_ref,c_ref,p_ref)):
        outs[i]=buf_ref[i*a:(i+1)*a,:].astype(f32)
        x=pltpu.make_async_copy(outs.at[i],ref.at[pl.ds(pl.multiple_of(h*a,128),a),:],sems.at[chunks+i])
        x.start()
        backs.append(x)
    r=lax.broadcasted_iota(jnp.int32,(LAST,HEADS*TAPS),0)
    c=lax.broadcasted_iota(jnp.int32,(LAST,HEADS*TAPS),1)
    spread=jnp.where(r==(c//TAPS)*16+c%TAPS,1.0,0.0).astype(bf16)
    ck_ref[...]=dot_tn(buf_ref[5*a:5*a+LAST,:],spread)
    small_ref[:,:a]=buf_ref[5*a:5*a+16,:].astype(f32)
    small_ref[:,a:]=buf_ref[5*a+16:5*a+32,:].astype(f32)
    for x in backs:
        x.wait()

def unpack_b(meta, which, part, d, a, chunks, carry):
    sd=jax.ShapeDtypeStruct
    def kernel(meta_ref, part_ref, *refs):
        unpack_b_kernel(chunks,which,meta_ref,part_ref,*refs[-10:])
    carry=() if carry is None else tuple(carry)
    return pl.pallas_call(kernel,in_specs=[SM,ANYS]+[ANYS]*len(carry),out_specs=[ANYS]*5+[VM]*2,
        out_shape=[sd((d,a),f32)]*5+[sd((a,HEADS*TAPS),f32),sd((16,d),f32)],cost_estimate=cost(4.0),
        input_output_aliases={2+i:i for i in range(len(carry))},
        scratch_shapes=[pltpu.VMEM(part.shape,bf16),pltpu.SemaphoreType.DMA((chunks+5,)),pltpu.VMEM((5,a,a),f32)],
        compiler_params=pltpu.CompilerParams(vmem_limit_bytes=12*2**20),name="unpack_b")(meta,part,*carry)

class Reduce:
    def __init__(self, meta, keep, send, rows, scatter):
        self.meta=meta; self.rows=rows
        self.stages,self.whole=stage_bits(rows,scatter)
        self.keep=keep
        self.got=lax.ppermute(send,"seq",swap_pairs())
        self.step=0
        self.axes=("rows","seq")
    def advance(self):
        n=len(self.stages); w=len(self.whole); k=self.step; self.step+=1
        self.last=k==2*n+w
        if k<n:
            self.keep,send=fold(self.meta,k,self.keep,self.got)
            self.got=lax.ppermute(send,self.axes,row_pairs(self.rows,self.stages[k]))
        elif k<n+w:
            self.keep=add_low(self.keep,self.got)
            b=self.whole[k-n]
            self.got=lax.ppermute(self.keep,self.axes,row_pairs(self.rows,(b,b)))
        elif k==n+w+n+1:
            self.other=self.got
            self.got=None
        else:
            self.keep=add_low(self.keep,self.got) if k==n+w else jnp.concatenate([self.keep,self.got],axis=0)
            m=2*n+w-1-k
            if m>=0:
                self.got=lax.ppermute(self.keep,self.axes,row_pairs(self.rows,self.stages[m]))
            else:
                self.got=lax.ppermute(self.keep,"seq",swap_pairs())
    def after(self, arrays):
        self.got,arrays=lax.optimization_barrier((self.got,tuple(arrays)))
        self.advance()
        self.keep,arrays=lax.optimization_barrier((self.keep,arrays))
        return arrays
    def follow(self, other):
        self.got,other.keep=lax.optimization_barrier((self.got,other.keep))
        self.advance()
    def finish(self):
        while self.got is not None:
            self.advance()
        return self.keep,self.other,2**len(self.stages)

def per_device(hidden_in,doc_lengths,out_grad,w_query,w_key,w_value,w_conv_out,depth_kernel,w_point,w_conv_kernel,
               w_output,ln1_gain,ln1_bias,w_ffn_in,w_ffn_out,ln2_gain,ln2_bias):
    row_count,local,d=hidden_in.shape
    a=w_query.shape[1]
    half=local//2
    rows=lax.axis_size("rows")
    side=lax.axis_index("seq")
    row=lax.axis_index("rows")
    hid=hidden_in[0]
    meta=jnp.concatenate([make_meta(doc_lengths[0],side,local,local*2),comm_meta(side,row,rows)])
    halo=lax.ppermute(lax.dynamic_slice_in_dim(hid,(1-side)*half,half,0),"seq",swap_pairs())
    q,kw,vw,cx,depth,ck,kern,cm=pre(meta,hid,halo,w_query,w_key,w_value,w_conv_out,depth_kernel,w_point,w_conv_kernel)
    ctx,lse=attn_fwd(meta,q,kw,vw)
    ln=jnp.stack([ln1_gain,ln1_bias,ln2_gain,ln2_bias]).astype(f32)
    ho,dres,dctx,dconv,keep,send,gln=ffn(meta,hid,ctx,cm,out_grad[0],w_output,w_ffn_in,w_ffn_out,ln)
    g,gi,go=w_ffn_in.shape
    ra=Reduce(meta,keep,send,rows,3)
    carry=attn_bwd(meta,2,1,q,kw,vw,ctx,dctx,lse,None)
    out=ra.after(tuple(carry)+(dconv,))
    carry,dconv=out[:4],out[4]
    dqc,dc,dda,ddb,rimc,gp=conv_back(meta,dconv,cm,kern,cx,q,ck,depth,w_point,w_conv_kernel)
    rimc=lax.ppermute(rimc,"seq",swap_pairs())
    out=ra.after(tuple(carry)+(dqc,dda))
    carry,dqc,dda=out[:4],out[4],out[5]
    dqa,dk,dv,dkv=attn_bwd(meta,0,2,q,kw,vw,ctx,dctx,lse,carry)
    dkv=lax.ppermute(dkv,"seq",swap_pairs())
    dda,dqa=ra.after((dda,dqa))
    dha,rima,gta=taps_back(meta,0,hid,halo,dda,depth_kernel)
    ddb,dha=ra.after((ddb,dha))
    dhb,rimb,gtb=taps_back(meta,1,hid,halo,ddb,depth_kernel)
    rima=lax.ppermute(rima,"seq",swap_pairs())
    rimb=lax.ppermute(rimb,"seq",swap_pairs())
    dp,keep,send=proj_back(meta,hid,dqa,dqc,dk,dv,dkv,dc,rimc,gp,gta,gtb,gln)
    rb=Reduce(meta,keep,send,rows,3)
    grad_in=grad_input(meta,dp,dres,dha,dhb,rima,rimb,w_query,w_key,w_value,w_conv_out)
    (grad_in,)=rb.after((grad_in,))
    for one,two in ((rb,ra),(ra,rb),(rb,ra),(ra,rb),(rb,ra),(ra,rb),(rb,ra),(rb,ra),(ra,rb),(rb,ra),(ra,rb)):
        one.follow(two)
    mine,other,chunks=ra.finish()
    ffn_out_grad,ffn_in_grad,output_grad=unpack_a(meta,mine,other,g,gi,go,d,chunks)
    ffn_in_grad,ffn_out_grad,output_grad=rb.after((ffn_in_grad,ffn_out_grad,output_grad))
    while not rb.last:
        rb.advance()
    first=unpack_b(meta,0,rb.keep,d,a,chunks,None)
    first,got=lax.optimization_barrier((tuple(first),rb.got))
    second=unpack_b(meta,1,got,d,a,chunks,first[:5])
    q_grad,k_grad,v_grad,c_grad,point_grad=second[:5]
    ck_grad=jnp.where(side==0,first[5],second[5])
    small=jnp.where(side==1,first[6],second[6])
    lng=small[KSIZE:KSIZE+4]
    return (ho[None],grad_in[None],q_grad,k_grad,v_grad,c_grad,small[:KSIZE],point_grad,ck_grad,output_grad,
            lng[0],lng[1],ffn_in_grad,ffn_out_grad,lng[2],lng[3])


def solution(mesh):
    placed=(P("rows","seq",None),P("rows",None),P("rows","seq",None))+(P(),)*14
    return jax.shard_map(per_device,mesh=mesh,in_specs=placed,
        out_specs=(P("rows","seq",None),P("rows","seq",None))+(P(),)*14,check_vma=False)
```

```python
import jax
import jax.numpy as jnp
from jax import lax
from jax.experimental import pallas as pl
from jax.experimental.pallas import tpu as pltpu
from jax.sharding import PartitionSpec as P

KSIZE = 9

HEADS=6
BLK=256
NEG=-1e30
f32=jnp.float32; bf16=jnp.bfloat16

def dot_nt(a,b):
    return lax.dot_general(a,b,(((1,),(1,)),((),())),preferred_element_type=f32)
def dot_nn(a,b):
    return lax.dot_general(a,b,(((1,),(0,)),((),())),preferred_element_type=f32)
def dot_tn(a,b):
    return lax.dot_general(a,b,(((0,),(0,)),((),())),preferred_element_type=f32)

def segs(meta, first, shape):
    pos=first+lax.broadcasted_iota(jnp.int32,shape,0)
    seg=jnp.zeros(shape,jnp.int32)
    for d in range(5):
        seg=seg+jnp.where(pos>=meta[d],1,0)
    return seg

def key_ext(meta, first, n):
    lane=lax.broadcasted_iota(jnp.int32,(n,128),1)
    seg=segs(meta,first,(n,128))
    diff=(lane>=24)&(lane<30)&(lane-24!=seg)
    return jnp.where(lane<24,-1.0,jnp.where(diff,NEG,0.0)).astype(bf16)

def fwd_kernel(meta, q_ref, k_ref, v_ref, ctx_ref, lse_ref, kx_ref, s_ref, m_ref, acc_ref):
    nkb=k_ref.shape[0]//BLK; nqb=q_ref.shape[0]//BLK; npair=HEADS//2
    for b in range(nkb):
        kx_ref[b*BLK:(b+1)*BLK,:]=key_ext(meta,meta[5]+b*BLK,BLK)
    lane=lax.broadcasted_iota(jnp.int32,(BLK,128),1)
    ones_lane=jnp.where(lane==0,1.0,0.0).astype(bf16)
    for qb in range(nqb):
        qrows=slice(qb*BLK,(qb+1)*BLK)
        seg=segs(meta,meta[6]+qb*BLK,(BLK,128))
        qext=jnp.where(lane-24==seg,1.0,0.0).astype(bf16)
        lo=meta[8+2*qb]; hi=meta[9+2*qb]
        m_ref[...]=jnp.full(m_ref.shape,NEG,f32)
        acc_ref[...]=jnp.zeros(acc_ref.shape,f32)
        def phase1(kb,_):
            r0=pl.multiple_of(kb*BLK,BLK)
            kext=kx_ref[pl.ds(r0,BLK),:]
            for j in range(npair):
                kk=jnp.concatenate([k_ref[pl.ds(r0,BLK),j*128:(j+1)*128],kext],axis=1)
                qp=q_ref[qrows,j*128:(j+1)*128]*jnp.asarray(0.125,bf16)
                for hh in range(2):
                    h=2*j+hh
                    qm=jnp.where((lane<64) if hh==0 else (lane>=64),qp,jnp.zeros_like(qp))
                    s=dot_nt(jnp.concatenate([qm,qext],axis=1),kk)
                    s_ref[h,:,pl.ds(r0,BLK)]=s
                    m_ref[h]=jnp.maximum(m_ref[h],jnp.maximum(s[:,:128],s[:,128:]))
            return 0
        lax.fori_loop(lo,hi,phase1,0)
        for h in range(HEADS):
            m_ref[h]=jnp.broadcast_to(jnp.max(m_ref[h],axis=1,keepdims=True),(BLK,128))
        def phase2(kb,_):
            r0=pl.multiple_of(kb*BLK,BLK)
            for j in range(npair):
                vv=jnp.concatenate([v_ref[pl.ds(r0,BLK),j*128:(j+1)*128],ones_lane],axis=1)
                for hh in range(2):
                    h=2*j+hh
                    mm=m_ref[h]
                    p=jnp.exp(s_ref[h,:,pl.ds(r0,BLK)]-jnp.concatenate([mm,mm],axis=1)).astype(bf16)
                    acc_ref[h]=acc_ref[h]+dot_nn(p,vv)
            return 0
        lax.fori_loop(lo,hi,phase2,0)
        lse_all=jnp.zeros((BLK,128),f32)
        for j in range(npair):
            parts=[]
            for hh in range(2):
                h=2*j+hh
                l=jnp.broadcast_to(acc_ref[h][:,128:129],(BLK,128))
                parts.append(acc_ref[h][:,:128]/l)
                lse=m_ref[h]+jnp.log(l)
                sel=(lane==h)|(lane==h+8)|(lane==h+16)
                lse_all=jnp.where(sel,lse,lse_all)
            ctx_ref[qrows,j*128:(j+1)*128]=jnp.where(lane<64,parts[0],parts[1]).astype(ctx_ref.dtype)
        lse_ref[qrows,:]=lse_all

def bwd_kernel(head, meta, q_ref, k_ref, v_ref, ctx_ref, dctx_ref, lse_ref, dq_ref, dko_ref, dvo_ref, dkv_ref, kx_ref, dk_ref, dv_ref):
    nkb=k_ref.shape[0]//BLK; nqb=q_ref.shape[0]//BLK; npair=q_ref.shape[1]//128
    width=q_ref.shape[1]
    for b in range(nkb):
        kx_ref[b*BLK:(b+1)*BLK,:]=key_ext(meta,meta[5]+b*BLK,BLK)
    dk_ref[...]=jnp.zeros(dk_ref.shape,f32)
    dv_ref[...]=jnp.zeros(dv_ref.shape,f32)
    dq_ref[...]=jnp.zeros(dq_ref.shape,f32)
    lane=lax.broadcasted_iota(jnp.int32,(BLK,128),1)
    vext=jnp.where(lane<16,-1.0,0.0).astype(bf16)
    r=head+lax.broadcasted_iota(jnp.int32,(width,128),0)//64
    cl=lax.broadcasted_iota(jnp.int32,(width,128),1)
    heads_of=jnp.where((cl<16)&(cl%8==r),1.0,0.0).astype(bf16)
    low=lane<64
    for qb in range(nqb):
        qrows=slice(qb*BLK,(qb+1)*BLK)
        seg=segs(meta,meta[6]+qb*BLK,(BLK,128))
        onehot=lane-24==seg
        lse=lse_ref[qrows,:]
        hi_=lse.astype(bf16).astype(f32)
        r1=lse-hi_
        mid=r1.astype(bf16).astype(f32)
        lo_=r1-mid
        split=jnp.where(lane<8,hi_,jnp.where(lane<16,mid,lo_))
        prod=ctx_ref[qrows,:].astype(f32)*dctx_ref[qrows,:].astype(f32)
        ph=prod.astype(bf16)
        plo=(prod-ph.astype(f32)).astype(bf16)
        dd=dot_nn(ph,heads_of)+dot_nn(plo,heads_of)
        dh=dd.astype(bf16).astype(f32)
        dsplit=jnp.where(lane<8,dh,dd-dh)
        qx=[];dcx=[];qms=[];dcs=[]
        for h in range(head,head+2*npair):
            j=(h-head)//2
            side=low if h%2==0 else ~low
            qp=q_ref[qrows,j*128:(j+1)*128]*jnp.asarray(0.125,bf16)
            qm=jnp.where(side,qp,jnp.zeros_like(qp))
            sel=(lane==h)|(lane==h+8)|(lane==h+16)
            qe=jnp.where(sel,split,jnp.where(onehot,1.0,0.0)).astype(bf16)
            qx.append(jnp.concatenate([qm,qe],axis=1))
            dp=dctx_ref[qrows,j*128:(j+1)*128]
            dm=jnp.where(side,dp,jnp.zeros_like(dp))
            de=jnp.where((lane==h)|(lane==h+8),dsplit,0.0).astype(bf16)
            dcx.append(jnp.concatenate([dm,de],axis=1))
            qms.append(qm);dcs.append(dm)
        lo=meta[8+2*qb]; hi=meta[9+2*qb]
        def body(kb,_):
            r0=pl.multiple_of(kb*BLK,BLK)
            kext=kx_ref[pl.ds(r0,BLK),:]
            for j in range(npair):
                cols=slice(j*128,(j+1)*128)
                kp=k_ref[pl.ds(r0,BLK),cols]
                kk=jnp.concatenate([kp,kext],axis=1)
                vv=jnp.concatenate([v_ref[pl.ds(r0,BLK),cols],vext],axis=1)
                pts=[];dss=[];ks=[]
                for hh in range(2):
                    h=2*j+hh
                    pt=jnp.exp(dot_nt(kk,qx[h]))
                    dpt=dot_nt(vv,dcx[h])
                    pts.append(pt.astype(bf16))
                    dss.append((pt*dpt).astype(bf16))
                    ks.append(jnp.where(low if hh==0 else ~low,kp,jnp.zeros_like(kp)))
                dv_ref[pl.ds(r0,BLK),cols]+=dot_nn(jnp.concatenate(pts,axis=1),jnp.concatenate(dcs[2*j:2*j+2],axis=0))
                dk_ref[pl.ds(r0,BLK),cols]+=dot_nn(jnp.concatenate(dss,axis=1),jnp.concatenate(qms[2*j:2*j+2],axis=0))
                dq_ref[qrows,cols]+=dot_tn(jnp.concatenate(dss,axis=0),jnp.concatenate(ks,axis=0))
            return 0
        lax.fori_loop(lo,hi,body,0)
        dq_ref[qrows,:]=dq_ref[qrows,:]*0.125
    n=q_ref.shape[0]; half=dkv_ref.shape[0]
    own_off=meta[7]*half; halo_off=(1-meta[7])*n
    for b in range(n//BLK):
        src=pl.multiple_of(own_off+b*BLK,BLK)
        dko_ref[b*BLK:(b+1)*BLK,:]=dk_ref[pl.ds(src,BLK),:]
        dvo_ref[b*BLK:(b+1)*BLK,:]=dv_ref[pl.ds(src,BLK),:]
    for b in range(half//BLK):
        src=pl.multiple_of(halo_off+b*BLK,BLK)
        for j in range(npair):
            dkv_ref[b*BLK:(b+1)*BLK,j*256:j*256+128]=dk_ref[pl.ds(src,BLK),j*128:(j+1)*128].astype(bf16)
            dkv_ref[b*BLK:(b+1)*BLK,j*256+128:(j+1)*256]=dv_ref[pl.ds(src,BLK),j*128:(j+1)*128].astype(bf16)

VM=pl.BlockSpec(memory_space=pltpu.VMEM)
SM=pl.BlockSpec(memory_space=pltpu.SMEM)
def attn_fwd(meta,q,k,v):
    t,w=q.shape
    return pl.pallas_call(fwd_kernel,in_specs=[SM,VM,VM,VM],out_specs=[VM,VM],
        out_shape=[jax.ShapeDtypeStruct((t,w),bf16),jax.ShapeDtypeStruct((t,128),f32)],
        scratch_shapes=[pltpu.VMEM((k.shape[0],128),bf16),pltpu.VMEM((HEADS,BLK,k.shape[0]),f32),
            pltpu.VMEM((HEADS,BLK,128),f32),pltpu.VMEM((HEADS,BLK,256),f32)],
        compiler_params=pltpu.CompilerParams(vmem_limit_bytes=30*2**20),cost_estimate=cost(15.0),name="attn_fwd")(meta,q,k,v)
def attn_bwd(meta,first,pairs,q,k,v,ctx,dctx,lse,carry):
    t,w=q.shape; kn=k.shape[0]; wide=128*pairs
    sd=jax.ShapeDtypeStruct
    def col(n,width):
        return pl.BlockSpec((n,width),lambda i:(0,first//pairs))
    def kernel(*refs):
        bwd_kernel(2*first,*refs[:7],*refs[-7:])
    carry=() if carry is None else tuple(carry)
    return pl.pallas_call(kernel,grid=(1,),
        in_specs=[SM,col(t,wide),col(kn,wide),col(kn,wide),col(t,wide),col(t,wide),pl.BlockSpec((t,128),lambda i:(0,0))]+[pl.BlockSpec(memory_space=pl.ANY)]*len(carry),
        out_specs=[col(t,wide)]*3+[col(kn-t,2*wide)],
        out_shape=[sd((t,w),f32)]*3+[sd((kn-t,2*w),bf16)],
        scratch_shapes=[pltpu.VMEM((kn,128),bf16),pltpu.VMEM((kn,wide),f32),pltpu.VMEM((kn,wide),f32)],
        input_output_aliases={7+i:i for i in range(len(carry))},cost_estimate=cost(9.0*pairs),
        compiler_params=pltpu.CompilerParams(vmem_limit_bytes=(16+4*pairs)*2**20),name="attn_bwd")(meta,q,k,v,ctx,dctx,lse,*carry)

def make_meta(lengths, side, local, full):
    ends=jnp.cumsum(lengths)
    starts=ends-lengths
    win=side*(local//2); own=side*local
    nqb=local//BLK
    b0=own+jnp.arange(nqb)*BLK
    b1=b0+BLK-1
    bounds_lo=jnp.concatenate([jnp.zeros((1,),jnp.int32),ends])
    bounds_hi=jnp.concatenate([ends,jnp.full((1,),full,jnp.int32)])
    seg0=jnp.sum((b0[:,None]>=ends[None]).astype(jnp.int32),1)
    seg1=jnp.sum((b1[:,None]>=ends[None]).astype(jnp.int32),1)
    first=jnp.sum(jnp.where(jnp.arange(6)[None]==seg0[:,None],bounds_lo[None],0),1)
    last=jnp.sum(jnp.where(jnp.arange(6)[None]==seg1[:,None],bounds_hi[None],0),1)
    lo=jnp.maximum(first-win,0)//BLK
    hi=jnp.minimum((last-win+BLK-1)//BLK,(local+local//2)//BLK)
    return jnp.concatenate([ends,win[None],own[None],side[None],jnp.stack([lo,hi],1).reshape(-1)]).astype(jnp.int32)


TB=256

def gelu_parts(z):
    a=jnp.abs(z)
    t=1.0/(1.0+a*(0.3275911*0.7071067811865476))
    e=jnp.exp(-0.5*z*z)
    poly=t*(0.127414796+t*(-0.142248368+t*(0.7107068705+t*(-0.7265760135+t*0.5307027145))))
    ht=poly*e
    phi=jnp.where(z>=0.0,1.0-ht,ht)
    return z*phi, phi+z*(e*0.3989422804014327)

def rows8(x):
    return jnp.sum(x.reshape(x.shape[0]//8,8,x.shape[1]),axis=0)

def norm_parts(z):
    mu=jnp.mean(z,axis=-1,keepdims=True)
    c=z-mu
    var=jnp.mean(c*c,axis=-1,keepdims=True)
    rstd=lax.rsqrt(var+1e-6)
    return c*rstd, rstd

def norm_back(d, gain, xhat, rstd):
    dx=d*gain
    a=jnp.mean(dx,axis=-1,keepdims=True)
    b=jnp.mean(dx*xhat,axis=-1,keepdims=True)
    return rstd*(dx-a-xhat*b)

def ffn_kernel(meta, hid_ref, ctx_ref, cm_ref, og_ref, wo_ref, win_ref, wout_ref, ln_ref,
               ho_ref, dres_ref, dctx_ref, dconv_ref, keep_ref, send_ref, gln_ref,
               act_ref, dff_ref, x1_ref, dfo_ref, datt_ref, mix_ref):
    n=hid_ref.shape[0]; d=hid_ref.shape[1]; groups=win_ref.shape[0]; gi=d//groups; go=win_ref.shape[2]
    attn=dctx_ref.shape[1]
    tile=512
    gln_ref[...]=jnp.zeros(gln_ref.shape,f32)
    def block(i,_):
        r0=pl.multiple_of(i*TB,TB)
        rows=pl.ds(r0,TB)
        g1=ln_ref[0:1,:];b1=ln_ref[1:2,:];g2=ln_ref[2:3,:];b2=ln_ref[3:4,:]
        att=dot_nn(jnp.concatenate([ctx_ref[rows,:],cm_ref[rows,:]],axis=1),wo_ref[...])
        xhat1,rstd1=norm_parts(hid_ref[rows,:].astype(f32)+att)
        first=xhat1*g1+b1
        x1=first.astype(bf16)
        for g in range(groups):
            x1_ref[g,rows,:]=x1[:,g*gi:(g+1)*gi]
        mix_ref[0,rows,:]=ctx_ref[rows,:]
        mix_ref[1,rows,:]=cm_ref[rows,:]
        tiles=[(g,c) for g in range(groups) for c in range(go//tile)]
        def up(g,c):
            return dot_nn(x1[:,g*gi:(g+1)*gi],win_ref[g,:,c*tile:(c+1)*tile])
        outs=[None]*groups
        ahead=up(*tiles[0])
        for t,(g,c) in enumerate(tiles):
            z=ahead
            if t+1<len(tiles):
                ahead=up(*tiles[t+1])
            cols=slice(c*tile,(c+1)*tile)
            a,gp=gelu_parts(z)
            ab=a.astype(bf16)
            act_ref[g,rows,cols]=ab
            dff_ref[g,rows,cols]=gp.astype(bf16)
            o=dot_nn(ab,wout_ref[g,cols,:])
            outs[g]=o if outs[g] is None else outs[g]+o
        xhat2,rstd2=norm_parts(first+jnp.concatenate(outs,axis=1))
        pos=meta[6]+r0+lax.broadcasted_iota(jnp.int32,(TB,d),0)
        valid=pos<meta[4]
        ho_ref[rows,:]=jnp.where(valid,xhat2*g2+b2,0.0).astype(bf16)
        gn=jnp.where(valid,og_ref[rows,:].astype(f32),0.0)
        gln_ref[16:24,:]+=rows8(gn*xhat2)
        gln_ref[24:32,:]+=rows8(gn)
        dres2=norm_back(gn,g2,xhat2,rstd2)
        dfo=dres2.astype(bf16)
        for g in range(groups):
            dfo_ref[g,rows,:]=dfo[:,g*gi:(g+1)*gi]
        def down(g,c):
            return dot_nt(dfo[:,g*gi:(g+1)*gi],wout_ref[g,c*tile:(c+1)*tile,:])
        backs=[None]*groups
        ahead=down(*tiles[0])
        for t,(g,c) in enumerate(tiles):
            da=ahead
            if t+1<len(tiles):
                ahead=down(*tiles[t+1])
            cols=slice(c*tile,(c+1)*tile)
            dh=(da*dff_ref[g,rows,cols].astype(f32)).astype(bf16)
            dff_ref[g,rows,cols]=dh
            o=dot_nt(dh,win_ref[g,:,cols])
            backs[g]=o if backs[g] is None else backs[g]+o
        dfirst=dres2+jnp.concatenate(backs,axis=1)
        gln_ref[0:8,:]+=rows8(dfirst*xhat1)
        gln_ref[8:16,:]+=rows8(dfirst)
        dres1=norm_back(dfirst,g1,xhat1,rstd1)
        dres_ref[rows,:]=dres1
        datt=dres1.astype(bf16)
        datt_ref[rows,:]=datt
        dm=dot_nt(datt,wo_ref[...])
        dctx_ref[rows,:]=dm[:,:attn].astype(bf16)
        dconv_ref[rows,:]=dm[:,attn:]
        return 0
    lax.fori_loop(0,n//TB,block,0)
    side=meta[7]
    for ref,g in ((send_ref,1-side),(keep_ref,side)):
        at=0
        for c in range(go//gi):
            ref[at*gi:(at+1)*gi,:]=dot_tn(act_ref[g,:,c*gi:(c+1)*gi],dfo_ref[g]).astype(ref.dtype)
            at+=1
        wide=dot_tn(x1_ref[g],dff_ref[g]).astype(ref.dtype)
        for c in range(go//gi):
            ref[at*gi:(at+1)*gi,:]=wide[:,c*gi:(c+1)*gi]
            at+=1
        for c in range(d//attn):
            ref[at*gi:(at+1)*gi,:]=dot_tn(mix_ref[g],datt_ref[:,c*attn:(c+1)*attn]).astype(ref.dtype)
            at+=1

def ffn(meta,hid,ctx,cm,og,wo,win,wout,ln):
    n,d=hid.shape; g,gi,go=win.shape; attn=ctx.shape[1]
    sd=jax.ShapeDtypeStruct
    return pl.pallas_call(ffn_kernel,in_specs=[SM]+[VM]*8,out_specs=[VM]*7,
        out_shape=[sd((n,d),bf16),sd((n,d),f32),sd((n,attn),bf16),sd((n,attn),f32),
                   sd((2*go+d,attn),bf16),sd((2*go+d,attn),bf16),sd((32,d),f32)],
        scratch_shapes=[pltpu.VMEM((g,n,go),bf16),pltpu.VMEM((g,n,go),bf16),pltpu.VMEM((g,n,gi),bf16),
                        pltpu.VMEM((g,n,gi),bf16),pltpu.VMEM((n,d),bf16),pltpu.VMEM((2,n,attn),bf16)],
        cost_estimate=cost(40.0),compiler_params=pltpu.CompilerParams(vmem_limit_bytes=40*2**20),name="ffn")(meta,hid,ctx,cm,og,wo,win,wout,ln)

TAPS=9
HALF=4
PAD=8
TB=256
CH=64
CS=32
LAST=128

def doc_bounds(meta, first, shape):
    pos=first+lax.broadcasted_iota(jnp.int32,shape,0)
    nxt=jnp.full(shape,2**30,jnp.int32)
    prv=jnp.full(shape,-2**30,jnp.int32)
    for d in range(5):
        e=meta[d]
        nxt=jnp.minimum(nxt,jnp.where(e>pos,e,2**30))
        prv=jnp.maximum(prv,jnp.where(e<=pos,e,-2**30))
    return nxt-pos, pos-prv

def tap_mask(bounds, o):
    rem,age=bounds
    if o>HALF:
        return rem>(o-HALF)
    return age>=(HALF-o)

def masked(x, bounds, o):
    if o==HALF:
        return x
    return jnp.where(tap_mask(bounds,o),x,0.0)

def tap_onehot(rows, cols, o):
    r=lax.broadcasted_iota(jnp.int32,(rows,cols),0)
    c=lax.broadcasted_iota(jnp.int32,(rows,cols),1)
    return jnp.where(r==(c//64)*TAPS+o,1.0,0.0).astype(bf16)

def pre_kernel(meta, hid_ref, halo_ref, wq_ref, wk_ref, wv_ref, wc_ref, taps_ref, wp_ref, wck_ref,
               q_ref, kw_ref, vw_ref, cx_ref, depth_ref, ck_ref, kern_hbm, cm_ref,
               hx_ref, wx_ref, lx_ref, kern_ref, sems):
    n,d=hid_ref.shape; half=halo_ref.shape[0]; attn=q_ref.shape[1]
    side=meta[7]
    own_off=side*half; halo_off=(1-side)*n
    jt=attn//128; jd=d//128
    for o in range(TAPS):
        wx_ref[:,o*attn:(o+1)*attn]=dot_nn(wck_ref[...],tap_onehot(HEADS*TAPS,attn,o)).astype(bf16)
    left=jnp.where(side==1,halo_ref[half-16:half,:].astype(f32),0.0)
    right=jnp.where(side==0,halo_ref[0:16,:].astype(f32),0.0)
    rims=jnp.concatenate([left,right],axis=0).astype(bf16)
    crim=dot_nn(rims,wc_ref[...]).astype(bf16).astype(f32)
    for j in range(jd):
        hx_ref[j,0:PAD,:]=left[PAD:2*PAD,j*128:(j+1)*128]
        hx_ref[j,n+PAD:n+2*PAD,:]=right[0:PAD,j*128:(j+1)*128]
    for j in range(jt):
        cx_ref[j,0:PAD,:]=crim[PAD:2*PAD,j*128:(j+1)*128]
        cx_ref[j,n+PAD:n+2*PAD,:]=crim[16:16+PAD,j*128:(j+1)*128]
    def project(i,_):
        r0=pl.multiple_of(i*TB,TB)
        x=hid_ref[pl.ds(r0,TB),:]
        q_ref[pl.ds(r0,TB),:]=dot_nn(x,wq_ref[...]).astype(bf16)
        ow=pl.multiple_of(own_off+r0,TB)
        kw_ref[pl.ds(ow,TB),:]=dot_nn(x,wk_ref[...]).astype(bf16)
        vw_ref[pl.ds(ow,TB),:]=dot_nn(x,wv_ref[...]).astype(bf16)
        c=dot_nn(x,wc_ref[...]).astype(bf16).astype(f32)
        rp=pl.multiple_of(r0+PAD,PAD)
        for j in range(jt):
            cx_ref[j,pl.ds(rp,TB),:]=c[:,j*128:(j+1)*128]
        xf=x.astype(f32)
        for j in range(jd):
            hx_ref[j,pl.ds(rp,TB),:]=xf[:,j*128:(j+1)*128]
        return 0
    lax.fori_loop(0,n//TB,project,0)
    def project_halo(i,_):
        r0=pl.multiple_of(i*TB,TB)
        x=halo_ref[pl.ds(r0,TB),:]
        ow=pl.multiple_of(halo_off+r0,TB)
        kw_ref[pl.ds(ow,TB),:]=dot_nn(x,wk_ref[...]).astype(bf16)
        vw_ref[pl.ds(ow,TB),:]=dot_nn(x,wv_ref[...]).astype(bf16)
        return 0
    lax.fori_loop(0,half//TB,project_halo,0)
    def depthwise(i,_):
        r0=pl.multiple_of(i*CH,CH)
        bounds=doc_bounds(meta,meta[6]+r0,(CH,128))
        for j in range(jd):
            acc=None
            for o in range(TAPS):
                x=hx_ref[j,pl.ds(r0+PAD+o-HALF,CH),:]
                term=masked(x*taps_ref[o:o+1,j*128:(j+1)*128].astype(f32),bounds,o)
                acc=term if acc is None else acc+term
            depth_ref[pl.ds(r0,CH),j*128:(j+1)*128]=acc.astype(bf16)
        return 0
    lax.fori_loop(0,n//CH,depthwise,0)
    def dynamic(r0):
        ck=dot_nn(depth_ref[pl.ds(r0,TB),:],wp_ref[...])
        ck_ref[pl.ds(r0,TB),:]=ck
        mk=(ck*q_ref[pl.ds(r0,TB),:].astype(f32)).astype(bf16)
        for o in range(TAPS):
            lx_ref[o]=dot_nn(mk,wx_ref[:,o*attn:(o+1)*attn])
        def soft(s,_):
            s0=pl.multiple_of(s*CS,CS)
            rows=pl.ds(s0,CS)
            t0=pl.multiple_of(r0+s0,CS)
            bounds=doc_bounds(meta,meta[6]+t0,(CS,128))
            for j in range(jt):
                cols=slice(j*128,(j+1)*128)
                ls=[lx_ref[o,rows,cols] for o in range(TAPS)]
                m=ls[0]
                for o in range(1,TAPS):
                    m=jnp.maximum(m,ls[o])
                es=[jnp.exp(l-m) for l in ls]
                tot=es[0]
                for o in range(1,TAPS):
                    tot=tot+es[o]
                inv=1.0/tot
                acc=None
                for o in range(TAPS):
                    k=es[o]*inv
                    kern_ref[o,pl.ds(t0,CS),cols]=k.astype(bf16)
                    term=masked(k*cx_ref[j,pl.ds(t0+PAD+o-HALF,CS),:],bounds,o)
                    acc=term if acc is None else acc+term
                cm_ref[pl.ds(t0,CS),cols]=acc.astype(bf16)
            return 0
        lax.fori_loop(0,TB//CS,soft,0)
    stores=[]
    for b in range(n//TB):
        dynamic(b*TB)
        x=pltpu.make_async_copy(kern_ref.at[:,pl.ds(b*TB,TB),:],kern_hbm.at[:,pl.ds(b*TB,TB),:],sems.at[b])
        x.start()
        stores.append(x)
    for x in stores:
        x.wait()

def pre(meta,hid,halo,wq,wk,wv,wc,taps,wp,wck):
    n,d=hid.shape; half=halo.shape[0]; a=wq.shape[1]; sd=jax.ShapeDtypeStruct
    anys=pl.BlockSpec(memory_space=pl.ANY)
    def whole(*shape):
        return pl.BlockSpec(shape,lambda i:(0,)*len(shape))
    proj=whole(d,a)
    return pl.pallas_call(pre_kernel,grid=(1,),in_specs=[SM,whole(n,d),VM,proj,proj,proj,proj,VM,proj,VM],out_specs=[VM]*6+[anys,VM],
        out_shape=[sd((n,a),bf16),sd((n+half,a),bf16),sd((n+half,a),bf16),sd((a//128,n+2*PAD,128),f32),
                   sd((n,d),bf16),sd((n,a),f32),sd((TAPS,n,a),bf16),sd((n,a),bf16)],
        scratch_shapes=[pltpu.VMEM((d//128,n+2*PAD,128),f32),pltpu.VMEM((a,TAPS*a),bf16),pltpu.VMEM((TAPS,TB,a),f32),
                        pltpu.VMEM((TAPS,n,a),bf16),pltpu.SemaphoreType.DMA((n//TB,))],
        cost_estimate=cost(30.0),compiler_params=pltpu.CompilerParams(vmem_limit_bytes=40*2**20),name="pre")(meta,hid,halo,wq,wk,wv,wc,taps,wp,wck)

def conv_back_kernel(meta, dconv_ref, cm_ref, kern_ref, cx_ref, q_ref, ck_ref, depth_ref,
                     wp_ref, wck_ref,
                     dqc_ref, dc_ref, dda_ref, ddb_ref, rimc_ref, gp_ref,
                     p_ref, pr_ref, dlc_ref, mk_ref, dck_ref, wcx_ref, dep_ref):
    d=depth_ref.shape[1]; attn,n=q_ref.shape[1],dc_ref.shape[0]
    i=pl.program_id(0)
    side=meta[7]; jt=attn//128; jd=d//128; hd=jd//2
    dds=[(dda_ref,j) if j<hd else (ddb_ref,j-hd) for j in range(jd)]
    @pl.when(i==0)
    def _():
        zero=jnp.zeros((2*PAD,128),f32)
        for j in range(jt):
            for o in range(TAPS):
                p_ref[o,j,0:2*PAD,:]=zero
                p_ref[o,j,n+2*PAD:n+4*PAD,:]=zero
        for ref,j in dds:
            ref[j,0:2*PAD,:]=zero
            ref[j,n+2*PAD:n+4*PAD,:]=zero
        r=lax.broadcasted_iota(jnp.int32,(HEADS*TAPS,attn),0)
        c=lax.broadcasted_iota(jnp.int32,(HEADS*TAPS,attn),1)
        spread=jnp.where((c%64<TAPS)&(r==(c//64)*TAPS+c%64),1.0,0.0).astype(bf16)
        wcx_ref[...]=dot_nn(wck_ref[...],spread).astype(bf16)
    def ones_block(w):
        return jnp.where(lax.broadcasted_iota(jnp.int32,(w,w),0)//64==lax.broadcasted_iota(jnp.int32,(w,w),1)//64,1.0,0.0).astype(bf16)
    ones256=ones_block(256); ones128=ones_block(128)
    lane=lax.broadcasted_iota(jnp.int32,(TB,attn),1)%64
    def dynamic():
        r0=pl.multiple_of(i*TB,TB)
        rows=pl.ds(r0,TB)
        def products(s,_):
            s0=pl.multiple_of(s*CS,CS)
            t0=pl.multiple_of(r0+s0,CS)
            bounds=doc_bounds(meta,meta[6]+t0,(CS,128))
            for j in range(jt):
                cols=slice(j*128,(j+1)*128)
                g=dconv_ref[pl.ds(s0,CS),cols]
                cm=cm_ref[pl.ds(s0,CS),cols].astype(f32)
                for o in range(TAPS):
                    cs=masked(cx_ref[j,pl.ds(t0+PAD+o-HALF,CS),:],bounds,o)
                    pr_ref[o,pl.ds(s0,CS),cols]=(g*(cs-cm)).astype(bf16)
                    p_ref[o,j,pl.ds(t0+2*PAD,CS),:]=masked(kern_ref[o,pl.ds(s0,CS),cols].astype(f32)*g,bounds,o)
            return 0
        lax.fori_loop(0,TB//CS,products,0)
        dl=jnp.zeros((TB,attn),f32)
        for o in range(TAPS):
            pr=pr_ref[o]
            dk=jnp.concatenate([dot_nn(pr[:,:256],ones256),dot_nn(pr[:,256:],ones128)],axis=1)
            dl=jnp.where(lane==o,kern_ref[o].astype(f32)*dk,dl)
        dlb=dl.astype(bf16)
        dlc_ref[rows,:]=dlb
        dmk=dot_nt(dlb,wcx_ref[...])
        dep_ref[rows,:]=depth_ref[...]
        q=q_ref[...].astype(f32)
        ck=ck_ref[...]
        mk_ref[rows,:]=(ck*q).astype(bf16)
        dqc_ref[...]=dmk*ck
        dck=(dmk*q).astype(bf16)
        dck_ref[rows,:]=dck
        dd=dot_nt(dck,wp_ref[...])
        rp=pl.multiple_of(r0+2*PAD,PAD)
        for j in range(jd):
            dds[j][0][dds[j][1],pl.ds(rp,TB),:]=dd[:,j*128:(j+1)*128]
    dynamic()
    @pl.when(i==pl.num_programs(0)-1)
    def _():
        def gather_c(row, size):
            out=[]
            for j in range(jt):
                acc=None
                for o in range(TAPS):
                    x=p_ref[o,j,pl.ds(row+PAD+HALF-o,size),:]
                    acc=x if acc is None else acc+x
                out.append(acc)
            return out
        def own_c(i,_):
            r0=pl.multiple_of(i*CS,CS)
            out=gather_c(r0+PAD,CS)
            for j in range(jt):
                dc_ref[pl.ds(r0,CS),j*128:(j+1)*128]=out[j]
            return 0
        lax.fori_loop(0,n//CS,own_c,0)
        left=gather_c(0,PAD); right=gather_c(n+PAD,PAD)
        for j in range(jt):
            rimc_ref[:,j*128:(j+1)*128]=jnp.where(side==1,left[j],right[j])
        for b in range(d//attn):
            gp_ref[b]=dot_tn(dep_ref[:,b*attn:(b+1)*attn],dck_ref[...]).astype(gp_ref.dtype)
        gp_ref[d//attn]=dot_tn(dlc_ref[...],mk_ref[...]).astype(gp_ref.dtype)

def taps_back_kernel(meta, hid_ref, halo_ref, dd_ref, taps_ref, dh_ref, rim_ref, gtap_ref):
    n,d=hid_ref.shape; half=halo_ref.shape[0]
    side=meta[7]; jd=d//128
    def gather_h(row, size, j, hx, bounds, sums):
        acc=None; new=[]
        for o in range(TAPS):
            x=masked(dd_ref[j,pl.ds(row+PAD+o-HALF,size),:],bounds,o)
            b=TAPS-1-o
            term=x*taps_ref[b:b+1,j*128:(j+1)*128].astype(f32)
            acc=term if acc is None else acc+term
            new.append(jnp.sum((x*hx).reshape(size//8,8,128),axis=0))
        return acc,[s+t for s,t in zip(sums,new)]
    lhalo=jnp.where(side==1,halo_ref[half-16:half,:].astype(f32),0.0)[PAD:2*PAD,:]
    rhalo=jnp.where(side==0,halo_ref[0:16,:].astype(f32),0.0)[0:PAD,:]
    for j in range(jd):
        cols=slice(j*128,(j+1)*128)
        sums=[jnp.zeros((8,128),f32) for _ in range(TAPS)]
        la,sums=gather_h(0,PAD,j,lhalo[:,cols],doc_bounds(meta,meta[6]-PAD,(PAD,128)),sums)
        ra,sums=gather_h(n+PAD,PAD,j,rhalo[:,cols],doc_bounds(meta,meta[6]+n,(PAD,128)),sums)
        rim_ref[:,cols]=jnp.where(side==1,la,ra)
        def own_h(i,sums):
            r0=pl.multiple_of(i*CS,CS)
            acc,sums=gather_h(r0+PAD,CS,j,hid_ref[pl.ds(r0,CS),cols].astype(f32),doc_bounds(meta,meta[6]+r0,(CS,128)),sums)
            dh_ref[pl.ds(r0,CS),cols]=acc
            return sums
        sums=lax.fori_loop(0,n//CS,own_h,sums)
        for o in range(TAPS):
            b=TAPS-1-o
            gtap_ref[b*8:(b+1)*8,cols]=sums[o]

def conv_back(meta,dconv,cm,kern,cx,q,ck,depth,wp,wck):
    n,d=depth.shape; a=q.shape[1]; sd=jax.ShapeDtypeStruct
    def row(w):
        return pl.BlockSpec((TB,w),lambda i:(i,0))
    def whole(*shape):
        return pl.BlockSpec(shape,lambda i:(0,)*len(shape))
    half=(d//256,n+4*PAD,128)
    return pl.pallas_call(conv_back_kernel,grid=(n//TB,),
        in_specs=[SM,row(a),row(a),pl.BlockSpec((TAPS,TB,a),lambda i:(0,i,0)),VM,row(a),row(a),row(d),VM,VM],
        out_specs=[row(a),whole(n,a),whole(*half),whole(*half),whole(PAD,a),whole(d//a+1,a,a)],
        out_shape=[sd((n,a),f32),sd((n,a),f32),sd(half,f32),sd(half,f32),sd((PAD,a),f32),sd((d//a+1,a,a),bf16)],
        scratch_shapes=[pltpu.VMEM((TAPS,a//128,n+4*PAD,128),f32),pltpu.VMEM((TAPS,TB,a),bf16),
                        pltpu.VMEM((n,a),bf16),pltpu.VMEM((n,a),bf16),pltpu.VMEM((n,a),bf16),pltpu.VMEM((a,a),bf16),pltpu.VMEM((n,d),bf16)],
        cost_estimate=cost(20.0),compiler_params=pltpu.CompilerParams(vmem_limit_bytes=48*2**20),name="conv_back")(meta,dconv,cm,kern,cx,q,ck,depth,wp,wck)

def taps_back(meta,part,hid,halo,dd,taps):
    n=hid.shape[0]; d=dd.shape[0]*128; sd=jax.ShapeDtypeStruct
    def col(rows):
        return pl.BlockSpec((rows,d),lambda i:(0,part))
    def whole(*shape):
        return pl.BlockSpec(shape,lambda i:(0,)*len(shape))
    return pl.pallas_call(taps_back_kernel,grid=(1,),in_specs=[SM,col(n),col(halo.shape[0]),whole(*dd.shape),col(TAPS)],
        out_specs=[whole(n,d),whole(PAD,d),whole(TAPS*8,d)],
        out_shape=[sd((n,d),f32),sd((PAD,d),f32),sd((TAPS*8,d),f32)],
        cost_estimate=cost(6.0),compiler_params=pltpu.CompilerParams(vmem_limit_bytes=24*2**20),name="taps_back")(meta,hid,halo,dd,taps)

def proj_back_kernel(meta, hid_ref, dqa_ref, dqc_ref, dk_ref, dv_ref, dkv_ref, dc_ref, rimc_ref, gp_ref, gta_ref, gtb_ref, gln_ref,
                     dp_ref, keep_ref, send_ref):
    n,d=hid_ref.shape; attn=dqa_ref.shape[1]; half=dkv_ref.shape[0]
    side=meta[7]
    shift=(1-side)*half
    def block(i,_):
        r0=pl.multiple_of(i*TB,TB)
        rows=pl.ds(r0,TB)
        inside=(r0>=shift)&(r0<shift+half)
        scale=jnp.where(inside,1.0,0.0)
        hr=pl.multiple_of(jnp.where(inside,r0-shift,0),TB)
        other=dkv_ref[pl.ds(hr,TB),:].astype(f32)*scale
        top=jnp.where((side==1)&(i==0),rimc_ref[...],0.0)
        bottom=jnp.where((side==0)&(i==n//TB-1),rimc_ref[...],0.0)
        rim=jnp.concatenate([top,jnp.zeros((TB-2*PAD,attn),f32),bottom],axis=0)
        dp_ref[rows,0:attn]=(dqa_ref[rows,:]+dqc_ref[rows,:]).astype(bf16)
        for j in range(attn//128):
            cols=slice(j*128,(j+1)*128)
            dp_ref[rows,attn+j*128:attn+(j+1)*128]=(dk_ref[rows,cols]+other[:,j*256:j*256+128]).astype(bf16)
            dp_ref[rows,2*attn+j*128:2*attn+(j+1)*128]=(dv_ref[rows,cols]+other[:,j*256+128:(j+1)*256]).astype(bf16)
        dp_ref[rows,3*attn:]=(dc_ref[rows,:]+rim).astype(bf16)
        return 0
    lax.fori_loop(0,n//TB,block,0)
    zeros=jnp.zeros((1,d),f32)
    small=[jnp.concatenate([jnp.sum(t[o*8:(o+1)*8,:],axis=0,keepdims=True) for t in (gta_ref,gtb_ref)],axis=1) for o in range(TAPS)]
    small+=[jnp.sum(gln_ref[k*8:(k+1)*8,:],axis=0,keepdims=True) for k in range(4)]
    small=jnp.concatenate(small+[zeros]*(16-len(small)),axis=0)
    for ref,h in ((send_ref,1-side),(keep_ref,side)):
        hc=pl.ds(pl.multiple_of(h*attn,128),attn)
        for k in range(4):
            ref[k*attn:(k+1)*attn,:]=dot_tn(hid_ref[:,hc],dp_ref[:,k*attn:(k+1)*attn]).astype(ref.dtype)
        ref[4*attn:5*attn,:]=gp_ref[h]
        @pl.when(h==0)
        def _():
            for k in range(HEADS):
                ref[5*attn+16*k:5*attn+16*(k+1),:]=gp_ref[2,64*k:64*k+16,:]
            ref[5*attn+16*HEADS:5*attn+LAST,:]=jnp.zeros((LAST-16*HEADS,attn),bf16)
        @pl.when(h==1)
        def _():
            ref[5*attn:5*attn+16,:]=small[:,:attn].astype(bf16)
            ref[5*attn+16:5*attn+32,:]=small[:,attn:].astype(bf16)
            ref[5*attn+32:5*attn+LAST,:]=jnp.zeros((LAST-32,attn),bf16)

def proj_back(meta,hid,dqa,dqc,dk,dv,dkv,dc,rimc,gp,gta,gtb,gln):
    n,d=hid.shape; a=dqa.shape[1]; sd=jax.ShapeDtypeStruct
    return pl.pallas_call(proj_back_kernel,in_specs=[SM]+[VM]*12,out_specs=[VM]*3,
        out_shape=[sd((n,4*a),bf16),sd((5*a+LAST,a),bf16),sd((5*a+LAST,a),bf16)],cost_estimate=cost(9.0),
        compiler_params=pltpu.CompilerParams(vmem_limit_bytes=16*2**20),name="proj_back")(meta,hid,dqa,dqc,dk,dv,dkv,dc,rimc,gp,gta,gtb,gln)

def grad_in_kernel(meta, dp_ref, dres_ref, dha_ref, dhb_ref, rima_ref, rimb_ref, wq_ref, wk_ref, wv_ref, wc_ref, gi_ref):
    n,d=gi_ref.shape; attn=wq_ref.shape[1]
    side=meta[7]
    def block(i,_):
        r0=pl.multiple_of(i*TB,TB)
        rows=pl.ds(r0,TB)
        acc=dres_ref[rows,:]+jnp.concatenate([dha_ref[rows,:],dhb_ref[rows,:]],axis=1)
        for k,w in enumerate((wq_ref,wk_ref,wv_ref,wc_ref)):
            acc=acc+dot_nt(dp_ref[rows,k*attn:(k+1)*attn],w[...])
        gi_ref[rows,:]=acc
        return 0
    lax.fori_loop(0,n//TB,block,0)
    at=pl.multiple_of((1-side)*(n-PAD),PAD)
    gi_ref[pl.ds(at,PAD),:]+=jnp.concatenate([rima_ref[...],rimb_ref[...]],axis=1)

def grad_input(meta,dp,dres,dha,dhb,rima,rimb,wq,wk,wv,wc):
    n,d=dres.shape; sd=jax.ShapeDtypeStruct
    return pl.pallas_call(grad_in_kernel,in_specs=[SM]+[VM]*10,out_specs=VM,
        out_shape=sd((n,d),f32),cost_estimate=cost(9.0),
        compiler_params=pltpu.CompilerParams(vmem_limit_bytes=16*2**20),name="grad_input")(meta,dp,dres,dha,dhb,rima,rimb,wq,wk,wv,wc)

AT=16

def swap_pairs():
    return [(0,1),(1,0)]

def stage_bits(size, scatter):
    bits=[]
    b=1
    while b<size:
        bits.append(b)
        b*=2
    lead=bits[:3]
    other=lead[-1:]+lead[:-1]+bits[3:]
    n=min(scatter,len(bits))
    return list(zip(bits,other))[:n],bits[n:]

def row_pairs(rows, bits):
    return [(r*2+s,(r^bits[s])*2+s) for r in range(rows) for s in range(2)]

def comm_meta(side, row, rows):
    stages,_=stage_bits(rows,4)
    own=[jnp.where(side==0,(row//b0)%2,(row//b1)%2) for b0,b1 in stages]
    oth=[jnp.where(side==0,(row//b1)%2,(row//b0)%2) for b0,b1 in stages]
    c=jnp.int32(0); c2=jnp.int32(0)
    for u,v in list(zip(own,oth))[:3]:
        c=c*2+u; c2=c2*2+v
    own=own+[jnp.int32(0)]*(4-len(own))
    return jnp.stack(own+[c,c2]).astype(jnp.int32)

def cost(us):
    return pl.CostEstimate(flops=int(us*1.0e9),bytes_accessed=0,transcendentals=0)

def fold_kernel(stage, meta, keep_ref, got_ref, k_ref, s_ref):
    h=k_ref.shape[0]; ch=64 if k_ref.shape[0]%64==0 else 48
    b=meta[AT+stage]
    def body(i,_):
        r=pl.multiple_of(i*ch,16)
        for ref,at in ((k_ref,b*h),(s_ref,(1-b)*h)):
            src=pl.multiple_of(at+r,16)
            ref[pl.ds(r,ch),:]=(keep_ref[pl.ds(src,ch),:].astype(f32)+got_ref[pl.ds(src,ch),:].astype(f32)).astype(bf16)
        return 0
    lax.fori_loop(0,h//ch,body,0)

def fold(meta, stage, keep, got):
    h=keep.shape[0]//2; sd=jax.ShapeDtypeStruct((h,keep.shape[1]),keep.dtype)
    def kernel(meta_ref, keep_ref, got_ref, k_ref, s_ref):
        fold_kernel(stage, meta_ref, keep_ref, got_ref, k_ref, s_ref)
    return pl.pallas_call(kernel,in_specs=[SM,VM,VM],out_specs=[VM,VM],out_shape=[sd,sd],cost_estimate=cost(1.0),
        compiler_params=pltpu.CompilerParams(vmem_limit_bytes=16*2**20),name="fold")(meta,keep,got)

def add_low(x,y):
    return (x.astype(f32)+y.astype(f32)).astype(bf16)

def place(meta, mine_ref, other_ref, buf_ref, sems, chunks):
    side=meta[7]
    rows=mine_ref.shape[0]//chunks
    copies=[]
    for i in range(chunks):
        for k,ref in enumerate((mine_ref,other_ref)):
            half=side if k==0 else 1-side
            at=lax.bitwise_xor(meta[AT+4+k],jnp.int32(i))
            copies.append(pltpu.make_async_copy(ref.at[pl.ds(i*rows,rows),:],
                buf_ref.at[half,pl.ds(pl.multiple_of(at*rows,16),rows),:],sems.at[i,k]))
    for c in copies:
        c.start()
    for c in copies:
        c.wait()

def unpack_a_kernel(chunks, meta, mine_ref, other_ref, gout_ref, gin_ref, gwo_ref, buf_ref, sems):
    place(meta,mine_ref,other_ref,buf_ref,sems,chunks)
    a=buf_ref.shape[2]; g,go,_=gout_ref.shape; ch=128
    per=go//a
    def body(i,_):
        r=pl.multiple_of(i*ch,ch)
        for h in range(g):
            for c in range(per):
                gout_ref[h,pl.ds(pl.multiple_of(c*a+r,ch),ch),:]=buf_ref[h,pl.ds(pl.multiple_of(c*a+r,ch),ch),:].astype(f32)
                gin_ref[h,pl.ds(r,ch),c*a:(c+1)*a]=buf_ref[h,pl.ds(pl.multiple_of((per+c)*a+r,ch),ch),:].astype(f32)
            for c in range(gwo_ref.shape[1]//a):
                gwo_ref[pl.ds(pl.multiple_of(h*a+r,ch),ch),c*a:(c+1)*a]=buf_ref[h,pl.ds(pl.multiple_of((2*per+c)*a+r,ch),ch),:].astype(f32)
        return 0
    lax.fori_loop(0,a//ch,body,0)

ANYS=pl.BlockSpec(memory_space=pl.ANY)
def unpack_a(meta, mine, other, g, gi, go, d, chunks):
    sd=jax.ShapeDtypeStruct
    def kernel(*refs):
        unpack_a_kernel(chunks,*refs)
    return pl.pallas_call(kernel,in_specs=[SM,ANYS,ANYS],out_specs=[VM]*3,
        out_shape=[sd((g,go,gi),f32),sd((g,gi,go),f32),sd((d,d),f32)],cost_estimate=cost(20.0),
        scratch_shapes=[pltpu.VMEM((2,)+mine.shape,bf16),pltpu.SemaphoreType.DMA((chunks,2))],
        compiler_params=pltpu.CompilerParams(vmem_limit_bytes=20*2**20),name="unpack_a")(meta,mine,other)

def unpack_b_kernel(chunks, which, meta, part_ref, q_ref, k_ref, v_ref, c_ref, p_ref, ck_ref, small_ref, buf_ref, sems, outs):
    a=buf_ref.shape[1]; rows=part_ref.shape[0]//chunks
    h=meta[7] if which==0 else 1-meta[7]
    copies=[]
    for i in range(chunks):
        at=lax.bitwise_xor(meta[AT+4+which],jnp.int32(i))
        copies.append(pltpu.make_async_copy(part_ref.at[pl.ds(i*rows,rows),:],
            buf_ref.at[pl.ds(pl.multiple_of(at*rows,16),rows),:],sems.at[i]))
    for x in copies:
        x.start()
    for x in copies:
        x.wait()
    backs=[]
    for i,ref in enumerate((q_ref,k_ref,v_ref,c_ref,p_ref)):
        outs[i]=buf_ref[i*a:(i+1)*a,:].astype(f32)
        x=pltpu.make_async_copy(outs.at[i],ref.at[pl.ds(pl.multiple_of(h*a,128),a),:],sems.at[chunks+i])
        x.start()
        backs.append(x)
    r=lax.broadcasted_iota(jnp.int32,(LAST,HEADS*TAPS),0)
    c=lax.broadcasted_iota(jnp.int32,(LAST,HEADS*TAPS),1)
    spread=jnp.where(r==(c//TAPS)*16+c%TAPS,1.0,0.0).astype(bf16)
    ck_ref[...]=dot_tn(buf_ref[5*a:5*a+LAST,:],spread)
    small_ref[:,:a]=buf_ref[5*a:5*a+16,:].astype(f32)
    small_ref[:,a:]=buf_ref[5*a+16:5*a+32,:].astype(f32)
    for x in backs:
        x.wait()

def unpack_b(meta, which, part, d, a, chunks, carry):
    sd=jax.ShapeDtypeStruct
    def kernel(meta_ref, part_ref, *refs):
        unpack_b_kernel(chunks,which,meta_ref,part_ref,*refs[-10:])
    carry=() if carry is None else tuple(carry)
    return pl.pallas_call(kernel,in_specs=[SM,ANYS]+[ANYS]*len(carry),out_specs=[ANYS]*5+[VM]*2,
        out_shape=[sd((d,a),f32)]*5+[sd((a,HEADS*TAPS),f32),sd((16,d),f32)],cost_estimate=cost(4.0),
        input_output_aliases={2+i:i for i in range(len(carry))},
        scratch_shapes=[pltpu.VMEM(part.shape,bf16),pltpu.SemaphoreType.DMA((chunks+5,)),pltpu.VMEM((5,a,a),f32)],
        compiler_params=pltpu.CompilerParams(vmem_limit_bytes=12*2**20),name="unpack_b")(meta,part,*carry)

class Reduce:
    def __init__(self, meta, keep, send, rows, scatter):
        self.meta=meta; self.rows=rows
        self.stages,self.whole=stage_bits(rows,scatter)
        self.keep=keep
        self.got=lax.ppermute(send,"seq",swap_pairs())
        self.step=0
        self.axes=("rows","seq")
    def advance(self):
        n=len(self.stages); w=len(self.whole); k=self.step; self.step+=1
        self.last=k==2*n+w
        if k<n:
            self.keep,send=fold(self.meta,k,self.keep,self.got)
            self.got=lax.ppermute(send,self.axes,row_pairs(self.rows,self.stages[k]))
        elif k<n+w:
            self.keep=add_low(self.keep,self.got)
            b=self.whole[k-n]
            self.got=lax.ppermute(self.keep,self.axes,row_pairs(self.rows,(b,b)))
        elif k==n+w+n+1:
            self.other=self.got
            self.got=None
        else:
            self.keep=add_low(self.keep,self.got) if k==n+w else jnp.concatenate([self.keep,self.got],axis=0)
            m=2*n+w-1-k
            if m>=0:
                self.got=lax.ppermute(self.keep,self.axes,row_pairs(self.rows,self.stages[m]))
            else:
                self.got=lax.ppermute(self.keep,"seq",swap_pairs())
    def after(self, arrays):
        self.got,arrays=lax.optimization_barrier((self.got,tuple(arrays)))
        self.advance()
        self.keep,arrays=lax.optimization_barrier((self.keep,arrays))
        return arrays
    def follow(self, other):
        self.got,other.keep=lax.optimization_barrier((self.got,other.keep))
        self.advance()
    def finish(self):
        while self.got is not None:
            self.advance()
        return self.keep,self.other,2**len(self.stages)

def per_device(hidden_in,doc_lengths,out_grad,w_query,w_key,w_value,w_conv_out,depth_kernel,w_point,w_conv_kernel,
               w_output,ln1_gain,ln1_bias,w_ffn_in,w_ffn_out,ln2_gain,ln2_bias):
    row_count,local,d=hidden_in.shape
    a=w_query.shape[1]
    half=local//2
    rows=lax.axis_size("rows")
    side=lax.axis_index("seq")
    row=lax.axis_index("rows")
    hid=hidden_in[0]
    meta=jnp.concatenate([make_meta(doc_lengths[0],side,local,local*2),comm_meta(side,row,rows)])
    halo=lax.ppermute(lax.dynamic_slice_in_dim(hid,(1-side)*half,half,0),"seq",swap_pairs())
    q,kw,vw,cx,depth,ck,kern,cm=pre(meta,hid,halo,w_query,w_key,w_value,w_conv_out,depth_kernel,w_point,w_conv_kernel)
    ctx,lse=attn_fwd(meta,q,kw,vw)
    ln=jnp.stack([ln1_gain,ln1_bias,ln2_gain,ln2_bias]).astype(f32)
    ho,dres,dctx,dconv,keep,send,gln=ffn(meta,hid,ctx,cm,out_grad[0],w_output,w_ffn_in,w_ffn_out,ln)
    g,gi,go=w_ffn_in.shape
    ra=Reduce(meta,keep,send,rows,3)
    carry=attn_bwd(meta,2,1,q,kw,vw,ctx,dctx,lse,None)
    out=ra.after(tuple(carry)+(dconv,))
    carry,dconv=out[:4],out[4]
    dqc,dc,dda,ddb,rimc,gp=conv_back(meta,dconv,cm,kern,cx,q,ck,depth,w_point,w_conv_kernel)
    rimc=lax.ppermute(rimc,"seq",swap_pairs())
    out=ra.after(tuple(carry)+(dqc,dda))
    carry,dqc,dda=out[:4],out[4],out[5]
    dqa,dk,dv,dkv=attn_bwd(meta,0,2,q,kw,vw,ctx,dctx,lse,carry)
    dkv=lax.ppermute(dkv,"seq",swap_pairs())
    dda,dqa=ra.after((dda,dqa))
    dha,rima,gta=taps_back(meta,0,hid,halo,dda,depth_kernel)
    ddb,dha=ra.after((ddb,dha))
    dhb,rimb,gtb=taps_back(meta,1,hid,halo,ddb,depth_kernel)
    rima=lax.ppermute(rima,"seq",swap_pairs())
    rimb=lax.ppermute(rimb,"seq",swap_pairs())
    dp,keep,send=proj_back(meta,hid,dqa,dqc,dk,dv,dkv,dc,rimc,gp,gta,gtb,gln)
    rb=Reduce(meta,keep,send,rows,3)
    grad_in=grad_input(meta,dp,dres,dha,dhb,rima,rimb,w_query,w_key,w_value,w_conv_out)
    (grad_in,)=rb.after((grad_in,))
    for one,two in ((rb,ra),(ra,rb),(rb,ra),(ra,rb),(rb,ra),(ra,rb),(rb,ra),(rb,ra),(rb,ra),(ra,rb),(ra,rb)):
        one.follow(two)
    mine,other,chunks=ra.finish()
    ffn_out_grad,ffn_in_grad,output_grad=unpack_a(meta,mine,other,g,gi,go,d,chunks)
    ffn_in_grad,ffn_out_grad,output_grad=rb.after((ffn_in_grad,ffn_out_grad,output_grad))
    while not rb.last:
        rb.advance()
    first=unpack_b(meta,0,rb.keep,d,a,chunks,None)
    first,got=lax.optimization_barrier((tuple(first),rb.got))
    second=unpack_b(meta,1,got,d,a,chunks,first[:5])
    q_grad,k_grad,v_grad,c_grad,point_grad=second[:5]
    ck_grad=jnp.where(side==0,first[5],second[5])
    small=jnp.where(side==1,first[6],second[6])
    lng=small[KSIZE:KSIZE+4]
    return (ho[None],grad_in[None],q_grad,k_grad,v_grad,c_grad,small[:KSIZE],point_grad,ck_grad,output_grad,
            lng[0],lng[1],ffn_in_grad,ffn_out_grad,lng[2],lng[3])


def solution(mesh):
    placed=(P("rows","seq",None),P("rows",None),P("rows","seq",None))+(P(),)*14
    return jax.shard_map(per_device,mesh=mesh,in_specs=placed,
        out_specs=(P("rows","seq",None),P("rows","seq",None))+(P(),)*14,check_vma=False)
```

```python
import jax
import jax.numpy as jnp
from jax import lax
from jax.experimental import pallas as pl
from jax.experimental.pallas import tpu as pltpu
from jax.sharding import PartitionSpec as P

KSIZE = 9

HEADS=6
BLK=256
NEG=-1e30
f32=jnp.float32; bf16=jnp.bfloat16

def dot_nt(a,b):
    return lax.dot_general(a,b,(((1,),(1,)),((),())),preferred_element_type=f32)
def dot_nn(a,b):
    return lax.dot_general(a,b,(((1,),(0,)),((),())),preferred_element_type=f32)
def dot_tn(a,b):
    return lax.dot_general(a,b,(((0,),(0,)),((),())),preferred_element_type=f32)

def segs(meta, first, shape):
    pos=first+lax.broadcasted_iota(jnp.int32,shape,0)
    seg=jnp.zeros(shape,jnp.int32)
    for d in range(5):
        seg=seg+jnp.where(pos>=meta[d],1,0)
    return seg

def key_ext(meta, first, n):
    lane=lax.broadcasted_iota(jnp.int32,(n,128),1)
    seg=segs(meta,first,(n,128))
    diff=(lane>=24)&(lane<30)&(lane-24!=seg)
    return jnp.where(lane<24,-1.0,jnp.where(diff,NEG,0.0)).astype(bf16)

def fwd_kernel(meta, q_ref, k_ref, v_ref, ctx_ref, lse_ref, kx_ref, s_ref, m_ref, acc_ref):
    nkb=k_ref.shape[0]//BLK; nqb=q_ref.shape[0]//BLK; npair=HEADS//2
    for b in range(nkb):
        kx_ref[b*BLK:(b+1)*BLK,:]=key_ext(meta,meta[5]+b*BLK,BLK)
    lane=lax.broadcasted_iota(jnp.int32,(BLK,128),1)
    ones_lane=jnp.where(lane==0,1.0,0.0).astype(bf16)
    for qb in range(nqb):
        qrows=slice(qb*BLK,(qb+1)*BLK)
        seg=segs(meta,meta[6]+qb*BLK,(BLK,128))
        qext=jnp.where(lane-24==seg,1.0,0.0).astype(bf16)
        lo=meta[8+2*qb]; hi=meta[9+2*qb]
        m_ref[...]=jnp.full(m_ref.shape,NEG,f32)
        acc_ref[...]=jnp.zeros(acc_ref.shape,f32)
        def phase1(kb,_):
            r0=pl.multiple_of(kb*BLK,BLK)
            kext=kx_ref[pl.ds(r0,BLK),:]
            for j in range(npair):
                kk=jnp.concatenate([k_ref[pl.ds(r0,BLK),j*128:(j+1)*128],kext],axis=1)
                qp=q_ref[qrows,j*128:(j+1)*128]*jnp.asarray(0.125,bf16)
                for hh in range(2):
                    h=2*j+hh
                    qm=jnp.where((lane<64) if hh==0 else (lane>=64),qp,jnp.zeros_like(qp))
                    s=dot_nt(jnp.concatenate([qm,qext],axis=1),kk)
                    s_ref[h,:,pl.ds(r0,BLK)]=s
                    m_ref[h]=jnp.maximum(m_ref[h],jnp.maximum(s[:,:128],s[:,128:]))
            return 0
        lax.fori_loop(lo,hi,phase1,0)
        for h in range(HEADS):
            m_ref[h]=jnp.broadcast_to(jnp.max(m_ref[h],axis=1,keepdims=True),(BLK,128))
        def phase2(kb,_):
            r0=pl.multiple_of(kb*BLK,BLK)
            for j in range(npair):
                vv=jnp.concatenate([v_ref[pl.ds(r0,BLK),j*128:(j+1)*128],ones_lane],axis=1)
                for hh in range(2):
                    h=2*j+hh
                    mm=m_ref[h]
                    p=jnp.exp(s_ref[h,:,pl.ds(r0,BLK)]-jnp.concatenate([mm,mm],axis=1)).astype(bf16)
                    acc_ref[h]=acc_ref[h]+dot_nn(p,vv)
            return 0
        lax.fori_loop(lo,hi,phase2,0)
        lse_all=jnp.zeros((BLK,128),f32)
        for j in range(npair):
            parts=[]
            for hh in range(2):
                h=2*j+hh
                l=jnp.broadcast_to(acc_ref[h][:,128:129],(BLK,128))
                parts.append(acc_ref[h][:,:128]/l)
                lse=m_ref[h]+jnp.log(l)
                sel=(lane==h)|(lane==h+8)|(lane==h+16)
                lse_all=jnp.where(sel,lse,lse_all)
            ctx_ref[qrows,j*128:(j+1)*128]=jnp.where(lane<64,parts[0],parts[1]).astype(ctx_ref.dtype)
        lse_ref[qrows,:]=lse_all

def bwd_kernel(head, meta, q_ref, k_ref, v_ref, ctx_ref, dctx_ref, lse_ref, dq_ref, dko_ref, dvo_ref, dkv_ref, kx_ref, dk_ref, dv_ref):
    nkb=k_ref.shape[0]//BLK; nqb=q_ref.shape[0]//BLK; npair=q_ref.shape[1]//128
    width=q_ref.shape[1]
    for b in range(nkb):
        kx_ref[b*BLK:(b+1)*BLK,:]=key_ext(meta,meta[5]+b*BLK,BLK)
    dk_ref[...]=jnp.zeros(dk_ref.shape,f32)
    dv_ref[...]=jnp.zeros(dv_ref.shape,f32)
    dq_ref[...]=jnp.zeros(dq_ref.shape,f32)
    lane=lax.broadcasted_iota(jnp.int32,(BLK,128),1)
    vext=jnp.where(lane<16,-1.0,0.0).astype(bf16)
    r=head+lax.broadcasted_iota(jnp.int32,(width,128),0)//64
    cl=lax.broadcasted_iota(jnp.int32,(width,128),1)
    heads_of=jnp.where((cl<16)&(cl%8==r),1.0,0.0).astype(bf16)
    low=lane<64
    for qb in range(nqb):
        qrows=slice(qb*BLK,(qb+1)*BLK)
        seg=segs(meta,meta[6]+qb*BLK,(BLK,128))
        onehot=lane-24==seg
        lse=lse_ref[qrows,:]
        hi_=lse.astype(bf16).astype(f32)
        r1=lse-hi_
        mid=r1.astype(bf16).astype(f32)
        lo_=r1-mid
        split=jnp.where(lane<8,hi_,jnp.where(lane<16,mid,lo_))
        prod=ctx_ref[qrows,:].astype(f32)*dctx_ref[qrows,:].astype(f32)
        ph=prod.astype(bf16)
        plo=(prod-ph.astype(f32)).astype(bf16)
        dd=dot_nn(ph,heads_of)+dot_nn(plo,heads_of)
        dh=dd.astype(bf16).astype(f32)
        dsplit=jnp.where(lane<8,dh,dd-dh)
        qx=[];dcx=[];qms=[];dcs=[]
        for h in range(head,head+2*npair):
            j=(h-head)//2
            side=low if h%2==0 else ~low
            qp=q_ref[qrows,j*128:(j+1)*128]*jnp.asarray(0.125,bf16)
            qm=jnp.where(side,qp,jnp.zeros_like(qp))
            sel=(lane==h)|(lane==h+8)|(lane==h+16)
            qe=jnp.where(sel,split,jnp.where(onehot,1.0,0.0)).astype(bf16)
            qx.append(jnp.concatenate([qm,qe],axis=1))
            dp=dctx_ref[qrows,j*128:(j+1)*128]
            dm=jnp.where(side,dp,jnp.zeros_like(dp))
            de=jnp.where((lane==h)|(lane==h+8),dsplit,0.0).astype(bf16)
            dcx.append(jnp.concatenate([dm,de],axis=1))
            qms.append(qm);dcs.append(dm)
        lo=meta[8+2*qb]; hi=meta[9+2*qb]
        def body(kb,_):
            r0=pl.multiple_of(kb*BLK,BLK)
            kext=kx_ref[pl.ds(r0,BLK),:]
            for j in range(npair):
                cols=slice(j*128,(j+1)*128)
                kp=k_ref[pl.ds(r0,BLK),cols]
                kk=jnp.concatenate([kp,kext],axis=1)
                vv=jnp.concatenate([v_ref[pl.ds(r0,BLK),cols],vext],axis=1)
                pts=[];dss=[];ks=[]
                for hh in range(2):
                    h=2*j+hh
                    pt=jnp.exp(dot_nt(kk,qx[h]))
                    dpt=dot_nt(vv,dcx[h])
                    pts.append(pt.astype(bf16))
                    dss.append((pt*dpt).astype(bf16))
                    ks.append(jnp.where(low if hh==0 else ~low,kp,jnp.zeros_like(kp)))
                dv_ref[pl.ds(r0,BLK),cols]+=dot_nn(jnp.concatenate(pts,axis=1),jnp.concatenate(dcs[2*j:2*j+2],axis=0))
                dk_ref[pl.ds(r0,BLK),cols]+=dot_nn(jnp.concatenate(dss,axis=1),jnp.concatenate(qms[2*j:2*j+2],axis=0))
                dq_ref[qrows,cols]+=dot_tn(jnp.concatenate(dss,axis=0),jnp.concatenate(ks,axis=0))
            return 0
        lax.fori_loop(lo,hi,body,0)
        dq_ref[qrows,:]=dq_ref[qrows,:]*0.125
    n=q_ref.shape[0]; half=dkv_ref.shape[0]
    own_off=meta[7]*half; halo_off=(1-meta[7])*n
    for b in range(n//BLK):
        src=pl.multiple_of(own_off+b*BLK,BLK)
        dko_ref[b*BLK:(b+1)*BLK,:]=dk_ref[pl.ds(src,BLK),:]
        dvo_ref[b*BLK:(b+1)*BLK,:]=dv_ref[pl.ds(src,BLK),:]
    for b in range(half//BLK):
        src=pl.multiple_of(halo_off+b*BLK,BLK)
        for j in range(npair):
            dkv_ref[b*BLK:(b+1)*BLK,j*256:j*256+128]=dk_ref[pl.ds(src,BLK),j*128:(j+1)*128].astype(bf16)
            dkv_ref[b*BLK:(b+1)*BLK,j*256+128:(j+1)*256]=dv_ref[pl.ds(src,BLK),j*128:(j+1)*128].astype(bf16)

VM=pl.BlockSpec(memory_space=pltpu.VMEM)
SM=pl.BlockSpec(memory_space=pltpu.SMEM)
def attn_fwd(meta,q,k,v):
    t,w=q.shape
    return pl.pallas_call(fwd_kernel,in_specs=[SM,VM,VM,VM],out_specs=[VM,VM],
        out_shape=[jax.ShapeDtypeStruct((t,w),bf16),jax.ShapeDtypeStruct((t,128),f32)],
        scratch_shapes=[pltpu.VMEM((k.shape[0],128),bf16),pltpu.VMEM((HEADS,BLK,k.shape[0]),f32),
            pltpu.VMEM((HEADS,BLK,128),f32),pltpu.VMEM((HEADS,BLK,256),f32)],
        compiler_params=pltpu.CompilerParams(vmem_limit_bytes=20*2**20),cost_estimate=cost(15.0),name="attn_fwd")(meta,q,k,v)
def attn_bwd(meta,first,pairs,q,k,v,ctx,dctx,lse,carry):
    t,w=q.shape; kn=k.shape[0]; wide=128*pairs
    sd=jax.ShapeDtypeStruct
    def col(n,width):
        return pl.BlockSpec((n,width),lambda i:(0,first//pairs))
    def kernel(*refs):
        bwd_kernel(2*first,*refs[:7],*refs[-7:])
    carry=() if carry is None else tuple(carry)
    return pl.pallas_call(kernel,grid=(1,),
        in_specs=[SM,col(t,wide),col(kn,wide),col(kn,wide),col(t,wide),col(t,wide),pl.BlockSpec((t,128),lambda i:(0,0))]+[pl.BlockSpec(memory_space=pl.ANY)]*len(carry),
        out_specs=[col(t,wide)]*3+[col(kn-t,2*wide)],
        out_shape=[sd((t,w),f32)]*3+[sd((kn-t,2*w),bf16)],
        scratch_shapes=[pltpu.VMEM((kn,128),bf16),pltpu.VMEM((kn,wide),f32),pltpu.VMEM((kn,wide),f32)],
        input_output_aliases={7+i:i for i in range(len(carry))},cost_estimate=cost(9.0*pairs),
        compiler_params=pltpu.CompilerParams(vmem_limit_bytes=(16+4*pairs)*2**20),name="attn_bwd")(meta,q,k,v,ctx,dctx,lse,*carry)

def make_meta(lengths, side, local, full):
    ends=jnp.cumsum(lengths)
    starts=ends-lengths
    win=side*(local//2); own=side*local
    nqb=local//BLK
    b0=own+jnp.arange(nqb)*BLK
    b1=b0+BLK-1
    bounds_lo=jnp.concatenate([jnp.zeros((1,),jnp.int32),ends])
    bounds_hi=jnp.concatenate([ends,jnp.full((1,),full,jnp.int32)])
    seg0=jnp.sum((b0[:,None]>=ends[None]).astype(jnp.int32),1)
    seg1=jnp.sum((b1[:,None]>=ends[None]).astype(jnp.int32),1)
    first=jnp.sum(jnp.where(jnp.arange(6)[None]==seg0[:,None],bounds_lo[None],0),1)
    last=jnp.sum(jnp.where(jnp.arange(6)[None]==seg1[:,None],bounds_hi[None],0),1)
    lo=jnp.maximum(first-win,0)//BLK
    hi=jnp.minimum((last-win+BLK-1)//BLK,(local+local//2)//BLK)
    return jnp.concatenate([ends,win[None],own[None],side[None],jnp.stack([lo,hi],1).reshape(-1)]).astype(jnp.int32)


TB=256

def gelu_parts(z):
    a=jnp.abs(z)
    t=1.0/(1.0+a*(0.3275911*0.7071067811865476))
    e=jnp.exp(-0.5*z*z)
    poly=t*(0.127414796+t*(-0.142248368+t*(0.7107068705+t*(-0.7265760135+t*0.5307027145))))
    ht=poly*e
    phi=jnp.where(z>=0.0,1.0-ht,ht)
    return z*phi, phi+z*(e*0.3989422804014327)

def rows8(x):
    return jnp.sum(x.reshape(x.shape[0]//8,8,x.shape[1]),axis=0)

def norm_parts(z):
    mu=jnp.mean(z,axis=-1,keepdims=True)
    c=z-mu
    var=jnp.mean(c*c,axis=-1,keepdims=True)
    rstd=lax.rsqrt(var+1e-6)
    return c*rstd, rstd

def norm_back(d, gain, xhat, rstd):
    dx=d*gain
    a=jnp.mean(dx,axis=-1,keepdims=True)
    b=jnp.mean(dx*xhat,axis=-1,keepdims=True)
    return rstd*(dx-a-xhat*b)

def ffn_kernel(meta, hid_ref, ctx_ref, cm_ref, og_ref, wo_ref, win_ref, wout_ref, ln_ref,
               ho_ref, dres_ref, dctx_ref, dconv_ref, keep_ref, send_ref, gln_ref,
               act_ref, dff_ref, x1_ref, dfo_ref, datt_ref, mix_ref):
    n=hid_ref.shape[0]; d=hid_ref.shape[1]; groups=win_ref.shape[0]; gi=d//groups; go=win_ref.shape[2]
    attn=dctx_ref.shape[1]
    tile=512
    gln_ref[...]=jnp.zeros(gln_ref.shape,f32)
    def block(i,_):
        r0=pl.multiple_of(i*TB,TB)
        rows=pl.ds(r0,TB)
        g1=ln_ref[0:1,:];b1=ln_ref[1:2,:];g2=ln_ref[2:3,:];b2=ln_ref[3:4,:]
        att=dot_nn(jnp.concatenate([ctx_ref[rows,:],cm_ref[rows,:]],axis=1),wo_ref[...])
        xhat1,rstd1=norm_parts(hid_ref[rows,:].astype(f32)+att)
        first=xhat1*g1+b1
        x1=first.astype(bf16)
        for g in range(groups):
            x1_ref[g,rows,:]=x1[:,g*gi:(g+1)*gi]
        mix_ref[0,rows,:]=ctx_ref[rows,:]
        mix_ref[1,rows,:]=cm_ref[rows,:]
        tiles=[(g,c) for g in range(groups) for c in range(go//tile)]
        def up(g,c):
            return dot_nn(x1[:,g*gi:(g+1)*gi],win_ref[g,:,c*tile:(c+1)*tile])
        outs=[None]*groups
        ahead=up(*tiles[0])
        for t,(g,c) in enumerate(tiles):
            z=ahead
            if t+1<len(tiles):
                ahead=up(*tiles[t+1])
            cols=slice(c*tile,(c+1)*tile)
            a,gp=gelu_parts(z)
            ab=a.astype(bf16)
            act_ref[g,rows,cols]=ab
            dff_ref[g,rows,cols]=gp.astype(bf16)
            o=dot_nn(ab,wout_ref[g,cols,:])
            outs[g]=o if outs[g] is None else outs[g]+o
        xhat2,rstd2=norm_parts(first+jnp.concatenate(outs,axis=1))
        pos=meta[6]+r0+lax.broadcasted_iota(jnp.int32,(TB,d),0)
        valid=pos<meta[4]
        ho_ref[rows,:]=jnp.where(valid,xhat2*g2+b2,0.0).astype(bf16)
        gn=jnp.where(valid,og_ref[rows,:].astype(f32),0.0)
        gln_ref[16:24,:]+=rows8(gn*xhat2)
        gln_ref[24:32,:]+=rows8(gn)
        dres2=norm_back(gn,g2,xhat2,rstd2)
        dfo=dres2.astype(bf16)
        for g in range(groups):
            dfo_ref[g,rows,:]=dfo[:,g*gi:(g+1)*gi]
        def down(g,c):
            return dot_nt(dfo[:,g*gi:(g+1)*gi],wout_ref[g,c*tile:(c+1)*tile,:])
        backs=[None]*groups
        ahead=down(*tiles[0])
        for t,(g,c) in enumerate(tiles):
            da=ahead
            if t+1<len(tiles):
                ahead=down(*tiles[t+1])
            cols=slice(c*tile,(c+1)*tile)
            dh=(da*dff_ref[g,rows,cols].astype(f32)).astype(bf16)
            dff_ref[g,rows,cols]=dh
            o=dot_nt(dh,win_ref[g,:,cols])
            backs[g]=o if backs[g] is None else backs[g]+o
        dfirst=dres2+jnp.concatenate(backs,axis=1)
        gln_ref[0:8,:]+=rows8(dfirst*xhat1)
        gln_ref[8:16,:]+=rows8(dfirst)
        dres1=norm_back(dfirst,g1,xhat1,rstd1)
        dres_ref[rows,:]=dres1
        datt=dres1.astype(bf16)
        datt_ref[rows,:]=datt
        dm=dot_nt(datt,wo_ref[...])
        dctx_ref[rows,:]=dm[:,:attn].astype(bf16)
        dconv_ref[rows,:]=dm[:,attn:]
        return 0
    lax.fori_loop(0,n//TB,block,0)
    side=meta[7]
    for ref,g in ((send_ref,1-side),(keep_ref,side)):
        at=0
        for c in range(go//gi):
            ref[at*gi:(at+1)*gi,:]=dot_tn(act_ref[g,:,c*gi:(c+1)*gi],dfo_ref[g]).astype(ref.dtype)
            at+=1
        wide=dot_tn(x1_ref[g],dff_ref[g]).astype(ref.dtype)
        for c in range(go//gi):
            ref[at*gi:(at+1)*gi,:]=wide[:,c*gi:(c+1)*gi]
            at+=1
        for c in range(d//attn):
            ref[at*gi:(at+1)*gi,:]=dot_tn(mix_ref[g],datt_ref[:,c*attn:(c+1)*attn]).astype(ref.dtype)
            at+=1

def ffn(meta,hid,ctx,cm,og,wo,win,wout,ln):
    n,d=hid.shape; g,gi,go=win.shape; attn=ctx.shape[1]
    sd=jax.ShapeDtypeStruct
    return pl.pallas_call(ffn_kernel,in_specs=[SM]+[VM]*8,out_specs=[VM]*7,
        out_shape=[sd((n,d),bf16),sd((n,d),f32),sd((n,attn),bf16),sd((n,attn),f32),
                   sd((2*go+d,attn),bf16),sd((2*go+d,attn),bf16),sd((32,d),f32)],
        scratch_shapes=[pltpu.VMEM((g,n,go),bf16),pltpu.VMEM((g,n,go),bf16),pltpu.VMEM((g,n,gi),bf16),
                        pltpu.VMEM((g,n,gi),bf16),pltpu.VMEM((n,d),bf16),pltpu.VMEM((2,n,attn),bf16)],
        cost_estimate=cost(40.0),compiler_params=pltpu.CompilerParams(vmem_limit_bytes=38*2**20),name="ffn")(meta,hid,ctx,cm,og,wo,win,wout,ln)

TAPS=9
HALF=4
PAD=8
TB=256
CH=64
CS=32
LAST=128

def doc_bounds(meta, first, shape):
    pos=first+lax.broadcasted_iota(jnp.int32,shape,0)
    nxt=jnp.full(shape,2**30,jnp.int32)
    prv=jnp.full(shape,-2**30,jnp.int32)
    for d in range(5):
        e=meta[d]
        nxt=jnp.minimum(nxt,jnp.where(e>pos,e,2**30))
        prv=jnp.maximum(prv,jnp.where(e<=pos,e,-2**30))
    return nxt-pos, pos-prv

def tap_mask(bounds, o):
    rem,age=bounds
    if o>HALF:
        return rem>(o-HALF)
    return age>=(HALF-o)

def masked(x, bounds, o):
    if o==HALF:
        return x
    return jnp.where(tap_mask(bounds,o),x,0.0)

def tap_onehot(rows, cols, o):
    r=lax.broadcasted_iota(jnp.int32,(rows,cols),0)
    c=lax.broadcasted_iota(jnp.int32,(rows,cols),1)
    return jnp.where(r==(c//64)*TAPS+o,1.0,0.0).astype(bf16)

def pre_kernel(meta, hid_ref, halo_ref, wq_ref, wk_ref, wv_ref, wc_ref, taps_ref, wp_ref, wck_ref,
               q_ref, kw_ref, vw_ref, cx_ref, depth_ref, ck_ref, kern_hbm, cm_ref,
               hx_ref, wx_ref, lx_ref, kern_ref, sems):
    n,d=hid_ref.shape; half=halo_ref.shape[0]; attn=q_ref.shape[1]
    side=meta[7]
    own_off=side*half; halo_off=(1-side)*n
    jt=attn//128; jd=d//128
    for o in range(TAPS):
        wx_ref[:,o*attn:(o+1)*attn]=dot_nn(wck_ref[...],tap_onehot(HEADS*TAPS,attn,o)).astype(bf16)
    left=jnp.where(side==1,halo_ref[half-16:half,:].astype(f32),0.0)
    right=jnp.where(side==0,halo_ref[0:16,:].astype(f32),0.0)
    rims=jnp.concatenate([left,right],axis=0).astype(bf16)
    crim=dot_nn(rims,wc_ref[...]).astype(bf16).astype(f32)
    for j in range(jd):
        hx_ref[j,0:PAD,:]=left[PAD:2*PAD,j*128:(j+1)*128]
        hx_ref[j,n+PAD:n+2*PAD,:]=right[0:PAD,j*128:(j+1)*128]
    for j in range(jt):
        cx_ref[j,0:PAD,:]=crim[PAD:2*PAD,j*128:(j+1)*128]
        cx_ref[j,n+PAD:n+2*PAD,:]=crim[16:16+PAD,j*128:(j+1)*128]
    def project(i,_):
        r0=pl.multiple_of(i*TB,TB)
        x=hid_ref[pl.ds(r0,TB),:]
        q_ref[pl.ds(r0,TB),:]=dot_nn(x,wq_ref[...]).astype(bf16)
        ow=pl.multiple_of(own_off+r0,TB)
        kw_ref[pl.ds(ow,TB),:]=dot_nn(x,wk_ref[...]).astype(bf16)
        vw_ref[pl.ds(ow,TB),:]=dot_nn(x,wv_ref[...]).astype(bf16)
        c=dot_nn(x,wc_ref[...]).astype(bf16).astype(f32)
        rp=pl.multiple_of(r0+PAD,PAD)
        for j in range(jt):
            cx_ref[j,pl.ds(rp,TB),:]=c[:,j*128:(j+1)*128]
        xf=x.astype(f32)
        for j in range(jd):
            hx_ref[j,pl.ds(rp,TB),:]=xf[:,j*128:(j+1)*128]
        return 0
    lax.fori_loop(0,n//TB,project,0)
    def project_halo(i,_):
        r0=pl.multiple_of(i*TB,TB)
        x=halo_ref[pl.ds(r0,TB),:]
        ow=pl.multiple_of(halo_off+r0,TB)
        kw_ref[pl.ds(ow,TB),:]=dot_nn(x,wk_ref[...]).astype(bf16)
        vw_ref[pl.ds(ow,TB),:]=dot_nn(x,wv_ref[...]).astype(bf16)
        return 0
    lax.fori_loop(0,half//TB,project_halo,0)
    def depthwise(i,_):
        r0=pl.multiple_of(i*CH,CH)
        bounds=doc_bounds(meta,meta[6]+r0,(CH,128))
        for j in range(jd):
            acc=None
            for o in range(TAPS):
                x=hx_ref[j,pl.ds(r0+PAD+o-HALF,CH),:]
                term=masked(x*taps_ref[o:o+1,j*128:(j+1)*128].astype(f32),bounds,o)
                acc=term if acc is None else acc+term
            depth_ref[pl.ds(r0,CH),j*128:(j+1)*128]=acc.astype(bf16)
        return 0
    lax.fori_loop(0,n//CH,depthwise,0)
    def dynamic(r0):
        ck=dot_nn(depth_ref[pl.ds(r0,TB),:],wp_ref[...])
        ck_ref[pl.ds(r0,TB),:]=ck
        mk=(ck*q_ref[pl.ds(r0,TB),:].astype(f32)).astype(bf16)
        for o in range(TAPS):
            lx_ref[o]=dot_nn(mk,wx_ref[:,o*attn:(o+1)*attn])
        def soft(s,_):
            s0=pl.multiple_of(s*CS,CS)
            rows=pl.ds(s0,CS)
            t0=pl.multiple_of(r0+s0,CS)
            bounds=doc_bounds(meta,meta[6]+t0,(CS,128))
            for j in range(jt):
                cols=slice(j*128,(j+1)*128)
                ls=[lx_ref[o,rows,cols] for o in range(TAPS)]
                m=ls[0]
                for o in range(1,TAPS):
                    m=jnp.maximum(m,ls[o])
                es=[jnp.exp(l-m) for l in ls]
                tot=es[0]
                for o in range(1,TAPS):
                    tot=tot+es[o]
                inv=1.0/tot
                acc=None
                for o in range(TAPS):
                    k=es[o]*inv
                    kern_ref[o,pl.ds(t0,CS),cols]=k.astype(bf16)
                    term=masked(k*cx_ref[j,pl.ds(t0+PAD+o-HALF,CS),:],bounds,o)
                    acc=term if acc is None else acc+term
                cm_ref[pl.ds(t0,CS),cols]=acc.astype(bf16)
            return 0
        lax.fori_loop(0,TB//CS,soft,0)
    stores=[]
    for b in range(n//TB):
        dynamic(b*TB)
        x=pltpu.make_async_copy(kern_ref.at[:,pl.ds(b*TB,TB),:],kern_hbm.at[:,pl.ds(b*TB,TB),:],sems.at[b])
        x.start()
        stores.append(x)
    for x in stores:
        x.wait()

def pre(meta,hid,halo,wq,wk,wv,wc,taps,wp,wck):
    n,d=hid.shape; half=halo.shape[0]; a=wq.shape[1]; sd=jax.ShapeDtypeStruct
    anys=pl.BlockSpec(memory_space=pl.ANY)
    def whole(*shape):
        return pl.BlockSpec(shape,lambda i:(0,)*len(shape))
    proj=whole(d,a)
    return pl.pallas_call(pre_kernel,grid=(1,),in_specs=[SM,whole(n,d),VM,proj,proj,proj,proj,VM,proj,VM],out_specs=[VM]*6+[anys,VM],
        out_shape=[sd((n,a),bf16),sd((n+half,a),bf16),sd((n+half,a),bf16),sd((a//128,n+2*PAD,128),f32),
                   sd((n,d),bf16),sd((n,a),f32),sd((TAPS,n,a),bf16),sd((n,a),bf16)],
        scratch_shapes=[pltpu.VMEM((d//128,n+2*PAD,128),f32),pltpu.VMEM((a,TAPS*a),bf16),pltpu.VMEM((TAPS,TB,a),f32),
                        pltpu.VMEM((TAPS,n,a),bf16),pltpu.SemaphoreType.DMA((n//TB,))],
        cost_estimate=cost(30.0),compiler_params=pltpu.CompilerParams(vmem_limit_bytes=34*2**20),name="pre")(meta,hid,halo,wq,wk,wv,wc,taps,wp,wck)

def conv_back_kernel(meta, dconv_ref, cm_ref, kern_ref, cx_ref, q_ref, ck_ref, depth_ref,
                     wp_ref, wck_ref,
                     dqc_ref, dc_ref, dda_ref, ddb_ref, rimc_ref, gp_ref,
                     p_ref, pr_ref, dlc_ref, mk_ref, dck_ref, wcx_ref, dep_ref):
    d=depth_ref.shape[1]; attn,n=q_ref.shape[1],dc_ref.shape[0]
    i=pl.program_id(0)
    side=meta[7]; jt=attn//128; jd=d//128; hd=jd//2
    dds=[(dda_ref,j) if j<hd else (ddb_ref,j-hd) for j in range(jd)]
    @pl.when(i==0)
    def _():
        zero=jnp.zeros((2*PAD,128),f32)
        for j in range(jt):
            for o in range(TAPS):
                p_ref[o,j,0:2*PAD,:]=zero
                p_ref[o,j,n+2*PAD:n+4*PAD,:]=zero
        for ref,j in dds:
            ref[j,0:2*PAD,:]=zero
            ref[j,n+2*PAD:n+4*PAD,:]=zero
        r=lax.broadcasted_iota(jnp.int32,(HEADS*TAPS,attn),0)
        c=lax.broadcasted_iota(jnp.int32,(HEADS*TAPS,attn),1)
        spread=jnp.where((c%64<TAPS)&(r==(c//64)*TAPS+c%64),1.0,0.0).astype(bf16)
        wcx_ref[...]=dot_nn(wck_ref[...],spread).astype(bf16)
    def ones_block(w):
        return jnp.where(lax.broadcasted_iota(jnp.int32,(w,w),0)//64==lax.broadcasted_iota(jnp.int32,(w,w),1)//64,1.0,0.0).astype(bf16)
    ones256=ones_block(256); ones128=ones_block(128)
    lane=lax.broadcasted_iota(jnp.int32,(TB,attn),1)%64
    def dynamic():
        r0=pl.multiple_of(i*TB,TB)
        rows=pl.ds(r0,TB)
        def products(s,_):
            s0=pl.multiple_of(s*CS,CS)
            t0=pl.multiple_of(r0+s0,CS)
            bounds=doc_bounds(meta,meta[6]+t0,(CS,128))
            for j in range(jt):
                cols=slice(j*128,(j+1)*128)
                g=dconv_ref[pl.ds(s0,CS),cols]
                cm=cm_ref[pl.ds(s0,CS),cols].astype(f32)
                for o in range(TAPS):
                    cs=masked(cx_ref[j,pl.ds(t0+PAD+o-HALF,CS),:],bounds,o)
                    pr_ref[o,pl.ds(s0,CS),cols]=(g*(cs-cm)).astype(bf16)
                    p_ref[o,j,pl.ds(t0+2*PAD,CS),:]=masked(kern_ref[o,pl.ds(s0,CS),cols].astype(f32)*g,bounds,o)
            return 0
        lax.fori_loop(0,TB//CS,products,0)
        dl=jnp.zeros((TB,attn),f32)
        for o in range(TAPS):
            pr=pr_ref[o]
            dk=jnp.concatenate([dot_nn(pr[:,:256],ones256),dot_nn(pr[:,256:],ones128)],axis=1)
            dl=jnp.where(lane==o,kern_ref[o].astype(f32)*dk,dl)
        dlb=dl.astype(bf16)
        dlc_ref[rows,:]=dlb
        dmk=dot_nt(dlb,wcx_ref[...])
        dep_ref[rows,:]=depth_ref[...]
        q=q_ref[...].astype(f32)
        ck=ck_ref[...]
        mk_ref[rows,:]=(ck*q).astype(bf16)
        dqc_ref[...]=dmk*ck
        dck=(dmk*q).astype(bf16)
        dck_ref[rows,:]=dck
        dd=dot_nt(dck,wp_ref[...])
        rp=pl.multiple_of(r0+2*PAD,PAD)
        for j in range(jd):
            dds[j][0][dds[j][1],pl.ds(rp,TB),:]=dd[:,j*128:(j+1)*128]
    dynamic()
    @pl.when(i==pl.num_programs(0)-1)
    def _():
        def gather_c(row, size):
            out=[]
            for j in range(jt):
                acc=None
                for o in range(TAPS):
                    x=p_ref[o,j,pl.ds(row+PAD+HALF-o,size),:]
                    acc=x if acc is None else acc+x
                out.append(acc)
            return out
        def own_c(i,_):
            r0=pl.multiple_of(i*CS,CS)
            out=gather_c(r0+PAD,CS)
            for j in range(jt):
                dc_ref[pl.ds(r0,CS),j*128:(j+1)*128]=out[j]
            return 0
        lax.fori_loop(0,n//CS,own_c,0)
        left=gather_c(0,PAD); right=gather_c(n+PAD,PAD)
        for j in range(jt):
            rimc_ref[:,j*128:(j+1)*128]=jnp.where(side==1,left[j],right[j])
        for b in range(d//attn):
            gp_ref[b]=dot_tn(dep_ref[:,b*attn:(b+1)*attn],dck_ref[...]).astype(gp_ref.dtype)
        gp_ref[d//attn]=dot_tn(dlc_ref[...],mk_ref[...]).astype(gp_ref.dtype)

def taps_back_kernel(meta, hid_ref, halo_ref, dd_ref, taps_ref, dh_ref, rim_ref, gtap_ref):
    n,d=hid_ref.shape; half=halo_ref.shape[0]
    side=meta[7]; jd=d//128
    def gather_h(row, size, j, hx, bounds, sums):
        acc=None; new=[]
        for o in range(TAPS):
            x=masked(dd_ref[j,pl.ds(row+PAD+o-HALF,size),:],bounds,o)
            b=TAPS-1-o
            term=x*taps_ref[b:b+1,j*128:(j+1)*128].astype(f32)
            acc=term if acc is None else acc+term
            new.append(jnp.sum((x*hx).reshape(size//8,8,128),axis=0))
        return acc,[s+t for s,t in zip(sums,new)]
    lhalo=jnp.where(side==1,halo_ref[half-16:half,:].astype(f32),0.0)[PAD:2*PAD,:]
    rhalo=jnp.where(side==0,halo_ref[0:16,:].astype(f32),0.0)[0:PAD,:]
    for j in range(jd):
        cols=slice(j*128,(j+1)*128)
        sums=[jnp.zeros((8,128),f32) for _ in range(TAPS)]
        la,sums=gather_h(0,PAD,j,lhalo[:,cols],doc_bounds(meta,meta[6]-PAD,(PAD,128)),sums)
        ra,sums=gather_h(n+PAD,PAD,j,rhalo[:,cols],doc_bounds(meta,meta[6]+n,(PAD,128)),sums)
        rim_ref[:,cols]=jnp.where(side==1,la,ra)
        def own_h(i,sums):
            r0=pl.multiple_of(i*CS,CS)
            acc,sums=gather_h(r0+PAD,CS,j,hid_ref[pl.ds(r0,CS),cols].astype(f32),doc_bounds(meta,meta[6]+r0,(CS,128)),sums)
            dh_ref[pl.ds(r0,CS),cols]=acc
            return sums
        sums=lax.fori_loop(0,n//CS,own_h,sums)
        for o in range(TAPS):
            b=TAPS-1-o
            gtap_ref[b*8:(b+1)*8,cols]=sums[o]

def conv_back(meta,dconv,cm,kern,cx,q,ck,depth,wp,wck):
    n,d=depth.shape; a=q.shape[1]; sd=jax.ShapeDtypeStruct
    def row(w):
        return pl.BlockSpec((TB,w),lambda i:(i,0))
    def whole(*shape):
        return pl.BlockSpec(shape,lambda i:(0,)*len(shape))
    half=(d//256,n+4*PAD,128)
    return pl.pallas_call(conv_back_kernel,grid=(n//TB,),
        in_specs=[SM,row(a),row(a),pl.BlockSpec((TAPS,TB,a),lambda i:(0,i,0)),VM,row(a),row(a),row(d),VM,VM],
        out_specs=[row(a),whole(n,a),whole(*half),whole(*half),whole(PAD,a),whole(d//a+1,a,a)],
        out_shape=[sd((n,a),f32),sd((n,a),f32),sd(half,f32),sd(half,f32),sd((PAD,a),f32),sd((d//a+1,a,a),bf16)],
        scratch_shapes=[pltpu.VMEM((TAPS,a//128,n+4*PAD,128),f32),pltpu.VMEM((TAPS,TB,a),bf16),
                        pltpu.VMEM((n,a),bf16),pltpu.VMEM((n,a),bf16),pltpu.VMEM((n,a),bf16),pltpu.VMEM((a,a),bf16),pltpu.VMEM((n,d),bf16)],
        cost_estimate=cost(20.0),compiler_params=pltpu.CompilerParams(vmem_limit_bytes=48*2**20),name="conv_back")(meta,dconv,cm,kern,cx,q,ck,depth,wp,wck)

def taps_back(meta,part,hid,halo,dd,taps):
    n=hid.shape[0]; d=dd.shape[0]*128; sd=jax.ShapeDtypeStruct
    def col(rows):
        return pl.BlockSpec((rows,d),lambda i:(0,part))
    def whole(*shape):
        return pl.BlockSpec(shape,lambda i:(0,)*len(shape))
    return pl.pallas_call(taps_back_kernel,grid=(1,),in_specs=[SM,col(n),col(halo.shape[0]),whole(*dd.shape),col(TAPS)],
        out_specs=[whole(n,d),whole(PAD,d),whole(TAPS*8,d)],
        out_shape=[sd((n,d),f32),sd((PAD,d),f32),sd((TAPS*8,d),f32)],
        cost_estimate=cost(6.0),compiler_params=pltpu.CompilerParams(vmem_limit_bytes=24*2**20),name="taps_back")(meta,hid,halo,dd,taps)

def proj_back_kernel(meta, hid_ref, dqa_ref, dqc_ref, dk_ref, dv_ref, dkv_ref, dc_ref, rimc_ref, gp_ref, gta_ref, gtb_ref, gln_ref,
                     dp_ref, keep_ref, send_ref):
    n,d=hid_ref.shape; attn=dqa_ref.shape[1]; half=dkv_ref.shape[0]
    side=meta[7]
    shift=(1-side)*half
    def block(i,_):
        r0=pl.multiple_of(i*TB,TB)
        rows=pl.ds(r0,TB)
        inside=(r0>=shift)&(r0<shift+half)
        scale=jnp.where(inside,1.0,0.0)
        hr=pl.multiple_of(jnp.where(inside,r0-shift,0),TB)
        other=dkv_ref[pl.ds(hr,TB),:].astype(f32)*scale
        top=jnp.where((side==1)&(i==0),rimc_ref[...],0.0)
        bottom=jnp.where((side==0)&(i==n//TB-1),rimc_ref[...],0.0)
        rim=jnp.concatenate([top,jnp.zeros((TB-2*PAD,attn),f32),bottom],axis=0)
        dp_ref[rows,0:attn]=(dqa_ref[rows,:]+dqc_ref[rows,:]).astype(bf16)
        for j in range(attn//128):
            cols=slice(j*128,(j+1)*128)
            dp_ref[rows,attn+j*128:attn+(j+1)*128]=(dk_ref[rows,cols]+other[:,j*256:j*256+128]).astype(bf16)
            dp_ref[rows,2*attn+j*128:2*attn+(j+1)*128]=(dv_ref[rows,cols]+other[:,j*256+128:(j+1)*256]).astype(bf16)
        dp_ref[rows,3*attn:]=(dc_ref[rows,:]+rim).astype(bf16)
        return 0
    lax.fori_loop(0,n//TB,block,0)
    zeros=jnp.zeros((1,d),f32)
    small=[jnp.concatenate([jnp.sum(t[o*8:(o+1)*8,:],axis=0,keepdims=True) for t in (gta_ref,gtb_ref)],axis=1) for o in range(TAPS)]
    small+=[jnp.sum(gln_ref[k*8:(k+1)*8,:],axis=0,keepdims=True) for k in range(4)]
    small=jnp.concatenate(small+[zeros]*(16-len(small)),axis=0)
    for ref,h in ((send_ref,1-side),(keep_ref,side)):
        hc=pl.ds(pl.multiple_of(h*attn,128),attn)
        for k in range(4):
            ref[k*attn:(k+1)*attn,:]=dot_tn(hid_ref[:,hc],dp_ref[:,k*attn:(k+1)*attn]).astype(ref.dtype)
        ref[4*attn:5*attn,:]=gp_ref[h]
        @pl.when(h==0)
        def _():
            for k in range(HEADS):
                ref[5*attn+16*k:5*attn+16*(k+1),:]=gp_ref[2,64*k:64*k+16,:]
            ref[5*attn+16*HEADS:5*attn+LAST,:]=jnp.zeros((LAST-16*HEADS,attn),bf16)
        @pl.when(h==1)
        def _():
            ref[5*attn:5*attn+16,:]=small[:,:attn].astype(bf16)
            ref[5*attn+16:5*attn+32,:]=small[:,attn:].astype(bf16)
            ref[5*attn+32:5*attn+LAST,:]=jnp.zeros((LAST-32,attn),bf16)

def proj_back(meta,hid,dqa,dqc,dk,dv,dkv,dc,rimc,gp,gta,gtb,gln):
    n,d=hid.shape; a=dqa.shape[1]; sd=jax.ShapeDtypeStruct
    return pl.pallas_call(proj_back_kernel,in_specs=[SM]+[VM]*12,out_specs=[VM]*3,
        out_shape=[sd((n,4*a),bf16),sd((5*a+LAST,a),bf16),sd((5*a+LAST,a),bf16)],cost_estimate=cost(9.0),
        compiler_params=pltpu.CompilerParams(vmem_limit_bytes=16*2**20),name="proj_back")(meta,hid,dqa,dqc,dk,dv,dkv,dc,rimc,gp,gta,gtb,gln)

def grad_in_kernel(meta, dp_ref, dres_ref, dha_ref, dhb_ref, rima_ref, rimb_ref, wq_ref, wk_ref, wv_ref, wc_ref, gi_ref):
    n,d=gi_ref.shape; attn=wq_ref.shape[1]
    side=meta[7]
    def block(i,_):
        r0=pl.multiple_of(i*TB,TB)
        rows=pl.ds(r0,TB)
        acc=dres_ref[rows,:]+jnp.concatenate([dha_ref[rows,:],dhb_ref[rows,:]],axis=1)
        for k,w in enumerate((wq_ref,wk_ref,wv_ref,wc_ref)):
            acc=acc+dot_nt(dp_ref[rows,k*attn:(k+1)*attn],w[...])
        gi_ref[rows,:]=acc
        return 0
    lax.fori_loop(0,n//TB,block,0)
    at=pl.multiple_of((1-side)*(n-PAD),PAD)
    gi_ref[pl.ds(at,PAD),:]+=jnp.concatenate([rima_ref[...],rimb_ref[...]],axis=1)

def grad_input(meta,dp,dres,dha,dhb,rima,rimb,wq,wk,wv,wc):
    n,d=dres.shape; sd=jax.ShapeDtypeStruct
    return pl.pallas_call(grad_in_kernel,in_specs=[SM]+[VM]*10,out_specs=VM,
        out_shape=sd((n,d),f32),cost_estimate=cost(9.0),
        compiler_params=pltpu.CompilerParams(vmem_limit_bytes=16*2**20),name="grad_input")(meta,dp,dres,dha,dhb,rima,rimb,wq,wk,wv,wc)

AT=16

def swap_pairs():
    return [(0,1),(1,0)]

def stage_bits(size, scatter):
    bits=[]
    b=1
    while b<size:
        bits.append(b)
        b*=2
    lead=bits[:3]
    other=lead[-1:]+lead[:-1]+bits[3:]
    n=min(scatter,len(bits))
    return list(zip(bits,other))[:n],bits[n:]

def row_pairs(rows, bits):
    return [(r*2+s,(r^bits[s])*2+s) for r in range(rows) for s in range(2)]

def comm_meta(side, row, rows):
    stages,_=stage_bits(rows,4)
    own=[jnp.where(side==0,(row//b0)%2,(row//b1)%2) for b0,b1 in stages]
    oth=[jnp.where(side==0,(row//b1)%2,(row//b0)%2) for b0,b1 in stages]
    c=jnp.int32(0); c2=jnp.int32(0)
    for u,v in list(zip(own,oth))[:3]:
        c=c*2+u; c2=c2*2+v
    own=own+[jnp.int32(0)]*(4-len(own))
    return jnp.stack(own+[c,c2]).astype(jnp.int32)

def cost(us):
    return pl.CostEstimate(flops=int(us*1.0e9),bytes_accessed=0,transcendentals=0)

def fold_kernel(stage, meta, keep_ref, got_ref, k_ref, s_ref):
    h=k_ref.shape[0]; ch=64 if k_ref.shape[0]%64==0 else 48
    b=meta[AT+stage]
    def body(i,_):
        r=pl.multiple_of(i*ch,16)
        for ref,at in ((k_ref,b*h),(s_ref,(1-b)*h)):
            src=pl.multiple_of(at+r,16)
            ref[pl.ds(r,ch),:]=(keep_ref[pl.ds(src,ch),:].astype(f32)+got_ref[pl.ds(src,ch),:].astype(f32)).astype(bf16)
        return 0
    lax.fori_loop(0,h//ch,body,0)

def fold(meta, stage, keep, got):
    h=keep.shape[0]//2; sd=jax.ShapeDtypeStruct((h,keep.shape[1]),keep.dtype)
    def kernel(meta_ref, keep_ref, got_ref, k_ref, s_ref):
        fold_kernel(stage, meta_ref, keep_ref, got_ref, k_ref, s_ref)
    return pl.pallas_call(kernel,in_specs=[SM,VM,VM],out_specs=[VM,VM],out_shape=[sd,sd],cost_estimate=cost(1.0),
        compiler_params=pltpu.CompilerParams(vmem_limit_bytes=16*2**20),name="fold")(meta,keep,got)

def add_low(x,y):
    return (x.astype(f32)+y.astype(f32)).astype(bf16)

def place(meta, mine_ref, other_ref, buf_ref, sems, chunks):
    side=meta[7]
    rows=mine_ref.shape[0]//chunks
    copies=[]
    for i in range(chunks):
        for k,ref in enumerate((mine_ref,other_ref)):
            half=side if k==0 else 1-side
            at=lax.bitwise_xor(meta[AT+4+k],jnp.int32(i))
            copies.append(pltpu.make_async_copy(ref.at[pl.ds(i*rows,rows),:],
                buf_ref.at[half,pl.ds(pl.multiple_of(at*rows,16),rows),:],sems.at[i,k]))
    for c in copies:
        c.start()
    for c in copies:
        c.wait()

def unpack_a_kernel(chunks, meta, mine_ref, other_ref, gout_ref, gin_ref, gwo_ref, buf_ref, sems):
    place(meta,mine_ref,other_ref,buf_ref,sems,chunks)
    a=buf_ref.shape[2]; g,go,_=gout_ref.shape; ch=128
    per=go//a
    def body(i,_):
        r=pl.multiple_of(i*ch,ch)
        for h in range(g):
            for c in range(per):
                gout_ref[h,pl.ds(pl.multiple_of(c*a+r,ch),ch),:]=buf_ref[h,pl.ds(pl.multiple_of(c*a+r,ch),ch),:].astype(f32)
                gin_ref[h,pl.ds(r,ch),c*a:(c+1)*a]=buf_ref[h,pl.ds(pl.multiple_of((per+c)*a+r,ch),ch),:].astype(f32)
            for c in range(gwo_ref.shape[1]//a):
                gwo_ref[pl.ds(pl.multiple_of(h*a+r,ch),ch),c*a:(c+1)*a]=buf_ref[h,pl.ds(pl.multiple_of((2*per+c)*a+r,ch),ch),:].astype(f32)
        return 0
    lax.fori_loop(0,a//ch,body,0)

ANYS=pl.BlockSpec(memory_space=pl.ANY)
def unpack_a(meta, mine, other, g, gi, go, d, chunks):
    sd=jax.ShapeDtypeStruct
    def kernel(*refs):
        unpack_a_kernel(chunks,*refs)
    return pl.pallas_call(kernel,in_specs=[SM,ANYS,ANYS],out_specs=[VM]*3,
        out_shape=[sd((g,go,gi),f32),sd((g,gi,go),f32),sd((d,d),f32)],cost_estimate=cost(20.0),
        scratch_shapes=[pltpu.VMEM((2,)+mine.shape,bf16),pltpu.SemaphoreType.DMA((chunks,2))],
        compiler_params=pltpu.CompilerParams(vmem_limit_bytes=20*2**20),name="unpack_a")(meta,mine,other)

def unpack_b_kernel(chunks, which, meta, part_ref, q_ref, k_ref, v_ref, c_ref, p_ref, ck_ref, small_ref, buf_ref, sems, outs):
    a=buf_ref.shape[1]; rows=part_ref.shape[0]//chunks
    h=meta[7] if which==0 else 1-meta[7]
    copies=[]
    for i in range(chunks):
        at=lax.bitwise_xor(meta[AT+4+which],jnp.int32(i))
        copies.append(pltpu.make_async_copy(part_ref.at[pl.ds(i*rows,rows),:],
            buf_ref.at[pl.ds(pl.multiple_of(at*rows,16),rows),:],sems.at[i]))
    for x in copies:
        x.start()
    for x in copies:
        x.wait()
    backs=[]
    for i,ref in enumerate((q_ref,k_ref,v_ref,c_ref,p_ref)):
        outs[i]=buf_ref[i*a:(i+1)*a,:].astype(f32)
        x=pltpu.make_async_copy(outs.at[i],ref.at[pl.ds(pl.multiple_of(h*a,128),a),:],sems.at[chunks+i])
        x.start()
        backs.append(x)
    r=lax.broadcasted_iota(jnp.int32,(LAST,HEADS*TAPS),0)
    c=lax.broadcasted_iota(jnp.int32,(LAST,HEADS*TAPS),1)
    spread=jnp.where(r==(c//TAPS)*16+c%TAPS,1.0,0.0).astype(bf16)
    ck_ref[...]=dot_tn(buf_ref[5*a:5*a+LAST,:],spread)
    small_ref[:,:a]=buf_ref[5*a:5*a+16,:].astype(f32)
    small_ref[:,a:]=buf_ref[5*a+16:5*a+32,:].astype(f32)
    for x in backs:
        x.wait()

def unpack_b(meta, which, part, d, a, chunks, carry):
    sd=jax.ShapeDtypeStruct
    def kernel(meta_ref, part_ref, *refs):
        unpack_b_kernel(chunks,which,meta_ref,part_ref,*refs[-10:])
    carry=() if carry is None else tuple(carry)
    return pl.pallas_call(kernel,in_specs=[SM,ANYS]+[ANYS]*len(carry),out_specs=[ANYS]*5+[VM]*2,
        out_shape=[sd((d,a),f32)]*5+[sd((a,HEADS*TAPS),f32),sd((16,d),f32)],cost_estimate=cost(4.0),
        input_output_aliases={2+i:i for i in range(len(carry))},
        scratch_shapes=[pltpu.VMEM(part.shape,bf16),pltpu.SemaphoreType.DMA((chunks+5,)),pltpu.VMEM((5,a,a),f32)],
        compiler_params=pltpu.CompilerParams(vmem_limit_bytes=12*2**20),name="unpack_b")(meta,part,*carry)

class Reduce:
    def __init__(self, meta, keep, send, rows, scatter):
        self.meta=meta; self.rows=rows
        self.stages,self.whole=stage_bits(rows,scatter)
        self.keep=keep
        self.got=lax.ppermute(send,"seq",swap_pairs())
        self.step=0
        self.axes=("rows","seq")
    def advance(self):
        n=len(self.stages); w=len(self.whole); k=self.step; self.step+=1
        self.last=k==2*n+w
        if k<n:
            self.keep,send=fold(self.meta,k,self.keep,self.got)
            self.got=lax.ppermute(send,self.axes,row_pairs(self.rows,self.stages[k]))
        elif k<n+w:
            self.keep=add_low(self.keep,self.got)
            b=self.whole[k-n]
            self.got=lax.ppermute(self.keep,self.axes,row_pairs(self.rows,(b,b)))
        elif k==n+w+n+1:
            self.other=self.got
            self.got=None
        else:
            self.keep=add_low(self.keep,self.got) if k==n+w else jnp.concatenate([self.keep,self.got],axis=0)
            m=2*n+w-1-k
            if m>=0:
                self.got=lax.ppermute(self.keep,self.axes,row_pairs(self.rows,self.stages[m]))
            else:
                self.got=lax.ppermute(self.keep,"seq",swap_pairs())
    def after(self, arrays):
        self.got,arrays=lax.optimization_barrier((self.got,tuple(arrays)))
        self.advance()
        self.keep,arrays=lax.optimization_barrier((self.keep,arrays))
        return arrays
    def follow(self, other):
        self.got,other.keep=lax.optimization_barrier((self.got,other.keep))
        self.advance()
    def finish(self):
        while self.got is not None:
            self.advance()
        return self.keep,self.other,2**len(self.stages)

def per_device(hidden_in,doc_lengths,out_grad,w_query,w_key,w_value,w_conv_out,depth_kernel,w_point,w_conv_kernel,
               w_output,ln1_gain,ln1_bias,w_ffn_in,w_ffn_out,ln2_gain,ln2_bias):
    row_count,local,d=hidden_in.shape
    a=w_query.shape[1]
    half=local//2
    rows=lax.axis_size("rows")
    side=lax.axis_index("seq")
    row=lax.axis_index("rows")
    hid=hidden_in[0]
    meta=jnp.concatenate([make_meta(doc_lengths[0],side,local,local*2),comm_meta(side,row,rows)])
    halo=lax.ppermute(lax.dynamic_slice_in_dim(hid,(1-side)*half,half,0),"seq",swap_pairs())
    q,kw,vw,cx,depth,ck,kern,cm=pre(meta,hid,halo,w_query,w_key,w_value,w_conv_out,depth_kernel,w_point,w_conv_kernel)
    ctx,lse=attn_fwd(meta,q,kw,vw)
    ln=jnp.stack([ln1_gain,ln1_bias,ln2_gain,ln2_bias]).astype(f32)
    ho,dres,dctx,dconv,keep,send,gln=ffn(meta,hid,ctx,cm,out_grad[0],w_output,w_ffn_in,w_ffn_out,ln)
    g,gi,go=w_ffn_in.shape
    ra=Reduce(meta,keep,send,rows,3)
    carry=attn_bwd(meta,2,1,q,kw,vw,ctx,dctx,lse,None)
    out=ra.after(tuple(carry)+(dconv,))
    carry,dconv=out[:4],out[4]
    dqc,dc,dda,ddb,rimc,gp=conv_back(meta,dconv,cm,kern,cx,q,ck,depth,w_point,w_conv_kernel)
    rimc=lax.ppermute(rimc,"seq",swap_pairs())
    out=ra.after(tuple(carry)+(dqc,dda))
    carry,dqc,dda=out[:4],out[4],out[5]
    dqa,dk,dv,dkv=attn_bwd(meta,0,2,q,kw,vw,ctx,dctx,lse,carry)
    dkv=lax.ppermute(dkv,"seq",swap_pairs())
    dda,dqa=ra.after((dda,dqa))
    dha,rima,gta=taps_back(meta,0,hid,halo,dda,depth_kernel)
    ddb,dha=ra.after((ddb,dha))
    dhb,rimb,gtb=taps_back(meta,1,hid,halo,ddb,depth_kernel)
    rima=lax.ppermute(rima,"seq",swap_pairs())
    rimb=lax.ppermute(rimb,"seq",swap_pairs())
    dp,keep,send=proj_back(meta,hid,dqa,dqc,dk,dv,dkv,dc,rimc,gp,gta,gtb,gln)
    rb=Reduce(meta,keep,send,rows,3)
    grad_in=grad_input(meta,dp,dres,dha,dhb,rima,rimb,w_query,w_key,w_value,w_conv_out)
    (grad_in,)=rb.after((grad_in,))
    for one,two in ((rb,ra),(ra,rb),(rb,ra),(ra,rb),(rb,ra),(ra,rb),(rb,ra),(rb,ra),(rb,ra),(ra,rb),(ra,rb)):
        one.follow(two)
    mine,other,chunks=ra.finish()
    ffn_out_grad,ffn_in_grad,output_grad=unpack_a(meta,mine,other,g,gi,go,d,chunks)
    ffn_in_grad,ffn_out_grad,output_grad=rb.after((ffn_in_grad,ffn_out_grad,output_grad))
    while not rb.last:
        rb.advance()
    first=unpack_b(meta,0,rb.keep,d,a,chunks,None)
    first,got=lax.optimization_barrier((tuple(first),rb.got))
    second=unpack_b(meta,1,got,d,a,chunks,first[:5])
    q_grad,k_grad,v_grad,c_grad,point_grad=second[:5]
    ck_grad=jnp.where(side==0,first[5],second[5])
    small=jnp.where(side==1,first[6],second[6])
    lng=small[KSIZE:KSIZE+4]
    return (ho[None],grad_in[None],q_grad,k_grad,v_grad,c_grad,small[:KSIZE],point_grad,ck_grad,output_grad,
            lng[0],lng[1],ffn_in_grad,ffn_out_grad,lng[2],lng[3])


def solution(mesh):
    placed=(P("rows","seq",None),P("rows",None),P("rows","seq",None))+(P(),)*14
    return jax.shard_map(per_device,mesh=mesh,in_specs=placed,
        out_specs=(P("rows","seq",None),P("rows","seq",None))+(P(),)*14,check_vma=False)
```
